32 devices in a mesh: dp: 16 (over z, y, x), mp: 2 (over core).
Axes of the slice: x: 2, y: 2, z: 4, core: 2. Of those that a mesh axis runs over, the one named last changes fastest.
Arguments:
- tokens: bfloat16 [2, 16384, 768], P(None, 'dp', 'mp'), may hold values from -7.5 to 7.5, as said below
- cotangent: bfloat16 [2, 16384, 768], P(None, 'dp', 'mp'), may hold values from -6 to 6
- segments: int32 [2, 16, 1024], P(None, 'dp'), may hold values from 0 to 3, never falling along the last dimension, each value on 1 to 512 neighbouring positions
- head_gates: int32 [12], P('mp'), may hold values 0 or 1
- unit_gates: int32 [3072], P('mp'), may hold values 0 or 1
- hidden_gates: int32 [768], P('mp'), may hold values 0 or 1
- layer_gates: float32 [2], replicated, may hold values from 0.5 to 1
- w_qkv: float32 [3, 768, 768], P(None, 'dp', 'mp'), may hold values from -0.21875 to 0.21875
- w_out: float32 [768, 768], P('mp', 'dp'), may hold values from -0.875 to 0.875
- w_in: float32 [768, 3072], P('dp', 'mp'), may hold values from -0.21875 to 0.21875
- w_back: float32 [3072, 768], P('mp', 'dp'), may hold values from -0.109375 to 0.109375
- norm_params: float32 [4, 768], P(None, 'mp'), may hold values from -1 to 3.2, as said below
- mom_qkv: float32 [3, 768, 768], P(None, 'dp', 'mp'), may hold values from -0.00061035156 to 0.00061035156
- mom_out: float32 [768, 768], P('mp', 'dp'), may hold values from -0.00061035156 to 0.00061035156
- mom_in: float32 [768, 3072], P('dp', 'mp'), may hold values from -0.00061035156 to 0.00061035156
- mom_back: float32 [3072, 768], P('mp', 'dp'), may hold values from -0.00061035156 to 0.00061035156
- mom_norm: float32 [4, 768], P(None, 'mp'), may hold values from -0.00061035156 to 0.00061035156
- sec_qkv: float32 [3, 768, 768], P(None, 'dp', 'mp'), may hold values from 7.061189e-11 to 1.1297903e-09
- sec_out: float32 [768, 768], P('mp', 'dp'), may hold values from 7.061189e-11 to 1.1297903e-09
- sec_in: float32 [768, 3072], P('dp', 'mp'), may hold values from 7.061189e-11 to 1.1297903e-09
- sec_back: float32 [3072, 768], P('mp', 'dp'), may hold values from 7.061189e-11 to 1.1297903e-09
- sec_norm: float32 [4, 768], P(None, 'mp'), may hold values from 7.061189e-11 to 1.1297903e-09
Outputs:
- out_tokens: bfloat16 [2, 16384, 768], P(None, 'dp', 'mp')
- input_grad: bfloat16 [2, 16384, 768], P(None, 'dp', 'mp')
- grad_norm: float32 [], replicated
- new_w_qkv: float32 [3, 768, 768], P(None, 'dp', 'mp')
- new_w_out: float32 [768, 768], P('mp', 'dp')
- new_w_in: float32 [768, 3072], P('dp', 'mp')
- new_w_back: float32 [3072, 768], P('mp', 'dp')
- new_norm: float32 [4, 768], P(None, 'mp')
- new_m_qkv: float32 [3, 768, 768], P(None, 'dp', 'mp')
- new_m_out: float32 [768, 768], P('mp', 'dp')
- new_m_in: float32 [768, 3072], P('dp', 'mp')
- new_m_back: float32 [3072, 768], P('mp', 'dp')
- new_m_norm: float32 [4, 768], P(None, 'mp')
- new_v_qkv: float32 [3, 768, 768], P(None, 'dp', 'mp')
- new_v_out: float32 [768, 768], P('mp', 'dp')
- new_v_in: float32 [768, 3072], P('dp', 'mp')
- new_v_back: float32 [3072, 768], P('mp', 'dp')
- new_v_norm: float32 [4, 768], P(None, 'mp')
The draws below stay inside these ranges and needn't reach their ends.
Inputs may be any that keep to these rules, and one draw needn't show every extreme that they name: `segments`: within each packed sequence of 1024 positions the ids never fall; a document has at most 512 positions, and one has exactly that many. `tokens`: entries of order one. `norm_params`: gains are positive.
All inputs are finite; a program needn't handle non-finite values. No bound on the sum of `head_gates` or of `unit_gates` or of `hidden_gates` on one device may be relied on, other than what follows from the above.
Results may differ from the reference program's by a relative error of at most 0.0098.
Values may be sent and summed in bfloat16 or wider, within the bound.
No kernel may reach another device: no remote copies, remote signals or barrier semaphores. Data moves between devices by JAX's collectives and lax.ppermute only.
A program may use at most 192 MiB of HBM per device.

```python
import math
import jax
import jax.numpy as jnp
import numpy as np
from jax import lax

D = 768
HEADS = 12
HEAD_DIM = 64
FF = 3072
SEQ = 1024
MICRO = 2
DOCS = 4
BLOCK = 512
STEP = 10
PACKS = 16
TOKENS = 16384
PARAMS = 7080960


def draw_tokens(key, part):
    key = jax.random.fold_in(key, 11)
    column = jnp.arange(D, dtype=jnp.float32) / (D - 1)
    base_vals = jnp.clip(jax.random.normal(key, (MICRO, TOKENS, D), jnp.float32), -4.0, 4.0)
    column_scale = 0.6 * 3.0 ** column
    return (base_vals * column_scale).astype(jnp.bfloat16)


def draw_norm_params(key, part):
    key = jax.random.fold_in(key, 12)
    gain_key, shift_key = jax.random.split(key)
    column = jnp.arange(D, dtype=jnp.float32) / (D - 1)
    factors = jax.random.uniform(gain_key, (2, D), jnp.float32, 0.8, 1.25)
    gains = 0.6 * 3.0 ** column * factors
    shifts = 0.3 * jnp.clip(jax.random.normal(shift_key, (2, D), jnp.float32), -3.0, 3.0)
    return jnp.stack([gains[0], shifts[0], gains[1], shifts[1]]).astype(jnp.float32)


def with_ends(drawn, own_key, least, largest):
    index_at = [jax.random.randint(jax.random.fold_in(own_key, axis), (), 0, length) for axis, length in enumerate(drawn.shape)]
    widest = drawn.shape.index(max(drawn.shape))
    beside = index_at[:widest] + [(index_at[widest] + 1) % drawn.shape[widest]] + index_at[widest + 1:]
    return drawn.at[tuple(index_at)].set(least).at[tuple(beside)].set(largest)


def steps_of(key, extent, cuts, smallest, largest):
    factor_of, own = 1.0, jax.random.fold_in(key, 6)
    for position, shards_of in cuts:
        steps = jnp.exp(jax.random.uniform(jax.random.fold_in(own, position), (shards_of,), jnp.float32, smallest / len(cuts), largest / len(cuts)))
        factor_of = factor_of * jnp.repeat(steps, extent[position] // shards_of).reshape([-1 if axis == position else 1 for axis in range(len(extent))])
    return factor_of


def length_profile(count, total, reach, lean):
    loads = [(1 << 20) // math.isqrt(grade ** lean) + 1 for grade in range(2, count + 1)]
    spare, holding = total - reach - (count - 1), [1] * (count - 1)
    while spare > 0:
        free = [i for i in range(count - 1) if holding[i] < reach]
        mass, budget = sum([loads[i] for i in free]), spare
        for i in free:
            addition = min(reach - holding[i], max(1, budget * loads[i] // mass), spare)
            holding[i] = holding[i] + addition
            spare = spare - addition
    return np.array([reach] + holding)


def uneven_parts(key, amount, total, reach, lean):
    if amount == 2:
        one = jax.random.randint(key, (), max(1, total - reach), min(reach, total - 1) + 1)
        return jnp.stack([one, total - one])
    lengths = jnp.asarray(length_profile(amount, total, reach, lean), jnp.int32)
    couples = (amount - 1) // 2
    giver, receiver = lengths[1:1 + 2 * couples:2], lengths[2:2 + 2 * couples:2]
    room = jnp.minimum(giver - 1, reach - receiver)
    passed = jax.random.randint(jax.random.fold_in(key, 1), (couples,), 0, 1 << 20) % (room + 1)
    lengths = lengths.at[1:1 + 2 * couples:2].set(giver - passed).at[2:2 + 2 * couples:2].set(receiver + passed)
    return lengths[jax.random.permutation(jax.random.fold_in(key, 2), amount)]


def centred(rng, shape, deviation, reach, cuts=(), kind=jnp.bfloat16):
    result = deviation * jax.random.normal(rng, shape, jnp.float32)
    if cuts:
        result = result * steps_of(rng, shape, cuts, -0.22, 0.18)
    return jnp.clip(result, -reach, reach).astype(kind)


def setup_inputs(seed: int = 0) -> dict:
    key_list = jax.random.split(jax.random.key(seed), 23)
    return {
        "tokens": draw_tokens(jax.random.fold_in(key_list[22], 71), 0),
        "cotangent": centred(key_list[1], (MICRO, TOKENS, D), 1.0, 6.0, ((1, 16), (2, 2))),
        "segments": jax.vmap(lambda own: jnp.searchsorted(jnp.cumsum(uneven_parts(own, DOCS, SEQ, SEQ // 2, 2)), jnp.arange(SEQ), side="right"))(jax.random.split(key_list[2], MICRO * PACKS)).reshape((MICRO, PACKS, SEQ)).astype(jnp.int32),
        "head_gates": with_ends((jax.random.randint(key_list[3], (HEADS,), 0, 8) < 7).astype(jnp.int32), jax.random.fold_in(key_list[3], 1), 0, 1),
        "unit_gates": with_ends((jax.random.randint(key_list[4], (FF,), 0, 4) < 3).astype(jnp.int32), jax.random.fold_in(key_list[4], 1), 0, 1),
        "hidden_gates": with_ends((jax.random.randint(key_list[5], (D,), 0, 8) < 7).astype(jnp.int32), jax.random.fold_in(key_list[5], 1), 0, 1),
        "layer_gates": jnp.clip(jax.random.uniform(key_list[6], (2,), jnp.float32, 0.5, 1.0), 0.5, 1.0),
        "w_qkv": centred(key_list[7], (3, D, D), D ** -0.5, 0.21875, ((1, 16), (2, 2)), jnp.float32),
        "w_out": centred(key_list[8], (D, D), (D // 16) ** -0.5, 0.875, ((0, 2), (1, 16)), jnp.float32),
        "w_in": centred(key_list[9], (D, FF), D ** -0.5, 0.21875, ((0, 16), (1, 2)), jnp.float32),
        "w_back": centred(key_list[10], (FF, D), FF ** -0.5, 0.109375, ((0, 2), (1, 16)), jnp.float32),
        "norm_params": draw_norm_params(jax.random.fold_in(key_list[22], 71), 0),
        "mom_qkv": centred(key_list[12], (3, D, D), (0.11 / PARAMS ** 0.5), 0.00061035156, ((1, 16), (2, 2)), jnp.float32),
        "mom_out": centred(key_list[13], (D, D), (0.11 / PARAMS ** 0.5), 0.00061035156, ((0, 2), (1, 16)), jnp.float32),
        "mom_in": centred(key_list[14], (D, FF), (0.11 / PARAMS ** 0.5), 0.00061035156, ((0, 16), (1, 2)), jnp.float32),
        "mom_back": centred(key_list[15], (FF, D), (0.11 / PARAMS ** 0.5), 0.00061035156, ((0, 2), (1, 16)), jnp.float32),
        "mom_norm": centred(key_list[16], (4, D), (0.11 / PARAMS ** 0.5), 0.00061035156, ((1, 2),), jnp.float32),
        "sec_qkv": jnp.clip(jnp.exp(math.log(1.129790261344965e-09) - 2.7725887 * jax.random.uniform(key_list[17], (3, D, D), jnp.float32) ** steps_of(key_list[17], (3, D, D), ((1, 16), (2, 2)), -0.2, 0.2)), 7.061189133406032e-11, 1.129790261344965e-09),
        "sec_out": jnp.clip(jnp.exp(math.log(1.129790261344965e-09) - 2.7725887 * jax.random.uniform(key_list[18], (D, D), jnp.float32) ** steps_of(key_list[18], (D, D), ((0, 2), (1, 16)), -0.2, 0.2)), 7.061189133406032e-11, 1.129790261344965e-09),
        "sec_in": jnp.clip(jnp.exp(math.log(1.129790261344965e-09) - 2.7725887 * jax.random.uniform(key_list[19], (D, FF), jnp.float32) ** steps_of(key_list[19], (D, FF), ((0, 16), (1, 2)), -0.2, 0.2)), 7.061189133406032e-11, 1.129790261344965e-09),
        "sec_back": jnp.clip(jnp.exp(math.log(1.129790261344965e-09) - 2.7725887 * jax.random.uniform(key_list[20], (FF, D), jnp.float32) ** steps_of(key_list[20], (FF, D), ((0, 2), (1, 16)), -0.2, 0.2)), 7.061189133406032e-11, 1.129790261344965e-09),
        "sec_norm": jnp.clip(jnp.exp(math.log(1.129790261344965e-09) - 2.7725887 * jax.random.uniform(key_list[21], (4, D), jnp.float32) ** steps_of(key_list[21], (4, D), ((1, 2),), -0.2, 0.2)), 7.061189133406032e-11, 1.129790261344965e-09),
    }


@jax.custom_vjp
def low(v):
    return lax.optimization_barrier(v.astype(jnp.bfloat16)).astype(jnp.float32)

@jax.custom_vjp
def low_back(v):
    return v

def low_keep(v):
    return (low(v), None)

def low_pass(kept, grad):
    return (grad,)

def back_keep(v):
    return (v, None)

def back_low(kept, grad):
    return (low(grad),)
low.defvjp(low_keep, low_pass)
low_back.defvjp(back_keep, back_low)
PREC_HIGH = lax.Precision.HIGHEST
LN_EPS = 1e-12
NEG_FILL = -1000000000.0
CLIP_NORM = 1.0
LEARN_RATE = 0.06
NORM_RATE = 0.3
WEIGHT_DECAY = 0.01
BETA_ONE = 0.9
BETA_TWO = 0.999
ADAM_EPS = 1e-08

def layer_norm(residual, gain_vec, shift_vec):
    mean_val = lax.optimization_barrier(jnp.mean(residual, axis=-1, keepdims=True))
    var_val = lax.optimization_barrier(jnp.mean(residual * residual, axis=-1, keepdims=True)) - mean_val * mean_val
    return (residual - mean_val) * lax.rsqrt(var_val + LN_EPS) * gain_vec + shift_vec

def attend_block(query_blk, seg_blk, keys_all, values_all, segment):
    scores = low_back(jnp.einsum('qhc,khc->hqk', query_blk, keys_all, precision=PREC_HIGH) * HEAD_DIM ** (-0.5))
    allowed = seg_blk[:, None] == segment[None, :]
    scores = jnp.where(allowed[None], scores, NEG_FILL)
    top_val = lax.optimization_barrier(jnp.max(scores, axis=-1, keepdims=True))
    expo_vals = jnp.exp(scores - top_val)
    attn_prob = expo_vals / lax.optimization_barrier(jnp.sum(expo_vals, axis=-1, keepdims=True))
    context = jnp.einsum('hqk,khc->qhc', low(attn_prob), values_all, precision=PREC_HIGH)
    return low_back(context)

def layer_pack(w_qkv, w_out, w_in, w_back, norm_params, tokens, segment, head_mask, unit_mask, hidden_mask, layer_gates):
    qkv_val = jnp.einsum('rd,tde->tre', tokens, low(w_qkv), precision=PREC_HIGH)
    qkv_val = low(low_back(qkv_val))
    queries = qkv_val[0].reshape(SEQ, HEADS, HEAD_DIM)
    keys_all = qkv_val[1].reshape(SEQ, HEADS, HEAD_DIM)
    values_all = qkv_val[2].reshape(SEQ, HEADS, HEAD_DIM)
    blocks = SEQ // BLOCK
    checked = jax.checkpoint(attend_block)

    def one_block(block_pair):
        return checked(block_pair[0], block_pair[1], keys_all, values_all, segment)
    context = lax.map(one_block, (queries.reshape(blocks, BLOCK, HEADS, HEAD_DIM), segment.reshape(blocks, BLOCK)))
    context = context.reshape(SEQ, HEADS, HEAD_DIM)
    gated_low = low((context * head_mask[None, :, None]).reshape(SEQ, D))
    attn_val = low_back(jnp.dot(gated_low, low(w_out), precision=PREC_HIGH))
    resid_one = tokens + layer_gates[0] * attn_val * hidden_mask
    normed = layer_norm(resid_one, norm_params[0], norm_params[1])
    pre_act = low_back(jnp.dot(low(normed), low(w_in), precision=PREC_HIGH))
    hidden_act = low(jax.nn.gelu(pre_act, approximate=False) * unit_mask)
    ffn_val = low_back(jnp.dot(hidden_act, low(w_back), precision=PREC_HIGH))
    resid_two = normed + layer_gates[1] * ffn_val * hidden_mask
    return layer_norm(resid_two, norm_params[2], norm_params[3])

def adam_step(weight, gradient, first_mom, second, step_rate, decay_rate):
    first_new = BETA_ONE * first_mom + (1.0 - BETA_ONE) * gradient
    second_new = BETA_TWO * second + (1.0 - BETA_TWO) * gradient * gradient
    update = first_new / (1.0 - BETA_ONE ** STEP) / (jnp.sqrt(second_new / (1.0 - BETA_TWO ** STEP)) + ADAM_EPS)
    return (weight - step_rate * (update + decay_rate * weight), first_new, second_new)

def reference(tokens, cotangent, segments, head_gates, unit_gates, hidden_gates, layer_gates, w_qkv, w_out, w_in, w_back, norm_params, mom_qkv, mom_out, mom_in, mom_back, mom_norm, sec_qkv, sec_out, sec_in, sec_back, sec_norm):
    pack_count = MICRO * PACKS
    flat_tok = tokens.astype(jnp.float32).reshape(pack_count, SEQ, D)
    flat_cot = cotangent.astype(jnp.float32).reshape(pack_count, SEQ, D)
    flat_seg = segments.reshape(pack_count, SEQ)
    head_mask = head_gates.astype(jnp.float32)
    unit_mask = unit_gates.astype(jnp.float32)
    hidden_mask = hidden_gates.astype(jnp.float32)
    weights = (w_qkv, w_out, w_in, w_back, norm_params)

    def one_pack(totals, pack_item):
        tok_pack, cot_pack, seg_pack = pack_item

        def forward(wq_arg, wo_arg, wi_arg, wb_arg, norm_arg, tok_arg):
            return layer_pack(wq_arg, wo_arg, wi_arg, wb_arg, norm_arg, tok_arg, seg_pack, head_mask, unit_mask, hidden_mask, layer_gates)
        output, pullback = jax.vjp(forward, w_qkv, w_out, w_in, w_back, norm_params, tok_pack)
        grads = pullback(cot_pack)
        totals = tuple((summed + gradient for summed, gradient in zip(totals, grads[:5])))
        return (totals, (output.astype(jnp.bfloat16), grads[5].astype(jnp.bfloat16)))
    zeros = tuple((jnp.zeros_like(weight) for weight in weights))
    totals, (outputs, input_grads) = lax.scan(one_pack, zeros, (flat_tok, flat_cot, flat_seg))
    square_sum = jnp.sum(totals[0] * totals[0])
    for gradient in totals[1:]:
        square_sum = square_sum + jnp.sum(gradient * gradient)
    grad_norm = jnp.sqrt(square_sum)
    factor = jnp.minimum(1.0, CLIP_NORM / grad_norm)
    firsts = (mom_qkv, mom_out, mom_in, mom_back, mom_norm)
    seconds = (sec_qkv, sec_out, sec_in, sec_back, sec_norm)
    results = []
    for index in range(5):
        step_rate = LEARN_RATE if index < 4 else NORM_RATE
        decay_rate = WEIGHT_DECAY if index < 4 else 0.0
        results.append(adam_step(weights[index], totals[index] * factor, firsts[index], seconds[index], step_rate, decay_rate))
    return (outputs.reshape(MICRO, TOKENS, D), input_grads.reshape(MICRO, TOKENS, D), grad_norm, results[0][0], results[1][0], results[2][0], results[3][0], results[4][0], results[0][1], results[1][1], results[2][1], results[3][1], results[4][1], results[0][2], results[1][2], results[2][2], results[3][2], results[4][2])
```

```python
import jax
import jax.numpy as jnp
from jax import lax
from jax.experimental import pallas as pl
from jax.experimental.pallas import tpu as pltpu
from jax.sharding import PartitionSpec as P

D = 768
HEAD_DIM = 64
SEQ = 1024
STEP = 10
TILE = 256
TILES = SEQ // TILE
PAIR = 128

LN_EPS = 1e-12
CLIP_NORM = 1.0
LEARN_RATE = 0.06
NORM_RATE = 0.3
WEIGHT_DECAY = 0.01
BETA_ONE = 0.9
BETA_TWO = 0.999
ADAM_EPS = 1e-08
ATTN_SCALE = HEAD_DIM ** (-0.5)
MASK_STEP = float(2**30)
NT = (((1,), (1,)), ((), ()))
NN = (((1,), (0,)), ((), ()))
TN = (((0,), (0,)), ((), ()))
BF = jnp.bfloat16
F32 = jnp.float32


def dot(left, right, dims):
    return lax.dot_general(left, right, dims, preferred_element_type=F32)


def segment_tables(segment):
    first = segment[::TILE]
    last = segment[TILE - 1 :: TILE]
    low = jnp.sum((last[None, :] < first[:, None]).astype(jnp.int32), axis=1)
    high = jnp.sum((first[None, :] <= last[:, None]).astype(jnp.int32), axis=1)
    lane = lax.broadcasted_iota(jnp.int32, (SEQ, PAIR), 1) % HEAD_DIM
    same = lane == segment[:, None]
    key_lanes = jnp.where(same, 1.0, 0.0).astype(BF)
    query_lanes = jnp.where((lane < 4) & (~same), -MASK_STEP, 0.0).astype(BF)
    return low, high, key_lanes, query_lanes


def attend_fwd_kernel(low_ref, high_ref, qkv_ref, klane_ref, qlane_ref, ctx_ref, lse_ref, kh_ref, qh_ref, ls_ref):
    lane = lax.broadcasted_iota(jnp.int32, (SEQ, PAIR), 1)
    query = qkv_ref[:, 0:PAIR] * ATTN_SCALE
    keys = qkv_ref[:, PAIR : 2 * PAIR]
    for h in range(2):
        mine = (lane // HEAD_DIM) == h
        kh_ref[h] = jnp.where(mine, keys, klane_ref[...])
        qh_ref[h] = jnp.where(mine, query, qlane_ref[...])
    is_first = lax.broadcasted_iota(jnp.int32, (TILE, PAIR), 1) < HEAD_DIM

    def row_block(qb, carry):
        low = low_ref[qb]
        count = high_ref[qb] - low
        rows = pl.ds(pl.multiple_of(qb * TILE, TILE), TILE)
        for width in range(1, TILES + 1):

            @pl.when(count == width)
            def _():
                span = pl.ds(pl.multiple_of(low * TILE, TILE), width * TILE)
                scores = [dot(qh_ref[h, rows, :], kh_ref[h, span, :], NT) for h in range(2)]
                tops = [jnp.max(s, axis=1, keepdims=True) for s in scores]
                expo = [jnp.exp(s - m) for s, m in zip(scores, tops)]
                sums = [jnp.sum(p, axis=1, keepdims=True) for p in expo]
                outs = [dot(p.astype(BF), qkv_ref[span, 2 * PAIR : 3 * PAIR], NN) for p in expo]
                ctx_ref[rows, :] = jnp.where(is_first, outs[0] / sums[0], outs[1] / sums[1]).astype(BF)
                ls_ref[rows, :] = jnp.where(
                    is_first, tops[0] + jnp.log(sums[0]), tops[1] + jnp.log(sums[1])
                )

        return carry

    lax.fori_loop(0, TILES, row_block, 0)
    turned = ls_ref[...].T
    lse_ref[0, 0:1, :] = turned[0:1]
    lse_ref[0, 1:2, :] = turned[HEAD_DIM : HEAD_DIM + 1]


def attend_forward(qkv, tables):
    pairs = qkv.shape[1] // (3 * PAIR)
    low, high, key_lanes, query_lanes = tables
    whole = pl.BlockSpec((SEQ, PAIR), lambda p, *_: (0, 0))
    return pl.pallas_call(
        attend_fwd_kernel,
        grid_spec=pltpu.PrefetchScalarGridSpec(
            num_scalar_prefetch=2,
            grid=(pairs,),
            in_specs=[pl.BlockSpec((SEQ, 3 * PAIR), lambda p, *_: (0, p)), whole, whole],
            out_specs=[
                pl.BlockSpec((SEQ, PAIR), lambda p, *_: (0, p)),
                pl.BlockSpec((1, 2, SEQ), lambda p, *_: (p, 0, 0)),
            ],
            scratch_shapes=[
                pltpu.VMEM((2, SEQ, PAIR), BF),
                pltpu.VMEM((2, SEQ, PAIR), BF),
                pltpu.VMEM((SEQ, PAIR), F32),
            ],
        ),
        out_shape=[
            jax.ShapeDtypeStruct((SEQ, pairs * PAIR), BF),
            jax.ShapeDtypeStruct((pairs, 2, SEQ), F32),
        ],
        compiler_params=pltpu.CompilerParams(vmem_limit_bytes=32 << 20),
        cost_estimate=pl.CostEstimate(
            flops=pairs * 4 * SEQ * SEQ * 256, bytes_accessed=pairs * SEQ * 1100, transcendentals=0
        ),
        name="attend_fwd",
    )(low, high, qkv, key_lanes, query_lanes)


def attend_bwd_kernel(
    low_ref, high_ref, qkv_ref, dctx_ref, ctx_ref, lse_ref, klane_ref, qlane_ref, dqkv_ref,
    kh_ref, qh_ref, kt_ref, q0_ref, d0_ref, delta_ref, dqt_ref,
):
    lane = lax.broadcasted_iota(jnp.int32, (SEQ, PAIR), 1)
    query = qkv_ref[:, 0:PAIR] * ATTN_SCALE
    keys = qkv_ref[:, PAIR : 2 * PAIR]
    dctx = dctx_ref[...]
    kt_ref[...] = keys.T
    prod = (dctx.astype(F32) * ctx_ref[...].astype(F32)).T
    zero = jnp.zeros((SEQ, PAIR), BF)
    for h in range(2):
        mine = (lane // HEAD_DIM) == h
        kh_ref[h] = jnp.where(mine, keys, klane_ref[...])
        qh_ref[h] = jnp.where(mine, query, qlane_ref[...])
        q0_ref[h] = jnp.where(mine, query, zero)
        d0_ref[h] = jnp.where(mine, dctx, zero)
        delta_ref[h : h + 1, :] = jnp.sum(
            prod[h * HEAD_DIM : (h + 1) * HEAD_DIM], axis=0, keepdims=True
        )
    dqt_ref[...] = jnp.zeros((PAIR, SEQ), F32)

    def key_block(kb, carry):
        low = low_ref[kb]
        count = high_ref[kb] - low
        cols = pl.ds(pl.multiple_of(kb * TILE, TILE), TILE)
        for width in range(1, TILES + 1):

            @pl.when(count == width)
            def _():
                span = pl.ds(pl.multiple_of(low * TILE, TILE), width * TILE)
                values = qkv_ref[cols, 2 * PAIR : 3 * PAIR]
                scores = [dot(kh_ref[h, cols, :], qh_ref[h, span, :], NT) for h in range(2)]
                dprob = [dot(values, d0_ref[h, span, :], NT) for h in range(2)]
                prob = [jnp.exp(scores[h] - lse_ref[0, h : h + 1, span]) for h in range(2)]
                low_p = [p.astype(BF) for p in prob]
                dscore = [
                    (prob[h] * (dprob[h] - delta_ref[h : h + 1, span])).astype(BF) for h in range(2)
                ]
                dvals = dot(low_p[0], d0_ref[0, span, :], NN) + dot(low_p[1], d0_ref[1, span, :], NN)
                dkeys = dot(dscore[0], q0_ref[0, span, :], NN) + dot(dscore[1], q0_ref[1, span, :], NN)
                for h in range(2):
                    part = slice(h * HEAD_DIM, (h + 1) * HEAD_DIM)
                    dqt_ref[part, span] += dot(kt_ref[part, cols], dscore[h], NN)
                dqkv_ref[cols, PAIR : 2 * PAIR] = dkeys.astype(BF)
                dqkv_ref[cols, 2 * PAIR : 3 * PAIR] = dvals.astype(BF)

        return carry

    lax.fori_loop(0, TILES, key_block, 0)
    dqkv_ref[:, 0:PAIR] = (dqt_ref[...].T * ATTN_SCALE).astype(BF)


def attend_backward(qkv, dctx, ctx, lse, tables):
    pairs = qkv.shape[1] // (3 * PAIR)
    low, high, key_lanes, query_lanes = tables
    whole = pl.BlockSpec((SEQ, PAIR), lambda p, *_: (0, 0))
    column = pl.BlockSpec((SEQ, PAIR), lambda p, *_: (0, p))
    triple = pl.BlockSpec((SEQ, 3 * PAIR), lambda p, *_: (0, p))
    return pl.pallas_call(
        attend_bwd_kernel,
        grid_spec=pltpu.PrefetchScalarGridSpec(
            num_scalar_prefetch=2,
            grid=(pairs,),
            in_specs=[
                triple, column, column, pl.BlockSpec((1, 2, SEQ), lambda p, *_: (p, 0, 0)), whole, whole,
            ],
            out_specs=triple,
            scratch_shapes=[
                pltpu.VMEM((2, SEQ, PAIR), BF),
                pltpu.VMEM((2, SEQ, PAIR), BF),
                pltpu.VMEM((PAIR, SEQ), BF),
                pltpu.VMEM((2, SEQ, PAIR), BF),
                pltpu.VMEM((2, SEQ, PAIR), BF),
                pltpu.VMEM((2, SEQ), F32),
                pltpu.VMEM((PAIR, SEQ), F32),
            ],
        ),
        out_shape=jax.ShapeDtypeStruct((SEQ, pairs * 3 * PAIR), BF),
        compiler_params=pltpu.CompilerParams(vmem_limit_bytes=32 << 20),
        cost_estimate=pl.CostEstimate(
            flops=pairs * 8 * SEQ * SEQ * 256, bytes_accessed=pairs * SEQ * 2100, transcendentals=0
        ),
        name="attend_bwd",
    )(low, high, qkv, dctx, ctx, lse, key_lanes, query_lanes)


def gelu_pair(value):
    size = jnp.abs(value)
    bell = jnp.exp(-0.5 * value * value)
    step = 1.0 / (1.0 + (0.3275911 * 0.7071067811865476) * size)
    poly = step * (
        0.127414796
        + step * (-0.142248368 + step * (0.7107068705 + step * (-0.7265760135 + step * 0.5307027145)))
    )
    tail = poly * bell
    phi = jnp.where(value >= 0.0, 1.0 - tail, tail)
    return value * phi, phi + value * bell * 0.3989422804014327


def ffn_in_kernel(x_ref, w_ref, act_ref, slope_ref):
    pre = dot(x_ref[...], w_ref[...], NN)
    act, slope = gelu_pair(pre)
    act_ref[...] = act.astype(BF)
    slope_ref[...] = slope.astype(BF)


def ffn_in(normed, weight):
    units = weight.shape[1]
    width = 256
    return pl.pallas_call(
        ffn_in_kernel,
        grid=(units // width,),
        in_specs=[
            pl.BlockSpec((SEQ, D), lambda n: (0, 0)),
            pl.BlockSpec((D, width), lambda n: (0, n)),
        ],
        out_specs=[pl.BlockSpec((SEQ, width), lambda n: (0, n))] * 2,
        out_shape=[jax.ShapeDtypeStruct((SEQ, units), BF)] * 2,
        compiler_params=pltpu.CompilerParams(vmem_limit_bytes=32 << 20),
        cost_estimate=pl.CostEstimate(
            flops=4 * SEQ * D * units, bytes_accessed=SEQ * units * 4, transcendentals=0
        ),
        name="ffn_in",
    )(normed, weight)


def digits_of(count):
    found, shift = [], 0
    while (1 << shift) < count:
        radix = min(4, count >> shift)
        found.append((shift, radix))
        shift += 2 if radix == 4 else 1
    return found


def swap(value, count, mask, axis="dp"):
    return lax.ppermute(value, axis, [(i, i ^ mask) for i in range(count)])


def place_kernel(digit_ref, *refs):
    pieces, out, sems = refs[:-2], refs[-2], refs[-1]
    digit = digit_ref[0]
    copies = [
        pltpu.make_async_copy(piece, out.at[:, digit ^ j], sems.at[j]) for j, piece in enumerate(pieces)
    ]
    for copy in copies:
        copy.start()
    for copy in copies:
        copy.wait()


def place(pieces, digit):
    outer, rows, cols = pieces[0].shape
    radix = len(pieces)
    return pl.pallas_call(
        place_kernel,
        grid_spec=pltpu.PrefetchScalarGridSpec(
            num_scalar_prefetch=1,
            grid=(),
            in_specs=[pl.BlockSpec(memory_space=pl.ANY)] * radix,
            out_specs=pl.BlockSpec(memory_space=pl.ANY),
            scratch_shapes=[pltpu.SemaphoreType.DMA((radix,))],
        ),
        out_shape=jax.ShapeDtypeStruct((outer, radix, rows, cols), pieces[0].dtype),
        cost_estimate=pl.CostEstimate(
            flops=0, bytes_accessed=outer * radix * rows * cols * 4, transcendentals=0
        ),
        name="place",
    )(digit[None], *pieces)


def gather_rows(shard, count, index):
    rows, cols = shard.shape
    held = shard[None]
    for shift, radix in reversed(digits_of(count)):
        pieces = [held] + [swap(held, count, j << shift) for j in range(1, radix)]
        held = place(pieces, (index >> shift) & (radix - 1)).reshape(-1, rows, cols)
    return held.reshape(-1, cols)


def scatter_rows(total, count, index):
    rows, cols = total.shape[0] // count, total.shape[1]
    held = total
    for shift, radix in digits_of(count):
        digit = (index >> shift) & (radix - 1)
        parts = held.reshape(-1, radix, rows, cols)
        own = lax.dynamic_index_in_dim(parts, digit, 1, keepdims=False).astype(F32)
        for j in range(1, radix):
            away = lax.dynamic_index_in_dim(parts, digit ^ j, 1, keepdims=False)
            own = own + swap(away.astype(BF), count, j << shift).astype(F32)
        held = own
        if shift != digits_of(count)[-1][0]:
            held = held.astype(BF)
    return held.reshape(rows, cols)


def sum_all(value, count):
    value = value + swap(value, 2, 1, "mp")
    for shift, radix in digits_of(count):
        parts = [value] + [swap(value, count, j << shift) for j in range(1, radix)]
        value = parts[0] + parts[1]
        if radix == 4:
            value = value + (parts[2] + parts[3])
    return value


def norm_forward(residual, gain_vec, shift_vec):
    mean_val = jnp.sum(residual, axis=-1, keepdims=True) / D
    var_val = jnp.sum(residual * residual, axis=-1, keepdims=True) / D - mean_val * mean_val
    inv_std = lax.rsqrt(var_val + LN_EPS)
    centred = (residual - mean_val) * inv_std
    return (centred * gain_vec + shift_vec, centred, inv_std)


def norm_backward(grad_out, centred, inv_std, gain_vec):
    scaled = grad_out * gain_vec
    mean_one = jnp.sum(scaled, axis=-1, keepdims=True) / D
    mean_two = jnp.sum(scaled * centred, axis=-1, keepdims=True) / D
    grad_in = inv_std * (scaled - mean_one - centred * mean_two)
    return (grad_in, jnp.sum(grad_out * centred, axis=0), jnp.sum(grad_out, axis=0))


def adam_step(weight, gradient, first_mom, second, step_rate, decay_rate):
    first_new = BETA_ONE * first_mom + (1.0 - BETA_ONE) * gradient
    second_new = BETA_TWO * second + (1.0 - BETA_TWO) * gradient * gradient
    update = (
        first_new
        / (1.0 - BETA_ONE**STEP)
        / (jnp.sqrt(second_new / (1.0 - BETA_TWO**STEP)) + ADAM_EPS)
    )
    return (weight - step_rate * (update + decay_rate * weight), first_new, second_new)


def shards(
    count,
    tokens,
    cotangent,
    segments,
    head_gates,
    unit_gates,
    hidden_gates,
    layer_gates,
    w_qkv,
    w_out,
    w_in,
    w_back,
    norm_params,
    mom_qkv,
    mom_out,
    mom_in,
    mom_back,
    mom_norm,
    sec_qkv,
    sec_out,
    sec_in,
    sec_back,
    sec_norm,
):
    index = lax.axis_index("dp")
    core = lax.axis_index("mp")
    rows = D // count
    half = D // 2
    pairs = half // PAIR
    head_mask = jnp.repeat(head_gates.astype(F32), HEAD_DIM)
    unit_mask = unit_gates.astype(F32)
    gate_attn = layer_gates[0]
    gate_ffn = layer_gates[1]

    shard_qkv = (
        w_qkv.astype(BF).reshape(3, rows, pairs, PAIR).transpose(1, 2, 0, 3).reshape(rows, 3 * half)
    )
    shard_out = (w_out.T * head_mask[None, :]).astype(BF)
    shard_one = jnp.concatenate([shard_qkv, shard_out], axis=1)
    shard_in = w_in.astype(BF)
    shard_back = (w_back.T * unit_mask[None, :]).astype(BF)

    def other_core(value):
        return swap(value, 2, 1, "mp")

    def both(own, away):
        return jnp.where(
            core == 0, jnp.concatenate([own, away], axis=-1), jnp.concatenate([away, own], axis=-1)
        )

    mine_one = gather_rows(shard_one, count, index)
    away_one = other_core(mine_one)
    mine_in = gather_rows(shard_in, count, index)
    away_in = other_core(mine_in)
    mine_back = gather_rows(shard_back, count, index)
    away_back = other_core(mine_back)
    qkv_sides = (mine_one[:, : 3 * half], away_one[:, : 3 * half])
    out_sides = (mine_one[:, 3 * half :], away_one[:, 3 * half :])
    in_sides = (mine_in, away_in)
    back_sides = (mine_back, away_back)

    def bring(value):
        own = lax.dynamic_index_in_dim(value, core, 0, keepdims=False)
        away = other_core(lax.dynamic_index_in_dim(value, 1 - core, 0, keepdims=False))
        return both(own, away)

    x = bring(tokens)
    grad_out = bring(cotangent)
    vectors = jnp.concatenate([hidden_gates.astype(F32)[None], norm_params], axis=0)
    vectors = both(vectors, other_core(vectors))
    hidden_mask, params = vectors[0], vectors[1:]
    segment = lax.dynamic_index_in_dim(segments, core, 0, keepdims=False)[0]
    tables = segment_tables(segment)

    qkv = [dot(x, side, NN).astype(BF) for side in qkv_sides]
    ctx, lse = [], []
    for side in range(2):
        context, log_sum = attend_forward(qkv[side], tables)
        ctx.append(context)
        lse.append(log_sum)
    attn = dot(ctx[0], out_sides[0], NT) + dot(ctx[1], out_sides[1], NT)
    resid_one = x.astype(F32) + (gate_attn * hidden_mask) * attn
    normed, centred_one, inv_one = norm_forward(resid_one, params[0], params[1])
    normed_low = normed.astype(BF)
    acts, slopes = [], []
    for side in range(2):
        act, slope = ffn_in(normed_low, in_sides[side])
        acts.append(act)
        slopes.append(slope)
    ffn = dot(acts[0], back_sides[0], NT) + dot(acts[1], back_sides[1], NT)
    resid_two = normed + (gate_ffn * hidden_mask) * ffn
    result, centred_two, inv_two = norm_forward(resid_two, params[2], params[3])

    grad_two, dgain_two, dshift_two = norm_backward(
        grad_out.astype(F32), centred_two, inv_two, params[2]
    )
    grad_ffn = ((gate_ffn * hidden_mask) * grad_two).astype(BF)

    def reduce_group(own, away):
        summed = own.astype(F32) + other_core(away.astype(BF)).astype(F32)
        return scatter_rows(summed.astype(BF), count, index)

    g_back = [dot(grad_ffn, act, TN).astype(BF) for act in acts]
    sum_back = reduce_group(*g_back)
    grad_pre = [
        (dot(grad_ffn, back_sides[s], NN) * slopes[s].astype(F32)).astype(BF) for s in range(2)
    ]
    g_in = [dot(normed_low, g, TN).astype(BF) for g in grad_pre]
    sum_in = reduce_group(*g_in)
    grad_normed = grad_two + (dot(grad_pre[0], in_sides[0], NT) + dot(grad_pre[1], in_sides[1], NT))
    grad_one, dgain_one, dshift_one = norm_backward(grad_normed, centred_one, inv_one, params[0])
    grad_attn = ((gate_attn * hidden_mask) * grad_one).astype(BF)
    g_out = [dot(grad_attn, context, TN).astype(BF) for context in ctx]
    dqkv = []
    for side in range(2):
        dctx = dot(grad_attn, out_sides[side], NN).astype(BF)
        dqkv.append(attend_backward(qkv[side], dctx, ctx[side], lse[side], tables))
    g_qkv = [dot(x, g, TN).astype(BF) for g in dqkv]
    sum_one = reduce_group(*[jnp.concatenate(pair, axis=1) for pair in zip(g_qkv, g_out)])
    grad_tok = grad_one + (dot(dqkv[0], qkv_sides[0], NT) + dot(dqkv[1], qkv_sides[1], NT))

    def send_back(value):
        first, second = value[:, :half], value[:, half:]
        own = jnp.where(core == 0, first, second)
        away = other_core(jnp.where(core == 0, second, first))
        return jnp.where(core == 0, jnp.stack([own, away]), jnp.stack([away, own]))

    out_tokens = send_back(result.astype(BF))
    input_grad = send_back(grad_tok.astype(BF))

    sum_qkv = sum_one[:, : 3 * half].reshape(rows, pairs, 3, PAIR).transpose(2, 0, 1, 3)
    sum_qkv = sum_qkv.reshape(3, rows, half)
    sum_out = (sum_one[:, 3 * half :] * head_mask[None, :]).T
    sum_wb = (sum_back * unit_mask[None, :]).T
    sums = (sum_qkv, sum_out, sum_in, sum_wb)
    square = sum(jnp.sum(g * g) for g in sums)
    norm_rows = jnp.stack([dgain_one, dshift_one, dgain_two, dshift_two]).reshape(-1, 128)
    packed = jnp.concatenate([norm_rows, jnp.full((8, 128), square / 1024.0, F32)], axis=0)
    packed = sum_all(packed, count)
    norm_full = packed[:-8].reshape(4, D)
    total_square = jnp.sum(packed[-8:]) + jnp.sum(norm_full * norm_full)
    grad_norm = jnp.sqrt(total_square)
    factor = jnp.minimum(1.0, CLIP_NORM / grad_norm)
    norm_here = lax.dynamic_slice_in_dim(norm_full, core * half, half, 1)
    weights = (w_qkv, w_out, w_in, w_back, norm_params)
    firsts = (mom_qkv, mom_out, mom_in, mom_back, mom_norm)
    seconds = (sec_qkv, sec_out, sec_in, sec_back, sec_norm)
    results = []
    for slot, gradient in enumerate(sums + (norm_here,)):
        results.append(
            adam_step(
                weights[slot],
                gradient * factor,
                firsts[slot],
                seconds[slot],
                LEARN_RATE if slot < 4 else NORM_RATE,
                WEIGHT_DECAY if slot < 4 else 0.0,
            )
        )
    return (
        out_tokens,
        input_grad,
        grad_norm,
        *[r[0] for r in results],
        *[r[1] for r in results],
        *[r[2] for r in results],
    )


def solution(mesh):
    weight_specs = (P(None, "dp", "mp"), P("mp", "dp"), P("dp", "mp"), P("mp", "dp"), P(None, "mp"))
    in_specs = (
        P(None, "dp", "mp"),
        P(None, "dp", "mp"),
        P(None, "dp", None),
        P("mp"),
        P("mp"),
        P("mp"),
        P(),
    ) + weight_specs * 3
    out_specs = (P(None, "dp", "mp"), P(None, "dp", "mp"), P()) + weight_specs * 3
    count = mesh.shape["dp"]

    def body(*args):
        return shards(count, *args)

    return jax.shard_map(body, mesh=mesh, in_specs=in_specs, out_specs=out_specs, check_vma=False)
```

```python
import functools

import jax
import jax.numpy as jnp
from jax import lax
from jax.experimental import pallas as pl
from jax.experimental.pallas import tpu as pltpu
from jax.sharding import PartitionSpec as P

D = 768
HEAD_DIM = 64
SEQ = 1024
STEP = 10
TILE = 256
TILES = SEQ // TILE
PAIR = 128

LN_EPS = 1e-12
CLIP_NORM = 1.0
LEARN_RATE = 0.06
NORM_RATE = 0.3
WEIGHT_DECAY = 0.01
BETA_ONE = 0.9
BETA_TWO = 0.999
ADAM_EPS = 1e-08
ATTN_SCALE = HEAD_DIM ** (-0.5)
MASK_STEP = float(2**30)
NT = (((1,), (1,)), ((), ()))
NN = (((1,), (0,)), ((), ()))
TN = (((0,), (0,)), ((), ()))
BF = jnp.bfloat16
F32 = jnp.float32


def dot(left, right, dims):
    return lax.dot_general(left, right, dims, preferred_element_type=F32)


def segment_tables(segment):
    first = segment[::TILE]
    last = segment[TILE - 1 :: TILE]
    low = jnp.sum((last[None, :] < first[:, None]).astype(jnp.int32), axis=1)
    high = jnp.sum((first[None, :] <= last[:, None]).astype(jnp.int32), axis=1)
    lane = lax.broadcasted_iota(jnp.int32, (SEQ, PAIR), 1) % HEAD_DIM
    same = lane == segment[:, None]
    key_lanes = jnp.where(same, 1.0, 0.0).astype(BF)
    query_lanes = jnp.where((lane < 4) & (~same), -MASK_STEP, 0.0).astype(BF)
    return low, high, key_lanes, query_lanes


def attend_fwd_kernel(low_ref, high_ref, qkv_ref, klane_ref, qlane_ref, ctx_ref, lse_ref, kh_ref, qh_ref, ls_ref):
    lane = lax.broadcasted_iota(jnp.int32, (SEQ, PAIR), 1)
    query = qkv_ref[:, 0:PAIR] * ATTN_SCALE
    keys = qkv_ref[:, PAIR : 2 * PAIR]
    for h in range(2):
        mine = (lane // HEAD_DIM) == h
        kh_ref[h] = jnp.where(mine, keys, klane_ref[...])
        qh_ref[h] = jnp.where(mine, query, qlane_ref[...])
    is_first = lax.broadcasted_iota(jnp.int32, (TILE, PAIR), 1) < HEAD_DIM

    def row_block(qb, carry):
        low = low_ref[qb]
        count = high_ref[qb] - low
        rows = pl.ds(pl.multiple_of(qb * TILE, TILE), TILE)
        for width in range(1, TILES + 1):

            @pl.when(count == width)
            def _():
                span = pl.ds(pl.multiple_of(low * TILE, TILE), width * TILE)
                scores = [dot(qh_ref[h, rows, :], kh_ref[h, span, :], NT) for h in range(2)]
                tops = [jnp.max(s, axis=1, keepdims=True) for s in scores]
                expo = [jnp.exp(s - m) for s, m in zip(scores, tops)]
                sums = [jnp.sum(p, axis=1, keepdims=True) for p in expo]
                outs = [dot(p.astype(BF), qkv_ref[span, 2 * PAIR : 3 * PAIR], NN) for p in expo]
                ctx_ref[rows, :] = jnp.where(is_first, outs[0] / sums[0], outs[1] / sums[1]).astype(BF)
                ls_ref[rows, :] = jnp.where(
                    is_first, tops[0] + jnp.log(sums[0]), tops[1] + jnp.log(sums[1])
                )

        return carry

    lax.fori_loop(0, TILES, row_block, 0)
    turned = ls_ref[...].T
    lse_ref[0, 0:1, :] = turned[0:1]
    lse_ref[0, 1:2, :] = turned[HEAD_DIM : HEAD_DIM + 1]


def attend_forward(qkv, tables):
    pairs = qkv.shape[1] // (3 * PAIR)
    low, high, key_lanes, query_lanes = tables
    whole = pl.BlockSpec((SEQ, PAIR), lambda p, *_: (0, 0))
    return pl.pallas_call(
        attend_fwd_kernel,
        grid_spec=pltpu.PrefetchScalarGridSpec(
            num_scalar_prefetch=2,
            grid=(pairs,),
            in_specs=[pl.BlockSpec((SEQ, 3 * PAIR), lambda p, *_: (0, p)), whole, whole],
            out_specs=[
                pl.BlockSpec((SEQ, PAIR), lambda p, *_: (0, p)),
                pl.BlockSpec((1, 2, SEQ), lambda p, *_: (p, 0, 0)),
            ],
            scratch_shapes=[
                pltpu.VMEM((2, SEQ, PAIR), BF),
                pltpu.VMEM((2, SEQ, PAIR), BF),
                pltpu.VMEM((SEQ, PAIR), F32),
            ],
        ),
        out_shape=[
            jax.ShapeDtypeStruct((SEQ, pairs * PAIR), BF),
            jax.ShapeDtypeStruct((pairs, 2, SEQ), F32),
        ],
        compiler_params=pltpu.CompilerParams(vmem_limit_bytes=32 << 20),
        cost_estimate=pl.CostEstimate(
            flops=pairs * 4 * SEQ * SEQ * 256, bytes_accessed=pairs * SEQ * 1100, transcendentals=0
        ),
        name="attend_fwd",
    )(low, high, qkv, key_lanes, query_lanes)


def attend_bwd_kernel(
    low_ref, high_ref, qkv_ref, dctx_ref, ctx_ref, lse_ref, klane_ref, qlane_ref, dqkv_ref,
    kh_ref, qh_ref, kt_ref, q0_ref, d0_ref, delta_ref, dqt_ref,
):
    lane = lax.broadcasted_iota(jnp.int32, (SEQ, PAIR), 1)
    query = qkv_ref[:, 0:PAIR] * ATTN_SCALE
    keys = qkv_ref[:, PAIR : 2 * PAIR]
    dctx = dctx_ref[...]
    kt_ref[...] = keys.T
    prod = (dctx.astype(F32) * ctx_ref[...].astype(F32)).T
    zero = jnp.zeros((SEQ, PAIR), BF)
    for h in range(2):
        mine = (lane // HEAD_DIM) == h
        kh_ref[h] = jnp.where(mine, keys, klane_ref[...])
        qh_ref[h] = jnp.where(mine, query, qlane_ref[...])
        q0_ref[h] = jnp.where(mine, query, zero)
        d0_ref[h] = jnp.where(mine, dctx, zero)
        delta_ref[h : h + 1, :] = jnp.sum(
            prod[h * HEAD_DIM : (h + 1) * HEAD_DIM], axis=0, keepdims=True
        )
    dqt_ref[...] = jnp.zeros((PAIR, SEQ), F32)

    def key_block(kb, carry):
        low = low_ref[kb]
        count = high_ref[kb] - low
        cols = pl.ds(pl.multiple_of(kb * TILE, TILE), TILE)
        for width in range(1, TILES + 1):

            @pl.when(count == width)
            def _():
                span = pl.ds(pl.multiple_of(low * TILE, TILE), width * TILE)
                values = qkv_ref[cols, 2 * PAIR : 3 * PAIR]
                scores = [dot(kh_ref[h, cols, :], qh_ref[h, span, :], NT) for h in range(2)]
                dprob = [dot(values, d0_ref[h, span, :], NT) for h in range(2)]
                prob = [jnp.exp(scores[h] - lse_ref[0, h : h + 1, span]) for h in range(2)]
                low_p = [p.astype(BF) for p in prob]
                dscore = [
                    (prob[h] * (dprob[h] - delta_ref[h : h + 1, span])).astype(BF) for h in range(2)
                ]
                dvals = dot(low_p[0], d0_ref[0, span, :], NN) + dot(low_p[1], d0_ref[1, span, :], NN)
                dkeys = dot(dscore[0], q0_ref[0, span, :], NN) + dot(dscore[1], q0_ref[1, span, :], NN)
                for h in range(2):
                    part = slice(h * HEAD_DIM, (h + 1) * HEAD_DIM)
                    dqt_ref[part, span] += dot(kt_ref[part, cols], dscore[h], NN)
                dqkv_ref[cols, PAIR : 2 * PAIR] = dkeys.astype(BF)
                dqkv_ref[cols, 2 * PAIR : 3 * PAIR] = dvals.astype(BF)

        return carry

    lax.fori_loop(0, TILES, key_block, 0)
    dqkv_ref[:, 0:PAIR] = (dqt_ref[...].T * ATTN_SCALE).astype(BF)


def attend_backward(qkv, dctx, ctx, lse, tables):
    pairs = qkv.shape[1] // (3 * PAIR)
    low, high, key_lanes, query_lanes = tables
    whole = pl.BlockSpec((SEQ, PAIR), lambda p, *_: (0, 0))
    column = pl.BlockSpec((SEQ, PAIR), lambda p, *_: (0, p))
    triple = pl.BlockSpec((SEQ, 3 * PAIR), lambda p, *_: (0, p))
    return pl.pallas_call(
        attend_bwd_kernel,
        grid_spec=pltpu.PrefetchScalarGridSpec(
            num_scalar_prefetch=2,
            grid=(pairs,),
            in_specs=[
                triple, column, column, pl.BlockSpec((1, 2, SEQ), lambda p, *_: (p, 0, 0)), whole, whole,
            ],
            out_specs=triple,
            scratch_shapes=[
                pltpu.VMEM((2, SEQ, PAIR), BF),
                pltpu.VMEM((2, SEQ, PAIR), BF),
                pltpu.VMEM((PAIR, SEQ), BF),
                pltpu.VMEM((2, SEQ, PAIR), BF),
                pltpu.VMEM((2, SEQ, PAIR), BF),
                pltpu.VMEM((2, SEQ), F32),
                pltpu.VMEM((PAIR, SEQ), F32),
            ],
        ),
        out_shape=jax.ShapeDtypeStruct((SEQ, pairs * 3 * PAIR), BF),
        compiler_params=pltpu.CompilerParams(vmem_limit_bytes=32 << 20),
        cost_estimate=pl.CostEstimate(
            flops=pairs * 8 * SEQ * SEQ * 256, bytes_accessed=pairs * SEQ * 2100, transcendentals=0
        ),
        name="attend_bwd",
    )(low, high, qkv, dctx, ctx, lse, key_lanes, query_lanes)


def gelu_pair(value):
    size = jnp.abs(value)
    bell = jnp.exp(-0.5 * value * value)
    step = 1.0 / (1.0 + (0.3275911 * 0.7071067811865476) * size)
    poly = step * (
        0.127414796
        + step * (-0.142248368 + step * (0.7107068705 + step * (-0.7265760135 + step * 0.5307027145)))
    )
    tail = poly * bell
    phi = jnp.where(value >= 0.0, 1.0 - tail, tail)
    return value * phi, phi + value * bell * 0.3989422804014327


def ffn_in_kernel(x_ref, w_ref, act_ref, slope_ref):
    pre = dot(x_ref[...], w_ref[...], NN)
    act, slope = gelu_pair(pre)
    act_ref[...] = act.astype(BF)
    slope_ref[...] = slope.astype(BF)


def ffn_in(normed, weight):
    units = weight.shape[1]
    width = 256
    return pl.pallas_call(
        ffn_in_kernel,
        grid=(units // width,),
        in_specs=[
            pl.BlockSpec((SEQ, D), lambda n: (0, 0)),
            pl.BlockSpec((D, width), lambda n: (0, n)),
        ],
        out_specs=[pl.BlockSpec((SEQ, width), lambda n: (0, n))] * 2,
        out_shape=[jax.ShapeDtypeStruct((SEQ, units), BF)] * 2,
        compiler_params=pltpu.CompilerParams(vmem_limit_bytes=32 << 20),
        cost_estimate=pl.CostEstimate(
            flops=4 * SEQ * D * units, bytes_accessed=SEQ * units * 4, transcendentals=0
        ),
        name="ffn_in",
    )(normed, weight)


def digits_of(count):
    found, shift = [], 0
    while (1 << shift) < count:
        radix = min(4, count >> shift)
        found.append((shift, radix))
        shift += 2 if radix == 4 else 1
    return found


def swap(value, count, mask, axis="dp"):
    return lax.ppermute(value, axis, [(i, i ^ mask) for i in range(count)])


def tie(value, *others):
    flat, tree = jax.tree.flatten(value)
    return jax.tree.unflatten(tree, lax.optimization_barrier(tuple(flat) + others)[: len(flat)])


def place_kernel(digit_ref, *refs):
    pieces, out = refs[:-1], refs[-1]
    for j, piece in enumerate(pieces):

        @pl.when(pl.program_id(0) == j)
        def _():
            out[:, 0] = piece[...]


def place(pieces, digit):
    outer, rows, cols = pieces[0].shape
    radix = len(pieces)
    return pl.pallas_call(
        place_kernel,
        grid_spec=pltpu.PrefetchScalarGridSpec(
            num_scalar_prefetch=1,
            grid=(radix,),
            in_specs=[pl.BlockSpec((outer, rows, cols), lambda g, d: (0, 0, 0))] * radix,
            out_specs=pl.BlockSpec((outer, 1, rows, cols), lambda g, d: (0, d[0] ^ g, 0, 0)),
        ),
        out_shape=jax.ShapeDtypeStruct((outer, radix, rows, cols), pieces[0].dtype),
        compiler_params=pltpu.CompilerParams(vmem_limit_bytes=32 << 20),
        cost_estimate=pl.CostEstimate(
            flops=0, bytes_accessed=outer * radix * rows * cols * 4, transcendentals=0
        ),
        name="place",
    )(digit[None], *pieces)


def sum_split_kernel(digit_ref, *refs, terms):
    total = refs[0][:, 0].astype(F32)
    for ref in refs[1:terms]:
        total = total + ref[:, 0].astype(F32)
    total = total.astype(BF)
    for j, out in enumerate(refs[terms:]):

        @pl.when(pl.program_id(0) == j)
        def _():
            out[...] = total


def sum_split(terms, digit):
    outer, radix, rows, cols = terms[0].shape
    return pl.pallas_call(
        functools.partial(sum_split_kernel, terms=len(terms)),
        grid_spec=pltpu.PrefetchScalarGridSpec(
            num_scalar_prefetch=1,
            grid=(radix,),
            in_specs=[pl.BlockSpec((outer, 1, rows, cols), lambda g, d: (0, d[0] ^ g, 0, 0))] * len(terms),
            out_specs=[pl.BlockSpec((outer, rows, cols), lambda g, d: (0, 0, 0))] * radix,
        ),
        out_shape=[jax.ShapeDtypeStruct((outer, rows, cols), BF)] * radix,
        compiler_params=pltpu.CompilerParams(vmem_limit_bytes=40 << 20),
        cost_estimate=pl.CostEstimate(
            flops=0,
            bytes_accessed=2 * outer * radix * rows * cols * (len(terms) + 1),
            transcendentals=0,
        ),
        name="sum_split",
    )(digit[None], *terms)


def gather_start(held, count, place_in):
    shift, radix = place_in
    return [held] + [swap(held, count, j << shift) for j in range(1, radix)]


def gather_place(pieces, index, place_in):
    shift, radix = place_in
    outer, rows, cols = pieces[0].shape
    return place(pieces, (index >> shift) & (radix - 1)).reshape(outer * radix, rows, cols)


def scatter_start(terms, count, index, place_in, rows):
    shift, radix = place_in
    cols = terms[0].shape[-1]
    shaped = [t.reshape(-1, radix, rows, cols) for t in terms]
    parts = sum_split(shaped, (index >> shift) & (radix - 1))
    return parts, [parts[0]] + [swap(parts[j], count, j << shift) for j in range(1, radix)]


def sum_all(value, count):
    value = value + swap(value, 2, 1, "mp")
    for shift, radix in digits_of(count):
        parts = [value] + [swap(value, count, j << shift) for j in range(1, radix)]
        value = parts[0] + parts[1]
        if radix == 4:
            value = value + (parts[2] + parts[3])
    return value


def norm_forward(residual, gain_vec, shift_vec):
    mean_val = jnp.sum(residual, axis=-1, keepdims=True) / D
    var_val = jnp.sum(residual * residual, axis=-1, keepdims=True) / D - mean_val * mean_val
    inv_std = lax.rsqrt(var_val + LN_EPS)
    centred = (residual - mean_val) * inv_std
    return (centred * gain_vec + shift_vec, centred, inv_std)


def norm_backward(grad_out, centred, inv_std, gain_vec):
    scaled = grad_out * gain_vec
    mean_one = jnp.sum(scaled, axis=-1, keepdims=True) / D
    mean_two = jnp.sum(scaled * centred, axis=-1, keepdims=True) / D
    grad_in = inv_std * (scaled - mean_one - centred * mean_two)
    return (grad_in, jnp.sum(grad_out * centred, axis=0), jnp.sum(grad_out, axis=0))


def adam_step(weight, gradient, first_mom, second, step_rate, decay_rate):
    first_new = BETA_ONE * first_mom + (1.0 - BETA_ONE) * gradient
    second_new = BETA_TWO * second + (1.0 - BETA_TWO) * gradient * gradient
    update = (
        first_new
        / (1.0 - BETA_ONE**STEP)
        / (jnp.sqrt(second_new / (1.0 - BETA_TWO**STEP)) + ADAM_EPS)
    )
    return (weight - step_rate * (update + decay_rate * weight), first_new, second_new)


def shards(
    count,
    tokens,
    cotangent,
    segments,
    head_gates,
    unit_gates,
    hidden_gates,
    layer_gates,
    w_qkv,
    w_out,
    w_in,
    w_back,
    norm_params,
    mom_qkv,
    mom_out,
    mom_in,
    mom_back,
    mom_norm,
    sec_qkv,
    sec_out,
    sec_in,
    sec_back,
    sec_norm,
):
    index = lax.axis_index("dp")
    core = lax.axis_index("mp")
    rows = D // count
    half = D // 2
    pairs = half // PAIR
    head_mask = jnp.repeat(head_gates.astype(F32), HEAD_DIM)
    unit_mask = unit_gates.astype(F32)
    gate_attn = layer_gates[0]
    gate_ffn = layer_gates[1]

    shard_qkv = (
        w_qkv.astype(BF).reshape(3, rows, pairs, PAIR).transpose(1, 2, 0, 3).reshape(rows, 3 * half)
    )
    shard_out = (w_out.T * head_mask[None, :]).astype(BF)
    shard_two = jnp.concatenate([w_in.astype(BF), shard_out], axis=1)
    shard_back = (w_back.T * unit_mask[None, :]).astype(BF)
    digits = digits_of(count)

    def other_core(value):
        return swap(value, 2, 1, "mp")

    def both(own, away):
        return jnp.where(
            core == 0, jnp.concatenate([own, away], axis=-1), jnp.concatenate([away, own], axis=-1)
        )

    def bring(value):
        own = lax.dynamic_index_in_dim(value, core, 0, keepdims=False)
        away = other_core(lax.dynamic_index_in_dim(value, 1 - core, 0, keepdims=False))
        return both(own, away)

    def early_start(held):
        for place_in in digits[:1:-1]:
            held = gather_place(gather_start(held, count, place_in), index, place_in)
        return gather_start(held, count, digits[1])

    def early_place(pieces):
        return gather_place(pieces, index, digits[1])

    def late_start(held):
        return gather_start(held, count, digits[0])

    def late_place(pieces):
        return gather_place(pieces, index, digits[0]).reshape(D, -1)

    one = early_start(shard_qkv[None])
    x = bring(tokens)
    vectors = jnp.concatenate([hidden_gates.astype(F32)[None], norm_params], axis=0)
    vectors = both(vectors, other_core(vectors))
    hidden_mask, params = vectors[0], vectors[1:]
    segment = lax.dynamic_index_in_dim(segments, core, 0, keepdims=False)[0]
    tables = segment_tables(segment)
    one = late_start(early_place(one))
    two = early_start(tie(shard_two[None], one[0]))
    one = tie(one, x, *tables)
    mine_qkv = late_place(one)
    away_qkv = other_core(mine_qkv)
    two = late_start(early_place(tie(two, mine_qkv)))
    back = early_start(tie(shard_back[None], two[0]))
    qkv_own = dot(tie(x, two[0]), mine_qkv, NN).astype(BF)
    ctx_own, lse_own = attend_forward(qkv_own, tables)
    two = tie(two, ctx_own)
    mine_two = late_place(two)
    away_two = other_core(mine_two)
    back = late_start(early_place(tie(back, mine_two)))
    qkv_away = dot(tie(x, back[0]), away_qkv, NN).astype(BF)
    ctx_away, lse_away = attend_forward(qkv_away, tables)
    ctx = (ctx_own, ctx_away)
    lse = (lse_own, lse_away)
    qkv = (qkv_own, qkv_away)
    qkv_sides = (mine_qkv, away_qkv)
    away_two = tie(away_two, ctx_away)
    in_sides = (mine_two[:, : 4 * half], away_two[:, : 4 * half])
    out_sides = (mine_two[:, 4 * half :], away_two[:, 4 * half :])
    attn = dot(ctx[0], out_sides[0], NT) + dot(ctx[1], out_sides[1], NT)
    resid_one = x.astype(F32) + (gate_attn * hidden_mask) * attn
    normed, centred_one, inv_one = norm_forward(resid_one, params[0], params[1])
    normed_low = normed.astype(BF)
    act_own, slope_own = ffn_in(normed_low, in_sides[0])
    back = tie(back, act_own)
    mine_back = late_place(back)
    away_back = other_core(mine_back)
    grad_out = bring(cotangent)
    act_away, slope_away = ffn_in(tie(normed_low, mine_back), in_sides[1])
    acts, slopes = (act_own, act_away), (slope_own, slope_away)
    back_sides = (mine_back, tie(away_back, act_away))
    ffn = dot(acts[0], back_sides[0], NT) + dot(acts[1], back_sides[1], NT)
    resid_two = normed + (gate_ffn * hidden_mask) * ffn
    result, centred_two, inv_two = norm_forward(resid_two, params[2], params[3])

    grad_two, dgain_two, dshift_two = norm_backward(
        grad_out.astype(F32), centred_two, inv_two, params[2]
    )
    grad_ffn = ((gate_ffn * hidden_mask) * grad_two).astype(BF)

    def first_scatter(own, arrived):
        return scatter_start([own, arrived], count, index, digits[0], rows)

    def next_scatter(terms, level):
        return scatter_start(terms, count, index, digits[level], rows)

    def rest_scatter(terms, level):
        while level < len(digits):
            _, terms = next_scatter(terms, level)
            level += 1
        return terms

    back_away = dot(grad_ffn, acts[1], TN).astype(BF)
    back_own = dot(grad_ffn, acts[0], TN).astype(BF)
    back_arrived = other_core(back_away)
    grad_ffn_b = tie(grad_ffn, back_away, back_own)
    grad_pre = [
        (dot(grad_ffn_b, back_sides[s], NN) * slopes[s].astype(F32)).astype(BF) for s in range(2)
    ]
    back_arrived = tie(back_arrived, *grad_pre)
    back_parts, back_terms = first_scatter(back_own, back_arrived)
    normed_b = tie(normed_low, *back_parts)
    in_away = dot(normed_b, grad_pre[1], TN).astype(BF)
    in_own = dot(normed_b, grad_pre[0], TN).astype(BF)
    in_arrived = other_core(in_away)
    grad_pre_b = tie(grad_pre, in_away, in_own)
    grad_normed = grad_two + (dot(grad_pre_b[0], in_sides[0], NT) + dot(grad_pre_b[1], in_sides[1], NT))
    grad_one, dgain_one, dshift_one = norm_backward(grad_normed, centred_one, inv_one, params[0])
    grad_attn = ((gate_attn * hidden_mask) * grad_one).astype(BF)
    out_away = dot(grad_attn, ctx[1], TN).astype(BF)
    out_own = dot(grad_attn, ctx[0], TN).astype(BF)
    out_arrived = other_core(out_away)
    dctx = [dot(grad_attn, side, NN).astype(BF) for side in out_sides]
    back_terms = tie(back_terms, dctx[1])
    back_last = rest_scatter(back_terms, 1)
    two_own = jnp.concatenate([in_own, out_own], axis=1)
    two_arrived = jnp.concatenate([in_arrived, out_arrived], axis=1)
    two_parts, two_terms = first_scatter(two_own, two_arrived)
    dctx = tie(dctx, *two_parts)
    dqkv_away = attend_backward(qkv[1], dctx[1], ctx[1], lse[1], tables)
    gq_away = dot(x, dqkv_away, TN).astype(BF)
    gq_arrived = other_core(gq_away)
    two_terms = tie(two_terms, gq_away)
    two_last = rest_scatter(two_terms, 1)
    dctx_own = tie(dctx[0], gq_away)
    dqkv_own = attend_backward(qkv[0], dctx_own, ctx[0], lse[0], tables)
    gq_own = dot(x, dqkv_own, TN).astype(BF)
    one_parts, one_terms = first_scatter(gq_own, gq_arrived)
    dqkv_own = tie(dqkv_own, *one_parts)
    grad_tok = grad_one + (dot(dqkv_own, qkv_sides[0], NT) + dot(dqkv_away, qkv_sides[1], NT))
    one_last = rest_scatter(one_terms, 1)

    def final(terms):
        total = terms[0].astype(F32)
        for term in terms[1:]:
            total = total + term.astype(F32)
        return total.reshape(rows, -1)

    sum_one, sum_two, sum_back = final(one_last), final(two_last), final(back_last)

    def send_back(value):
        first, second = value[:, :half], value[:, half:]
        own = jnp.where(core == 0, first, second)
        away = other_core(jnp.where(core == 0, second, first))
        return jnp.where(core == 0, jnp.stack([own, away]), jnp.stack([away, own]))

    out_tokens = send_back(result.astype(BF))
    input_grad = send_back(grad_tok.astype(BF))

    sum_qkv = sum_one.reshape(rows, pairs, 3, PAIR).transpose(2, 0, 1, 3).reshape(3, rows, half)
    sum_in = sum_two[:, : 4 * half]
    sum_out = (sum_two[:, 4 * half :] * head_mask[None, :]).T
    sum_wb = (sum_back * unit_mask[None, :]).T
    sums = (sum_qkv, sum_out, sum_in, sum_wb)
    square = sum(jnp.sum(g * g) for g in sums)
    norm_rows = jnp.stack([dgain_one, dshift_one, dgain_two, dshift_two]).reshape(-1, 128)
    packed = jnp.concatenate([norm_rows, jnp.full((8, 128), square / 1024.0, F32)], axis=0)
    packed = sum_all(packed, count)
    norm_full = packed[:-8].reshape(4, D)
    total_square = jnp.sum(packed[-8:]) + jnp.sum(norm_full * norm_full)
    grad_norm = jnp.sqrt(total_square)
    factor = jnp.minimum(1.0, CLIP_NORM / grad_norm)
    norm_here = lax.dynamic_slice_in_dim(norm_full, core * half, half, 1)
    weights = (w_qkv, w_out, w_in, w_back, norm_params)
    firsts = (mom_qkv, mom_out, mom_in, mom_back, mom_norm)
    seconds = (sec_qkv, sec_out, sec_in, sec_back, sec_norm)
    results = []
    for slot, gradient in enumerate(sums + (norm_here,)):
        results.append(
            adam_step(
                weights[slot],
                gradient * factor,
                firsts[slot],
                seconds[slot],
                LEARN_RATE if slot < 4 else NORM_RATE,
                WEIGHT_DECAY if slot < 4 else 0.0,
            )
        )
    return (
        out_tokens,
        input_grad,
        grad_norm,
        *[r[0] for r in results],
        *[r[1] for r in results],
        *[r[2] for r in results],
    )


def solution(mesh):
    weight_specs = (P(None, "dp", "mp"), P("mp", "dp"), P("dp", "mp"), P("mp", "dp"), P(None, "mp"))
    in_specs = (
        P(None, "dp", "mp"),
        P(None, "dp", "mp"),
        P(None, "dp", None),
        P("mp"),
        P("mp"),
        P("mp"),
        P(),
    ) + weight_specs * 3
    out_specs = (P(None, "dp", "mp"), P(None, "dp", "mp"), P()) + weight_specs * 3
    count = mesh.shape["dp"]

    def body(*args):
        return shards(count, *args)

    return jax.shard_map(body, mesh=mesh, in_specs=in_specs, out_specs=out_specs, check_vma=False)
```

```python
import functools

import jax
import jax.numpy as jnp
from jax import lax
from jax.experimental import pallas as pl
from jax.experimental.pallas import tpu as pltpu
from jax.sharding import PartitionSpec as P

D = 768
HEAD_DIM = 64
SEQ = 1024
STEP = 10
TILE = 256
TILES = SEQ // TILE
PAIR = 128

LN_EPS = 1e-12
CLIP_NORM = 1.0
LEARN_RATE = 0.06
NORM_RATE = 0.3
WEIGHT_DECAY = 0.01
BETA_ONE = 0.9
BETA_TWO = 0.999
ADAM_EPS = 1e-08
ATTN_SCALE = HEAD_DIM ** (-0.5)
MASK_STEP = float(2**30)
NT = (((1,), (1,)), ((), ()))
NN = (((1,), (0,)), ((), ()))
TN = (((0,), (0,)), ((), ()))
BF = jnp.bfloat16
F32 = jnp.float32
SMALL = pl.CostEstimate(flops=1024, bytes_accessed=1024, transcendentals=0)


def dot(left, right, dims):
    return lax.dot_general(left, right, dims, preferred_element_type=F32)


def spent(microseconds):
    return pl.CostEstimate(flops=int(microseconds * 1.1e9), bytes_accessed=1024, transcendentals=0)


def params_of(mebibytes):
    return pltpu.CompilerParams(vmem_limit_bytes=mebibytes << 20)


def whole(shape):
    return pl.BlockSpec(shape, lambda *_: (0,) * len(shape))


def row_tile(tile, cols):
    return pl.BlockSpec((tile, cols), lambda r: (r, 0))


def sds(shape, dtype):
    return jax.ShapeDtypeStruct(shape, dtype)


def row_sum(value):
    return jnp.sum(value, axis=1, keepdims=True)


def segment_tables(segment):
    first = segment[::TILE]
    last = segment[TILE - 1 :: TILE]
    low = jnp.sum((last[None, :] < first[:, None]).astype(jnp.int32), axis=1)
    high = jnp.sum((first[None, :] <= last[:, None]).astype(jnp.int32), axis=1)
    lane = lax.broadcasted_iota(jnp.int32, (SEQ, PAIR), 1) % HEAD_DIM
    same = lane == segment[:, None]
    key_lanes = jnp.where(same, 1.0, 0.0).astype(BF)
    query_lanes = jnp.where((lane < 4) & (~same), -MASK_STEP, 0.0).astype(BF)
    return low, high, key_lanes, query_lanes


def attend_fwd_kernel(
    low_ref, high_ref, x_ref, w_ref, klane_ref, qlane_ref, qkv_ref, ctx_ref, lse_ref, kh_ref, qh_ref, ls_ref
):
    qkv_ref[...] = dot(x_ref[...], w_ref[...], NN).astype(BF)
    lane = lax.broadcasted_iota(jnp.int32, (SEQ, PAIR), 1)
    query = qkv_ref[:, 0:PAIR] * ATTN_SCALE
    keys = qkv_ref[:, PAIR : 2 * PAIR]
    for h in range(2):
        mine = (lane // HEAD_DIM) == h
        kh_ref[h] = jnp.where(mine, keys, klane_ref[...])
        qh_ref[h] = jnp.where(mine, query, qlane_ref[...])
    is_first = lax.broadcasted_iota(jnp.int32, (TILE, PAIR), 1) < HEAD_DIM

    def row_block(qb, carry):
        low = low_ref[qb]
        count = high_ref[qb] - low
        rows = pl.ds(pl.multiple_of(qb * TILE, TILE), TILE)
        for width in range(1, TILES + 1):

            @pl.when(count == width)
            def _():
                span = pl.ds(pl.multiple_of(low * TILE, TILE), width * TILE)
                scores = [dot(qh_ref[h, rows, :], kh_ref[h, span, :], NT) for h in range(2)]
                tops = [jnp.max(s, axis=1, keepdims=True) for s in scores]
                expo = [jnp.exp(s - m) for s, m in zip(scores, tops)]
                sums = [jnp.sum(p, axis=1, keepdims=True) for p in expo]
                outs = [dot(p.astype(BF), qkv_ref[span, 2 * PAIR : 3 * PAIR], NN) for p in expo]
                ctx_ref[rows, :] = jnp.where(is_first, outs[0] / sums[0], outs[1] / sums[1]).astype(BF)
                ls_ref[rows, :] = jnp.where(
                    is_first, tops[0] + jnp.log(sums[0]), tops[1] + jnp.log(sums[1])
                )

        return carry

    lax.fori_loop(0, TILES, row_block, 0)
    turned = ls_ref[...].T
    lse_ref[0, 0:1, :] = turned[0:1]
    lse_ref[0, 1:2, :] = turned[HEAD_DIM : HEAD_DIM + 1]


def attend_forward(x, weight, tables):
    pairs = weight.shape[1] // (3 * PAIR)
    low, high, key_lanes, query_lanes = tables
    table = pl.BlockSpec((SEQ, PAIR), lambda p, *_: (0, 0))
    return pl.pallas_call(
        attend_fwd_kernel,
        grid_spec=pltpu.PrefetchScalarGridSpec(
            num_scalar_prefetch=2,
            grid=(pairs,),
            in_specs=[
                pl.BlockSpec((SEQ, D), lambda p, *_: (0, 0)),
                pl.BlockSpec((D, 3 * PAIR), lambda p, *_: (0, p)),
                table,
                table,
            ],
            out_specs=[
                pl.BlockSpec((SEQ, 3 * PAIR), lambda p, *_: (0, p)),
                pl.BlockSpec((SEQ, PAIR), lambda p, *_: (0, p)),
                pl.BlockSpec((1, 2, SEQ), lambda p, *_: (p, 0, 0)),
            ],
            scratch_shapes=[
                pltpu.VMEM((2, SEQ, PAIR), BF),
                pltpu.VMEM((2, SEQ, PAIR), BF),
                pltpu.VMEM((SEQ, PAIR), F32),
            ],
        ),
        out_shape=[
            sds((SEQ, pairs * 3 * PAIR), BF),
            sds((SEQ, pairs * PAIR), BF),
            sds((pairs, 2, SEQ), F32),
        ],
        compiler_params=params_of(24),
        cost_estimate=spent(11),
        name="attend_fwd",
    )(low, high, x, weight, key_lanes, query_lanes)


def attend_bwd_kernel(
    low_ref, high_ref, qkv_ref, dctx_ref, ctx_ref, lse_ref, klane_ref, qlane_ref, xt_ref, dqkv_ref, gq_ref,
    kh_ref, qh_ref, kt_ref, q0_ref, d0_ref, delta_ref, dqt_ref,
):
    lane = lax.broadcasted_iota(jnp.int32, (SEQ, PAIR), 1)
    query = qkv_ref[:, 0:PAIR] * ATTN_SCALE
    keys = qkv_ref[:, PAIR : 2 * PAIR]
    dctx = dctx_ref[...]
    kt_ref[...] = keys.T
    prod = (dctx.astype(F32) * ctx_ref[...].astype(F32)).T
    zero = jnp.zeros((SEQ, PAIR), BF)
    for h in range(2):
        mine = (lane // HEAD_DIM) == h
        kh_ref[h] = jnp.where(mine, keys, klane_ref[...])
        qh_ref[h] = jnp.where(mine, query, qlane_ref[...])
        q0_ref[h] = jnp.where(mine, query, zero)
        d0_ref[h] = jnp.where(mine, dctx, zero)
        delta_ref[h : h + 1, :] = jnp.sum(
            prod[h * HEAD_DIM : (h + 1) * HEAD_DIM], axis=0, keepdims=True
        )
    dqt_ref[...] = jnp.zeros((PAIR, SEQ), F32)

    def key_block(kb, carry):
        low = low_ref[kb]
        count = high_ref[kb] - low
        cols = pl.ds(pl.multiple_of(kb * TILE, TILE), TILE)
        for width in range(1, TILES + 1):

            @pl.when(count == width)
            def _():
                span = pl.ds(pl.multiple_of(low * TILE, TILE), width * TILE)
                values = qkv_ref[cols, 2 * PAIR : 3 * PAIR]
                scores = [dot(kh_ref[h, cols, :], qh_ref[h, span, :], NT) for h in range(2)]
                dprob = [dot(values, d0_ref[h, span, :], NT) for h in range(2)]
                prob = [jnp.exp(scores[h] - lse_ref[0, h : h + 1, span]) for h in range(2)]
                low_p = [p.astype(BF) for p in prob]
                dscore = [
                    (prob[h] * (dprob[h] - delta_ref[h : h + 1, span])).astype(BF) for h in range(2)
                ]
                dvals = dot(low_p[0], d0_ref[0, span, :], NN) + dot(low_p[1], d0_ref[1, span, :], NN)
                dkeys = dot(dscore[0], q0_ref[0, span, :], NN) + dot(dscore[1], q0_ref[1, span, :], NN)
                for h in range(2):
                    part = slice(h * HEAD_DIM, (h + 1) * HEAD_DIM)
                    dqt_ref[part, span] += dot(kt_ref[part, cols], dscore[h], NN)
                dqkv_ref[cols, PAIR : 2 * PAIR] = dkeys.astype(BF)
                dqkv_ref[cols, 2 * PAIR : 3 * PAIR] = dvals.astype(BF)

        return carry

    lax.fori_loop(0, TILES, key_block, 0)
    dqkv_ref[:, 0:PAIR] = (dqt_ref[...].T * ATTN_SCALE).astype(BF)
    gq_ref[...] = dot(xt_ref[...], dqkv_ref[...], NN).astype(BF)


def attend_backward(qkv, dctx, ctx, lse, tables, xt):
    pairs = qkv.shape[1] // (3 * PAIR)
    low, high, key_lanes, query_lanes = tables
    table = pl.BlockSpec((SEQ, PAIR), lambda p, *_: (0, 0))
    column = pl.BlockSpec((SEQ, PAIR), lambda p, *_: (0, p))
    triple = pl.BlockSpec((SEQ, 3 * PAIR), lambda p, *_: (0, p))
    return pl.pallas_call(
        attend_bwd_kernel,
        grid_spec=pltpu.PrefetchScalarGridSpec(
            num_scalar_prefetch=2,
            grid=(pairs,),
            in_specs=[
                triple,
                column,
                column,
                pl.BlockSpec((1, 2, SEQ), lambda p, *_: (p, 0, 0)),
                table,
                table,
                pl.BlockSpec((D, SEQ), lambda p, *_: (0, 0)),
            ],
            out_specs=[triple, pl.BlockSpec((D, 3 * PAIR), lambda p, *_: (0, p))],
            scratch_shapes=[
                pltpu.VMEM((2, SEQ, PAIR), BF),
                pltpu.VMEM((2, SEQ, PAIR), BF),
                pltpu.VMEM((PAIR, SEQ), BF),
                pltpu.VMEM((2, SEQ, PAIR), BF),
                pltpu.VMEM((2, SEQ, PAIR), BF),
                pltpu.VMEM((2, SEQ), F32),
                pltpu.VMEM((PAIR, SEQ), F32),
            ],
        ),
        out_shape=[sds((SEQ, pairs * 3 * PAIR), BF), sds((D, pairs * 3 * PAIR), BF)],
        compiler_params=params_of(28),
        cost_estimate=spent(15),
        name="attend_bwd",
    )(low, high, qkv, dctx, ctx, lse, key_lanes, query_lanes, xt)


def mid_kernel(ctx_a, ctx_b, wo_a, wo_b, x_ref, vec_ref, cen_ref, inv_ref, low_ref, lowt_ref):
    attn = dot(ctx_a[...], wo_a[...], NT) + dot(ctx_b[...], wo_b[...], NT)
    res = x_ref[...].astype(F32) + vec_ref[0:1,:]*attn
    mean = row_sum(res)/D
    var = row_sum(res*res)/D - mean*mean
    inv = lax.rsqrt(var+LN_EPS)
    cen = (res-mean)*inv
    cen_ref[...] = cen
    inv_ref[...] = jnp.broadcast_to(inv, inv_ref.shape)
    low = (cen*vec_ref[2:3,:]+vec_ref[3:4,:]).astype(BF)
    low_ref[...] = low
    lowt_ref[...] = low.T

def mid(ctx, two, x, vec, T=256):
    half = D//2
    wo = lambda: pl.BlockSpec((D, half), lambda r: (0, 4))
    return pl.pallas_call(mid_kernel, grid=(SEQ//T,),
        in_specs=[row_tile(T,half), row_tile(T,half), wo(), wo(), row_tile(T,D), whole((8,D))],
        out_specs=[row_tile(T,D), row_tile(T,128), row_tile(T,D), pl.BlockSpec((D,T), lambda r:(0,r))],
        out_shape=[sds((SEQ,D),F32), sds((SEQ,128),F32), sds((SEQ,D),BF), sds((D,SEQ),BF)],
        compiler_params=params_of(32), cost_estimate=spent(4), name="mid")(ctx[0],ctx[1],two[0],two[1],x,vec)

def gelu_pair(value):
    phi = 0.5 + 0.5 * lax.erf(value * 0.7071067811865476)
    bell = jnp.exp(-0.5 * value * value)
    return value * phi, phi + value * bell * 0.3989422804014327

def ffn_in_kernel(x_ref, w_ref, act_ref, slope_ref):
    pre = dot(x_ref[...], w_ref[...], NN)
    act, slope = gelu_pair(pre)
    act_ref[...] = act.astype(BF)
    slope_ref[...] = slope.astype(BF)

def ffn_in(low, two, width=256):
    units = 4*(D//2)
    return pl.pallas_call(ffn_in_kernel, grid=(units//width,),
        in_specs=[whole((SEQ,D)), pl.BlockSpec((D,width), lambda n:(0,n))],
        out_specs=[pl.BlockSpec((SEQ,width), lambda n:(0,n))]*2,
        out_shape=[sds((SEQ,units),BF)]*2,
        compiler_params=params_of(32), cost_estimate=spent(5.5), name="ffn_in")(low, two)

def ffn_out_kernel(act_a, act_b, wb_a, wb_b, cen_ref, cot_ref, vec_ref, res_ref, gtwo_ref, gffnt_ref, gffn_ref, dn_ref):
    ffn = dot(act_a[...], wb_a[...], NT) + dot(act_b[...], wb_b[...], NT)
    normed = cen_ref[...]*vec_ref[2:3,:]+vec_ref[3:4,:]
    res = normed + vec_ref[1:2,:]*ffn
    mean = row_sum(res)/D
    var = row_sum(res*res)/D - mean*mean
    inv = lax.rsqrt(var+LN_EPS)
    cen = (res-mean)*inv
    gain = vec_ref[4:5,:]
    res_ref[...] = (cen*gain+vec_ref[5:6,:]).astype(BF)
    cot = cot_ref[...].astype(F32)
    scaled = cot*gain
    m1 = row_sum(scaled)/D
    m2 = row_sum(scaled*cen)/D
    gtwo = inv*(scaled-m1-cen*m2)
    gtwo_ref[...] = gtwo
    gffn = (vec_ref[1:2,:]*gtwo).astype(BF)
    gffn_ref[...] = gffn
    gffnt_ref[...] = gffn.T
    @pl.when(pl.program_id(0)==0)
    def _(): dn_ref[...] = jnp.zeros(dn_ref.shape, F32)
    dn_ref[0:1,:] += jnp.sum(cot*cen, axis=0, keepdims=True)
    dn_ref[1:2,:] += jnp.sum(cot, axis=0, keepdims=True)

def ffn_out(acts, back, cen, cot, vec, T=256):
    units = 4*(D//2)
    return pl.pallas_call(ffn_out_kernel, grid=(SEQ//T,),
        in_specs=[row_tile(T,units), row_tile(T,units), whole((D,units)), whole((D,units)), row_tile(T,D), row_tile(T,D), whole((8,D))],
        out_specs=[row_tile(T,D), row_tile(T,D), pl.BlockSpec((D,T), lambda r:(0,r)), row_tile(T,D), whole((8,D))],
        out_shape=[sds((SEQ,D),BF), sds((SEQ,D),F32), sds((D,SEQ),BF), sds((SEQ,D),BF), sds((8,D),F32)],
        compiler_params=params_of(32), cost_estimate=spent(10), name="ffn_out")(acts[0],acts[1],back[0],back[1],cen,cot,vec)

def grad_back_kernel(lt_ref, own_ref, away_ref, gown_ref, gaway_ref):
    gaway_ref[...] = dot(lt_ref[...], away_ref[...], NN).astype(BF)
    gown_ref[...] = dot(lt_ref[...], own_ref[...], NN).astype(BF)

def grad_back(lt, acts, width=512):
    units = acts[0].shape[1]
    col = pl.BlockSpec((SEQ,width), lambda n:(0,n)); out=pl.BlockSpec((D,width), lambda n:(0,n))
    return pl.pallas_call(grad_back_kernel, grid=(units//width,),
        in_specs=[whole((D,SEQ)), col, col], out_specs=[out,out],
        out_shape=[sds((D,units),BF)]*2,
        compiler_params=params_of(32), cost_estimate=spent(6.5), name="grad_back")(lt, acts[0], acts[1])

def inner_bwd_kernel(gffn_ref, sl_a, sl_b, wb_a, wb_b, wi_a, wi_b, wo_a, wo_b, gtwo_ref, cen_ref, inv_ref, vec_ref,
                pre_a, pre_b, gone_ref, gattnt_ref, dctx_a, dctx_b, dn_ref):
    gffn = gffn_ref[...]
    pa = (dot(gffn, wb_a[...], NN)*sl_a[...].astype(F32)).astype(BF)
    pre_a[...] = pa
    pb = (dot(gffn, wb_b[...], NN)*sl_b[...].astype(F32)).astype(BF)
    pre_b[...] = pb
    gn = gtwo_ref[...] + dot(pa, wi_a[...], NT) + dot(pb, wi_b[...], NT)
    cen = cen_ref[...]
    scaled = gn*vec_ref[2:3,:]
    m1 = row_sum(scaled)/D
    m2 = row_sum(scaled*cen)/D
    inv = inv_ref[:,0:1]
    gone = inv*(scaled-m1-cen*m2)
    gone_ref[...] = gone
    gattn = (vec_ref[0:1,:]*gone).astype(BF)
    gattnt_ref[...] = gattn.T
    dctx_a[...] = dot(gattn, wo_a[...], NN).astype(BF)
    dctx_b[...] = dot(gattn, wo_b[...], NN).astype(BF)
    @pl.when(pl.program_id(0)==0)
    def _(): dn_ref[...] = jnp.zeros(dn_ref.shape, F32)
    dn_ref[0:1,:] += jnp.sum(gn*cen, axis=0, keepdims=True)
    dn_ref[1:2,:] += jnp.sum(gn, axis=0, keepdims=True)

def inner_bwd(gffn, slopes, back, two, gtwo, cen, inv, vec, T=256):
    half=D//2; units=4*half
    wi = lambda: pl.BlockSpec((D,units), lambda r:(0,0))
    wo = lambda: pl.BlockSpec((D,half), lambda r:(0,4))
    return pl.pallas_call(inner_bwd_kernel, grid=(SEQ//T,),
        in_specs=[row_tile(T,D), row_tile(T,units), row_tile(T,units), whole((D,units)), whole((D,units)), wi(), wi(), wo(), wo(), row_tile(T,D), row_tile(T,D), row_tile(T,128), whole((8,D))],
        out_specs=[row_tile(T,units), row_tile(T,units), row_tile(T,D), pl.BlockSpec((D,T), lambda r:(0,r)), row_tile(T,half), row_tile(T,half), whole((8,D))],
        out_shape=[sds((SEQ,units),BF)]*2+[sds((SEQ,D),F32), sds((D,SEQ),BF), sds((SEQ,half),BF), sds((SEQ,half),BF), sds((8,D),F32)],
        compiler_params=params_of(44), cost_estimate=spent(20), name="inner_bwd")(gffn,slopes[0],slopes[1],back[0],back[1],two[0],two[1],two[0],two[1],gtwo,cen,inv,vec)

def grad_weights_two_kernel(lowt_ref, gattnt_ref, pre_own, pre_away, ctx_own, ctx_away, gown_ref, gaway_ref):
    n = pl.program_id(0)
    @pl.when(n<4)
    def _():
        gaway_ref[...] = dot(lowt_ref[...], pre_away[...], NN).astype(BF)
        gown_ref[...] = dot(lowt_ref[...], pre_own[...], NN).astype(BF)
    @pl.when(n==4)
    def _():
        gaway_ref[...] = dot(gattnt_ref[...], ctx_away[...], NN).astype(BF)
        gown_ref[...] = dot(gattnt_ref[...], ctx_own[...], NN).astype(BF)

def grad_weights_two(lowt, gattnt, pre, ctx):
    half=D//2
    col = lambda: pl.BlockSpec((SEQ,half), lambda n:(0,jnp.minimum(n,3)))
    out = pl.BlockSpec((D,half), lambda n:(0,n))
    return pl.pallas_call(grad_weights_two_kernel, grid=(5,),
        in_specs=[whole((D,SEQ)), whole((D,SEQ)), col(), col(), whole((SEQ,half)), whole((SEQ,half))],
        out_specs=[out,out], out_shape=[sds((D,5*half),BF)]*2,
        compiler_params=params_of(32), cost_estimate=spent(9), name="grad_weights_two")(lowt,gattnt,pre[0],pre[1],ctx[0],ctx[1])

def grad_tokens_kernel(gone_ref, d_a, d_b, w_a, w_b, out_ref):
    out_ref[...] = (gone_ref[...] + dot(d_a[...], w_a[...], NT) + dot(d_b[...], w_b[...], NT)).astype(BF)

def grad_tokens(gone, dqkv, wq, T=256):
    c=dqkv[0].shape[1]
    return pl.pallas_call(grad_tokens_kernel, grid=(SEQ//T,),
        in_specs=[row_tile(T,D), row_tile(T,c), row_tile(T,c), whole((D,c)), whole((D,c))],
        out_specs=row_tile(T,D), out_shape=sds((SEQ,D),BF),
        compiler_params=params_of(32), cost_estimate=spent(6), name="grad_tokens")(gone,dqkv[0],dqkv[1],wq[0],wq[1])


def side_by_side_kernel(core_ref, own_ref, away_ref, out_ref, turned_ref):
    half = own_ref.shape[1]
    first = jnp.where(core_ref[0] == 0, own_ref[...], away_ref[...])
    second = jnp.where(core_ref[0] == 0, away_ref[...], own_ref[...])
    out_ref[:, :half] = first
    out_ref[:, half:] = second
    turned_ref[:half, :] = first.T
    turned_ref[half:, :] = second.T


def side_by_side(own, away, core):
    half = own.shape[1]
    tile = 256
    return pl.pallas_call(
        side_by_side_kernel,
        grid_spec=pltpu.PrefetchScalarGridSpec(
            num_scalar_prefetch=1,
            grid=(SEQ // tile,),
            in_specs=[pl.BlockSpec((tile, half), lambda r, c: (r, 0))] * 2,
            out_specs=[
                pl.BlockSpec((tile, 2 * half), lambda r, c: (r, 0)),
                pl.BlockSpec((2 * half, tile), lambda r, c: (0, r)),
            ],
        ),
        out_shape=[sds((SEQ, 2 * half), BF), sds((2 * half, SEQ), BF)],
        compiler_params=params_of(8),
        cost_estimate=spent(1.5),
        name="side_by_side",
    )(core[None], own, away)


def digits_of(count):
    found, shift = [], 0
    while (1 << shift) < count:
        radix = min(4, count >> shift)
        found.append((shift, radix))
        shift += 2 if radix == 4 else 1
    return found


def swap(value, count, mask, axis="dp"):
    return lax.ppermute(value, axis, [(i, i ^ mask) for i in range(count)])


def tie(value, *others):
    flat, tree = jax.tree.flatten(value)
    return jax.tree.unflatten(tree, lax.optimization_barrier(tuple(flat) + others)[: len(flat)])


def place_kernel(digit_ref, *refs, radix, widths):
    pieces, outs = refs[:radix], refs[radix:]
    for j, piece in enumerate(pieces):

        @pl.when(pl.program_id(0) == j)
        def _():
            start = 0
            for out, width in zip(outs, widths):
                out[:, 0] = piece[:, :, start : start + width]
                start += width


def place(pieces, digit, widths=None):
    outer, rows, cols = pieces[0].shape
    radix = len(pieces)
    widths = widths or (cols,)
    placed = pl.pallas_call(
        functools.partial(place_kernel, radix=radix, widths=widths),
        grid_spec=pltpu.PrefetchScalarGridSpec(
            num_scalar_prefetch=1,
            grid=(radix,),
            in_specs=[pl.BlockSpec((outer, rows, cols), lambda g, d: (0, 0, 0))] * radix,
            out_specs=[
                pl.BlockSpec((outer, 1, rows, width), lambda g, d: (0, d[0] ^ g, 0, 0)) for width in widths
            ],
        ),
        out_shape=[jax.ShapeDtypeStruct((outer, radix, rows, width), pieces[0].dtype) for width in widths],
        compiler_params=pltpu.CompilerParams(vmem_limit_bytes=32 << 20),
        cost_estimate=spent(1.2),
        name="place",
    )(digit[None], *pieces)
    placed = [p.reshape(outer * radix, rows, p.shape[-1]) for p in placed]
    return placed if len(widths) > 1 else placed[0]


def place_two_kernel(digit_ref, a_own, a_got, b_own, b_got, out):
    y = pl.program_id(0) // 2
    x = pl.program_id(0) % 2
    width = a_own.shape[-1]
    for source, hit in ((a_own, x == digit_ref[1]), (a_got, x != digit_ref[1])):

        @pl.when(hit)
        def _():
            out[:, 0, 0, :, :width] = source[:, 0]

    for source, hit in ((b_own, y == digit_ref[0]), (b_got, y != digit_ref[0])):

        @pl.when(hit)
        def _():
            out[:, 0, 0, :, width:] = source[:, 0]


def place_two(a_pieces, b_pieces, digit_y, digit_x):
    outer, rows, a_width = a_pieces[0].shape
    b_width = b_pieces[0].shape[-1]
    outer //= 2
    a_spec = pl.BlockSpec((outer, 1, rows, a_width), lambda g, d: (0, g // 2, 0, 0))
    b_spec = pl.BlockSpec((outer, 1, rows, b_width), lambda g, d: (0, g % 2, 0, 0))
    shaped = [p.reshape(outer, 2, rows, -1) for p in (*a_pieces, *b_pieces)]
    return pl.pallas_call(
        place_two_kernel,
        grid_spec=pltpu.PrefetchScalarGridSpec(
            num_scalar_prefetch=1,
            grid=(4,),
            in_specs=[a_spec, a_spec, b_spec, b_spec],
            out_specs=pl.BlockSpec(
                (outer, 1, 1, rows, a_width + b_width), lambda g, d: (0, g // 2, g % 2, 0, 0)
            ),
        ),
        out_shape=jax.ShapeDtypeStruct((outer, 2, 2, rows, a_width + b_width), BF),
        compiler_params=pltpu.CompilerParams(vmem_limit_bytes=32 << 20),
        cost_estimate=spent(2),
        name="place_two",
    )(jnp.stack([digit_y, digit_x]), *shaped).reshape(outer * 4 * rows, -1)


def sum_split_kernel(digit_ref, *refs, terms):
    total = refs[0][:, 0].astype(F32)
    for ref in refs[1:terms]:
        total = total + ref[:, 0].astype(F32)
    total = total.astype(BF)
    for j, out in enumerate(refs[terms:]):

        @pl.when(pl.program_id(0) == j)
        def _():
            out[...] = total


def sum_split(terms, digit):
    outer, radix, rows, cols = terms[0].shape
    return pl.pallas_call(
        functools.partial(sum_split_kernel, terms=len(terms)),
        grid_spec=pltpu.PrefetchScalarGridSpec(
            num_scalar_prefetch=1,
            grid=(radix,),
            in_specs=[pl.BlockSpec((outer, 1, rows, cols), lambda g, d: (0, d[0] ^ g, 0, 0))] * len(terms),
            out_specs=[pl.BlockSpec((outer, rows, cols), lambda g, d: (0, 0, 0))] * radix,
        ),
        out_shape=[jax.ShapeDtypeStruct((outer, rows, cols), BF)] * radix,
        compiler_params=pltpu.CompilerParams(vmem_limit_bytes=40 << 20),
        cost_estimate=pl.CostEstimate(
            flops=0,
            bytes_accessed=2 * outer * radix * rows * cols * (len(terms) + 1),
            transcendentals=0,
        ),
        name="sum_split",
    )(digit[None], *terms)


def gather_start(held, count, place_in):
    shift, radix = place_in
    return [held] + [swap(held, count, j << shift) for j in range(1, radix)]


def gather_place(pieces, index, place_in, widths=None):
    shift, radix = place_in
    return place(pieces, (index >> shift) & (radix - 1), widths)


def scatter_split(terms, index, place_in, rows):
    shift, radix = place_in
    cols = terms[0].shape[-1]
    shaped = [t.reshape(-1, radix, rows, cols) for t in terms]
    return sum_split(shaped, (index >> shift) & (radix - 1))


def scatter_send(parts, count, place_in):
    return [parts[0]] + [swap(parts[j], count, j << place_in[0]) for j in range(1, place_in[1])]


def sum_all(value, count):
    value = value + swap(value, 2, 1, "mp")
    for shift, radix in digits_of(count):
        parts = [value] + [swap(value, count, j << shift) for j in range(1, radix)]
        value = parts[0] + parts[1]
        if radix == 4:
            value = value + (parts[2] + parts[3])
    return value


def adam_step(weight, gradient, first_mom, second, step_rate, decay_rate):
    first_new = BETA_ONE * first_mom + (1.0 - BETA_ONE) * gradient
    second_new = BETA_TWO * second + (1.0 - BETA_TWO) * gradient * gradient
    update = (
        first_new
        / (1.0 - BETA_ONE**STEP)
        / (jnp.sqrt(second_new / (1.0 - BETA_TWO**STEP)) + ADAM_EPS)
    )
    return (weight - step_rate * (update + decay_rate * weight), first_new, second_new)


def shards(
    count,
    tokens,
    cotangent,
    segments,
    head_gates,
    unit_gates,
    hidden_gates,
    layer_gates,
    w_qkv,
    w_out,
    w_in,
    w_back,
    norm_params,
    mom_qkv,
    mom_out,
    mom_in,
    mom_back,
    mom_norm,
    sec_qkv,
    sec_out,
    sec_in,
    sec_back,
    sec_norm,
):
    index = lax.axis_index("dp")
    core = lax.axis_index("mp")
    rows = D // count
    half = D // 2
    pairs = half // PAIR
    head_mask = jnp.repeat(head_gates.astype(F32), HEAD_DIM)
    unit_mask = unit_gates.astype(F32)
    gate_attn = layer_gates[0]
    gate_ffn = layer_gates[1]

    shard_qkv = (
        w_qkv.astype(BF).reshape(3, rows, pairs, PAIR).transpose(1, 2, 0, 3).reshape(rows, 3 * half)
    )
    shard_out = (w_out.T * head_mask[None, :]).astype(BF)
    shard_two = jnp.concatenate([w_in.astype(BF), shard_out], axis=1)
    shard_back = (w_back.T * unit_mask[None, :]).astype(BF)
    digits = digits_of(count)

    def other_core(value):
        return swap(value, 2, 1, "mp")

    def both(own, away):
        return jnp.where(
            core == 0, jnp.concatenate([own, away], axis=-1), jnp.concatenate([away, own], axis=-1)
        )

    def bring(value):
        own = lax.dynamic_index_in_dim(value, core, 0, keepdims=False)
        away = other_core(lax.dynamic_index_in_dim(value, 1 - core, 0, keepdims=False))
        return side_by_side(own, away, core)

    plane = digits[0]
    upper = [(bit, 2) for bit in range(plane[1] // 2, count.bit_length() - 1)]
    bit_y, bit_x = (index >> 1) & 1, index & 1

    def direct_start(held):
        for place_in in digits[:1:-1]:
            held = gather_place(gather_start(held, count, place_in), index, place_in)
        return gather_start(held, count, digits[1])

    def far_start(held):
        for place_in in upper[:0:-1]:
            held = gather_place(gather_start(held, count, place_in), index, place_in)
        return gather_start(held, count, upper[0])

    def halves_start(pieces, widths):
        a, b = gather_place(pieces, index, upper[0], widths)
        return [a, swap(a, count, 2)], [b, swap(b, count, 1)]

    def halves_turn(halves):
        a = place(halves[0], bit_y)
        b = place(halves[1], bit_x)
        return [a, swap(a, count, 1)], [b, swap(b, count, 2)]

    def halves_place(halves):
        return place_two(*halves, bit_y, bit_x)

    one = direct_start(shard_qkv[None])
    x, xt = bring(tokens)
    segment = lax.dynamic_index_in_dim(segments, core, 0, keepdims=False)[0]
    tables = segment_tables(segment)
    one = tie(one, x, *tables, shard_two, shard_back)
    one = gather_start(gather_place(one, index, digits[1]), count, plane)
    far = upper[-1]
    two = gather_start(tie(shard_two[None], one[0]), count, far)
    back = tie(shard_back[None], one[0])
    vectors = jnp.concatenate([hidden_gates.astype(F32)[None], norm_params], axis=0)
    vectors = both(vectors, other_core(vectors))
    hidden_mask, params = vectors[0], vectors[1:]
    vec = jnp.concatenate(
        [gate_attn * hidden_mask[None], gate_ffn * hidden_mask[None], params, params[:2]], axis=0
    )
    two = gather_place(tie(two, vec), index, far)
    for place_in in upper[-2:0:-1]:
        two = gather_place(gather_start(two, count, place_in), index, place_in)
    two = gather_start(two, count, upper[0])
    one = tie(one, two[0])
    mine_qkv = gather_place(one, index, plane).reshape(D, -1)
    away_qkv = other_core(mine_qkv)
    two = halves_start(tie(two, mine_qkv), (1024, 5 * half - 1024))
    back = gather_start(tie(back, two[0][0]), count, far)
    qkv_own, ctx_own, lse_own = attend_forward(tie(x, two[0][0], back[0]), mine_qkv, tables)
    two = halves_turn(tie(two, ctx_own))
    back = gather_place(tie(back, two[0][0], two[1][0]), index, far)
    for place_in in upper[-2:0:-1]:
        back = gather_place(gather_start(back, count, place_in), index, place_in)
    back = gather_start(back, count, upper[0])
    qkv_away, ctx_away, lse_away = attend_forward(tie(x, back[0]), away_qkv, tables)
    mine_two = halves_place(tie(two, ctx_away))
    away_two = other_core(mine_two)
    back = halves_start(tie(back, mine_two), (2 * half, 2 * half))
    ctx = (ctx_own, ctx_away)
    lse = (lse_own, lse_away)
    qkv = (qkv_own, qkv_away)
    qkv_sides = (mine_qkv, away_qkv)
    two_sides = (mine_two, away_two)
    centred_one, inv_one, normed_low, normed_turned = mid(ctx, two_sides, tie(x, back[0][0]), vec)
    act_own, slope_own = ffn_in(normed_low, mine_two)
    back = halves_turn(tie(back, act_own))
    grad_out, _ = bring(tie(cotangent, act_own))
    act_away, slope_away = ffn_in(tie(normed_low, back[0][0], back[1][0]), away_two)
    mine_back = halves_place(tie(back, act_away, grad_out))
    away_back = other_core(mine_back)
    acts, slopes = (act_own, act_away), (slope_own, slope_away)
    back_sides = (mine_back, away_back)
    result, grad_two, grad_ffn_turned, grad_ffn, dnorm_two = ffn_out(
        acts, back_sides, centred_one, grad_out, vec
    )

    def send_back(value):
        first, second = value[:, :half], value[:, half:]
        own = jnp.where(core == 0, first, second)
        away = other_core(jnp.where(core == 0, second, first))
        return jnp.where(core == 0, jnp.stack([own, away]), jnp.stack([away, own]))

    def split_first(own, arrived):
        return scatter_split([own, arrived], index, plane, rows)

    def split_bit(terms, level):
        return scatter_split(terms, index, upper[level], rows)

    def send_bit(parts, level):
        return scatter_send(parts, count, upper[level])

    def bits_but_last(terms):
        for level in range(len(upper) - 1):
            terms = send_bit(split_bit(terms, level), level)
        return terms

    back_own, back_away = grad_back(grad_ffn_turned, acts)
    back_arrived = other_core(back_away)
    out_tokens = send_back(result)
    pre_own, pre_away, grad_one, grad_attn_turned, dctx_own, dctx_away, dnorm_one = inner_bwd(
        tie(grad_ffn, back_own), slopes, back_sides, two_sides, grad_two, centred_one, inv_one, vec
    )
    out_tokens = tie(out_tokens, pre_own)
    back_parts = split_first(back_own, tie(back_arrived, pre_own, out_tokens))
    back_terms = scatter_send(back_parts, count, plane)
    two_own, two_away = grad_weights_two(
        tie(normed_turned, *back_parts), grad_attn_turned, (pre_own, pre_away), ctx
    )
    two_arrived = other_core(two_away)
    dqkv_away, gq_away = attend_backward(
        qkv[1], tie(dctx_away, two_own), ctx[1], lse[1], tables, xt
    )
    two_parts = split_first(two_own, tie(two_arrived, dqkv_away))
    back_parts = split_bit(tie(back_terms, *two_parts), 0)
    back_terms = send_bit(back_parts, 0)
    two_terms = scatter_send(two_parts, count, plane)
    gq_arrived = other_core(tie(gq_away, *back_parts))
    dqkv_own, gq_own = attend_backward(
        qkv[0], tie(dctx_own, gq_away, *back_parts), ctx[0], lse[0], tables, xt
    )
    back_terms = tie(back_terms, dqkv_own)
    for level in range(1, len(upper)):
        back_parts = split_bit(back_terms, level)
        back_terms = send_bit(back_parts, level)
    one_parts = split_first(gq_own, tie(gq_arrived, *back_parts))
    two_parts = split_bit(tie(two_terms, *one_parts), 0)
    two_terms = send_bit(two_parts, 0)
    one_terms = scatter_send(one_parts, count, plane)
    grad_tok = grad_tokens(tie(grad_one, *two_parts), (dqkv_own, dqkv_away), qkv_sides)
    two_terms = tie(two_terms, grad_tok)
    for level in range(1, len(upper)):
        two_parts = split_bit(two_terms, level)
        two_terms = send_bit(two_parts, level)
    input_grad = send_back(tie(grad_tok, *two_parts))
    back_last = tie(back_terms, *two_parts)
    one_terms = tie(one_terms, *two_parts)
    for place_in in digits[1:]:
        one_parts = scatter_split(one_terms, index, place_in, rows)
        one_terms = scatter_send(one_parts, count, place_in)
    two_last = tie(two_terms, *one_parts)
    input_grad = tie(input_grad, *one_parts)
    one_last = one_terms

    def final(terms):
        total = terms[0].astype(F32)
        for term in terms[1:]:
            total = total + term.astype(F32)
        return total.reshape(rows, -1)

    sum_one, sum_two, sum_back = final(one_last), final(two_last), final(back_last)

    sum_qkv = sum_one.reshape(rows, pairs, 3, PAIR).transpose(2, 0, 1, 3).reshape(3, rows, half)
    sum_in = sum_two[:, : 4 * half]
    sum_out = (sum_two[:, 4 * half :] * head_mask[None, :]).T
    sum_wb = (sum_back * unit_mask[None, :]).T
    sums = (sum_qkv, sum_out, sum_in, sum_wb)
    square = sum(jnp.sum(g * g) for g in sums)
    norm_rows = jnp.concatenate([dnorm_one[:2], dnorm_two[:2]]).reshape(-1, 128)
    packed = jnp.concatenate([norm_rows, jnp.full((8, 128), square / 1024.0, F32)], axis=0)
    packed = sum_all(packed, count)
    norm_full = packed[:-8].reshape(4, D)
    total_square = jnp.sum(packed[-8:]) + jnp.sum(norm_full * norm_full)
    grad_norm = jnp.sqrt(total_square)
    factor = jnp.minimum(1.0, CLIP_NORM / grad_norm)
    norm_here = lax.dynamic_slice_in_dim(norm_full, core * half, half, 1)
    weights = (w_qkv, w_out, w_in, w_back, norm_params)
    firsts = (mom_qkv, mom_out, mom_in, mom_back, mom_norm)
    seconds = (sec_qkv, sec_out, sec_in, sec_back, sec_norm)
    results = []
    for slot, gradient in enumerate(sums + (norm_here,)):
        results.append(
            adam_step(
                weights[slot],
                gradient * factor,
                firsts[slot],
                seconds[slot],
                LEARN_RATE if slot < 4 else NORM_RATE,
                WEIGHT_DECAY if slot < 4 else 0.0,
            )
        )
    return (
        out_tokens,
        input_grad,
        grad_norm,
        *[r[0] for r in results],
        *[r[1] for r in results],
        *[r[2] for r in results],
    )


def solution(mesh):
    weight_specs = (P(None, "dp", "mp"), P("mp", "dp"), P("dp", "mp"), P("mp", "dp"), P(None, "mp"))
    in_specs = (
        P(None, "dp", "mp"),
        P(None, "dp", "mp"),
        P(None, "dp", None),
        P("mp"),
        P("mp"),
        P("mp"),
        P(),
    ) + weight_specs * 3
    out_specs = (P(None, "dp", "mp"), P(None, "dp", "mp"), P()) + weight_specs * 3
    count = mesh.shape["dp"]

    def body(*args):
        return shards(count, *args)

    return jax.shard_map(body, mesh=mesh, in_specs=in_specs, out_specs=out_specs, check_vma=False)
```

```python
import functools

import jax
import jax.numpy as jnp
from jax import lax
from jax.experimental import pallas as pl
from jax.experimental.pallas import tpu as pltpu
from jax.sharding import PartitionSpec as P

D = 768
HEAD_DIM = 64
SEQ = 1024
STEP = 10
TILE = 256
TILES = SEQ // TILE
PAIR = 128

LN_EPS = 1e-12
CLIP_NORM = 1.0
LEARN_RATE = 0.06
NORM_RATE = 0.3
WEIGHT_DECAY = 0.01
BETA_ONE = 0.9
BETA_TWO = 0.999
ADAM_EPS = 1e-08
ATTN_SCALE = HEAD_DIM ** (-0.5)
MASK_STEP = float(2**30)
NT = (((1,), (1,)), ((), ()))
NN = (((1,), (0,)), ((), ()))
TN = (((0,), (0,)), ((), ()))
BF = jnp.bfloat16
F32 = jnp.float32
LARGE = pl.CostEstimate(flops=33 * 10**9, bytes_accessed=1024, transcendentals=0)
SMALL = pl.CostEstimate(flops=1024, bytes_accessed=1024, transcendentals=0)


def dot(left, right, dims):
    return lax.dot_general(left, right, dims, preferred_element_type=F32)


def later(value):
    return lax.optimization_barrier((value, LINE[-1]))[0]


def hbm(shape, dtype):
    return pltpu.HBM(shape, dtype)


def in_hbm(value):
    return pltpu.with_memory_space_constraint(value, pltpu.HBM)


LINE = []


def wait_for(value):
    LINE.append(in_hbm(value))


def ordered_call(kernel, *, out_shape, grid=(), in_specs=(), out_specs=(), grid_spec=None, **rest):
    spec = dict(num_scalar_prefetch=0, grid=grid, in_specs=in_specs, out_specs=out_specs, scratch_shapes=())
    spec.update(grid_spec or {})
    single = not isinstance(out_shape, (list, tuple))
    shapes = [out_shape] if single else list(out_shape)
    outs = [spec["out_specs"]] if single else list(spec["out_specs"])
    before = list(LINE)
    first = spec["num_scalar_prefetch"] + len(spec["in_specs"])

    def body(*refs):
        after = refs[first + len(before) :]
        after[len(outs)][...] = jnp.zeros((8, 128), F32)
        kernel(*refs[:first], *after[: len(outs)], *after[len(outs) + 1 :])

    call = pl.pallas_call(
        body,
        grid_spec=pltpu.PrefetchScalarGridSpec(
            num_scalar_prefetch=spec["num_scalar_prefetch"],
            grid=spec["grid"],
            in_specs=list(spec["in_specs"]) + [pl.BlockSpec(memory_space=pl.ANY)] * len(before),
            out_specs=outs + [whole((8, 128))],
            scratch_shapes=spec["scratch_shapes"],
        ),
        out_shape=shapes + [sds((8, 128), F32)],
        **rest,
    )

    def run(*args):
        results = call(*args, *before)
        LINE[:] = [results[-1]]
        return results[0] if single else list(results[:-1])

    return run


def params_of(mebibytes):
    return pltpu.CompilerParams(vmem_limit_bytes=mebibytes << 20)


def whole(shape):
    return pl.BlockSpec(shape, lambda *_: (0,) * len(shape))


def row_tile(tile, cols):
    return pl.BlockSpec((tile, cols), lambda r, *_: (r, 0))


def sds(shape, dtype):
    return jax.ShapeDtypeStruct(shape, dtype)


def row_sum(value):
    return jnp.sum(value, axis=1, keepdims=True)


def segment_tables(segment):
    first = segment[::TILE]
    last = segment[TILE - 1 :: TILE]
    low = jnp.sum((last[None, :] < first[:, None]).astype(jnp.int32), axis=1)
    high = jnp.sum((first[None, :] <= last[:, None]).astype(jnp.int32), axis=1)
    lane = lax.broadcasted_iota(jnp.int32, (SEQ, PAIR), 1) % HEAD_DIM
    same = lane == segment[:, None]
    key_lanes = jnp.where(same, 1.0, 0.0).astype(BF)
    query_lanes = jnp.where((lane < 4) & (~same), -MASK_STEP, 0.0).astype(BF)
    return low, high, key_lanes, query_lanes


def attend_fwd_kernel(
    low_ref, high_ref, x_ref, w_ref, klane_ref, qlane_ref, qkv_ref, ctx_ref, lse_ref, kh_ref, qh_ref, ls_ref
):
    qkv_ref[...] = dot(x_ref[...], w_ref[...], NN).astype(BF)
    lane = lax.broadcasted_iota(jnp.int32, (SEQ, PAIR), 1)
    query = qkv_ref[:, 0:PAIR] * ATTN_SCALE
    keys = qkv_ref[:, PAIR : 2 * PAIR]
    for h in range(2):
        mine = (lane // HEAD_DIM) == h
        kh_ref[h] = jnp.where(mine, keys, klane_ref[...])
        qh_ref[h] = jnp.where(mine, query, qlane_ref[...])
    is_first = lax.broadcasted_iota(jnp.int32, (TILE, PAIR), 1) < HEAD_DIM

    def row_block(qb, carry):
        low = low_ref[qb]
        count = high_ref[qb] - low
        rows = pl.ds(pl.multiple_of(qb * TILE, TILE), TILE)
        for width in range(1, TILES + 1):

            @pl.when(count == width)
            def _():
                span = pl.ds(pl.multiple_of(low * TILE, TILE), width * TILE)
                scores = [dot(qh_ref[h, rows, :], kh_ref[h, span, :], NT) for h in range(2)]
                tops = [jnp.max(s, axis=1, keepdims=True) for s in scores]
                expo = [jnp.exp(s - m) for s, m in zip(scores, tops)]
                sums = [jnp.sum(p, axis=1, keepdims=True) for p in expo]
                outs = [dot(p.astype(BF), qkv_ref[span, 2 * PAIR : 3 * PAIR], NN) for p in expo]
                ctx_ref[rows, :] = jnp.where(is_first, outs[0] / sums[0], outs[1] / sums[1]).astype(BF)
                ls_ref[rows, :] = jnp.where(
                    is_first, tops[0] + jnp.log(sums[0]), tops[1] + jnp.log(sums[1])
                )

        return carry

    lax.fori_loop(0, TILES, row_block, 0)
    turned = ls_ref[...].T
    lse_ref[0, 0:1, :] = turned[0:1]
    lse_ref[0, 1:2, :] = turned[HEAD_DIM : HEAD_DIM + 1]


def attend_forward(x, weight, tables):
    pairs = weight.shape[1] // (3 * PAIR)
    low, high, key_lanes, query_lanes = tables
    table = pl.BlockSpec((SEQ, PAIR), lambda p, *_: (0, 0))
    return ordered_call(
        attend_fwd_kernel,
        grid_spec=dict(
            num_scalar_prefetch=2,
            grid=(pairs,),
            in_specs=[
                pl.BlockSpec((SEQ, D), lambda p, *_: (0, 0)),
                pl.BlockSpec((D, 3 * PAIR), lambda p, *_: (0, p)),
                table,
                table,
            ],
            out_specs=[
                pl.BlockSpec((SEQ, 3 * PAIR), lambda p, *_: (0, p)),
                pl.BlockSpec((SEQ, PAIR), lambda p, *_: (0, p)),
                pl.BlockSpec((1, 2, SEQ), lambda p, *_: (p, 0, 0)),
            ],
            scratch_shapes=[
                pltpu.VMEM((2, SEQ, PAIR), BF),
                pltpu.VMEM((2, SEQ, PAIR), BF),
                pltpu.VMEM((SEQ, PAIR), F32),
            ],
        ),
        out_shape=[
            hbm((SEQ, pairs * 3 * PAIR), BF),
            sds((SEQ, pairs * PAIR), BF),
            sds((pairs, 2, SEQ), F32),
        ],
        compiler_params=params_of(24),
        cost_estimate=LARGE,
        name="attend_fwd",
    )(low, high, x, weight, key_lanes, query_lanes)


def attend_bwd_kernel(
    low_ref, high_ref, qkv_ref, dctx_ref, ctx_ref, lse_ref, klane_ref, qlane_ref, xt_ref, dqkv_ref, gq_ref,
    kh_ref, qh_ref, kt_ref, q0_ref, d0_ref, delta_ref, dqt_ref,
):
    lane = lax.broadcasted_iota(jnp.int32, (SEQ, PAIR), 1)
    query = qkv_ref[:, 0:PAIR] * ATTN_SCALE
    keys = qkv_ref[:, PAIR : 2 * PAIR]
    dctx = dctx_ref[...]
    kt_ref[...] = keys.T
    prod = (dctx.astype(F32) * ctx_ref[...].astype(F32)).T
    zero = jnp.zeros((SEQ, PAIR), BF)
    for h in range(2):
        mine = (lane // HEAD_DIM) == h
        kh_ref[h] = jnp.where(mine, keys, klane_ref[...])
        qh_ref[h] = jnp.where(mine, query, qlane_ref[...])
        q0_ref[h] = jnp.where(mine, query, zero)
        d0_ref[h] = jnp.where(mine, dctx, zero)
        delta_ref[h : h + 1, :] = jnp.sum(
            prod[h * HEAD_DIM : (h + 1) * HEAD_DIM], axis=0, keepdims=True
        )
    dqt_ref[...] = jnp.zeros((PAIR, SEQ), F32)

    def key_block(kb, carry):
        low = low_ref[kb]
        count = high_ref[kb] - low
        cols = pl.ds(pl.multiple_of(kb * TILE, TILE), TILE)
        for width in range(1, TILES + 1):

            @pl.when(count == width)
            def _():
                span = pl.ds(pl.multiple_of(low * TILE, TILE), width * TILE)
                values = qkv_ref[cols, 2 * PAIR : 3 * PAIR]
                scores = [dot(kh_ref[h, cols, :], qh_ref[h, span, :], NT) for h in range(2)]
                dprob = [dot(values, d0_ref[h, span, :], NT) for h in range(2)]
                prob = [jnp.exp(scores[h] - lse_ref[0, h : h + 1, span]) for h in range(2)]
                low_p = [p.astype(BF) for p in prob]
                dscore = [
                    (prob[h] * (dprob[h] - delta_ref[h : h + 1, span])).astype(BF) for h in range(2)
                ]
                dvals = dot(low_p[0], d0_ref[0, span, :], NN) + dot(low_p[1], d0_ref[1, span, :], NN)
                dkeys = dot(dscore[0], q0_ref[0, span, :], NN) + dot(dscore[1], q0_ref[1, span, :], NN)
                for h in range(2):
                    part = slice(h * HEAD_DIM, (h + 1) * HEAD_DIM)
                    dqt_ref[part, span] += dot(kt_ref[part, cols], dscore[h], NN)
                dqkv_ref[cols, PAIR : 2 * PAIR] = dkeys.astype(BF)
                dqkv_ref[cols, 2 * PAIR : 3 * PAIR] = dvals.astype(BF)

        return carry

    lax.fori_loop(0, TILES, key_block, 0)
    dqkv_ref[:, 0:PAIR] = (dqt_ref[...].T * ATTN_SCALE).astype(BF)
    gq_ref[...] = dot(xt_ref[...], dqkv_ref[...], NN).astype(BF)


def attend_backward(qkv, dctx, ctx, lse, tables, xt, start, pairs):
    low, high, key_lanes, query_lanes = tables
    table = pl.BlockSpec((SEQ, PAIR), lambda p, *_: (0, 0))
    column = pl.BlockSpec((SEQ, PAIR), lambda p, *_: (0, p + start))
    triple = pl.BlockSpec((SEQ, 3 * PAIR), lambda p, *_: (0, p))
    return ordered_call(
        attend_bwd_kernel,
        grid_spec=dict(
            num_scalar_prefetch=2,
            grid=(pairs,),
            in_specs=[
                pl.BlockSpec((SEQ, 3 * PAIR), lambda p, *_: (0, p + start)),
                column,
                column,
                pl.BlockSpec((1, 2, SEQ), lambda p, *_: (p + start, 0, 0)),
                table,
                table,
                pl.BlockSpec((D, SEQ), lambda p, *_: (0, 0)),
            ],
            out_specs=[triple, pl.BlockSpec((D, 3 * PAIR), lambda p, *_: (0, p))],
            scratch_shapes=[
                pltpu.VMEM((2, SEQ, PAIR), BF),
                pltpu.VMEM((2, SEQ, PAIR), BF),
                pltpu.VMEM((PAIR, SEQ), BF),
                pltpu.VMEM((2, SEQ, PAIR), BF),
                pltpu.VMEM((2, SEQ, PAIR), BF),
                pltpu.VMEM((2, SEQ), F32),
                pltpu.VMEM((PAIR, SEQ), F32),
            ],
        ),
        out_shape=[hbm((SEQ, pairs * 3 * PAIR), BF), sds((D, pairs * 3 * PAIR), BF)],
        compiler_params=params_of(28),
        cost_estimate=LARGE,
        name="attend_bwd",
    )(
        low, high, in_hbm(qkv), dctx, ctx, lse, key_lanes, query_lanes, xt
    )


def mid_kernel(ctx_a, ctx_b, wo_a, wo_b, x_ref, vec_ref, cen_ref, inv_ref, low_ref, lowt_ref):
    attn = dot(ctx_a[...], wo_a[...], NT) + dot(ctx_b[...], wo_b[...], NT)
    res = x_ref[...].astype(F32) + vec_ref[0:1,:]*attn
    mean = row_sum(res)/D
    var = row_sum(res*res)/D - mean*mean
    inv = lax.rsqrt(var+LN_EPS)
    cen = (res-mean)*inv
    cen_ref[...] = cen
    inv_ref[...] = jnp.broadcast_to(inv, inv_ref.shape)
    low = (cen*vec_ref[2:3,:]+vec_ref[3:4,:]).astype(BF)
    low_ref[...] = low
    lowt_ref[...] = low.T

def mid(ctx, out, x, vec, T=256):
    half = D//2
    wo = lambda: whole((D, half))
    return ordered_call(mid_kernel, grid=(SEQ//T,),
        in_specs=[row_tile(T,half), row_tile(T,half), wo(), wo(), row_tile(T,D), whole((8,D))],
        out_specs=[row_tile(T,D), row_tile(T,128), row_tile(T,D), pl.BlockSpec((D,T), lambda r:(0,r))],
        out_shape=[sds((SEQ,D),F32), hbm((SEQ,128),F32), sds((SEQ,D),BF), sds((D,SEQ),BF)],
        compiler_params=params_of(32), cost_estimate=LARGE, name="mid")(ctx[0],ctx[1],out[0],out[1],x,vec)

def gelu_pair(value):
    phi = 0.5 + 0.5 * lax.erf(value * 0.7071067811865476)
    bell = jnp.exp(-0.5 * value * value)
    return value * phi, phi + value * bell * 0.3989422804014327

def ffn_in_kernel(x_ref, w_ref, act_ref, slope_ref):
    pre = dot(x_ref[...], w_ref[...], NN)
    act, slope = gelu_pair(pre)
    act_ref[...] = act.astype(BF)
    slope_ref[...] = slope.astype(BF)

def ffn_in(low, two, width=256):
    units = 4*(D//2)
    return ordered_call(ffn_in_kernel, grid=(units//width,),
        in_specs=[whole((SEQ,D)), pl.BlockSpec((D,width), lambda n:(0,n))],
        out_specs=[pl.BlockSpec((SEQ,width), lambda n:(0,n))]*2,
        out_shape=[hbm((SEQ,units),BF)]*2,
        compiler_params=params_of(32), cost_estimate=LARGE, name="ffn_in")(low, two)

def ffn_out_kernel(core_ref, act_a, act_b, wb_a, wb_b, cen_ref, cot_ref, vec_ref, own_ref, away_ref, gtwo_ref, gffnt_ref, gffn_ref, dn_ref):
    ffn = dot(act_a[...], wb_a[...], NT) + dot(act_b[...], wb_b[...], NT)
    normed = cen_ref[...]*vec_ref[2:3,:]+vec_ref[3:4,:]
    res = normed + vec_ref[1:2,:]*ffn
    mean = row_sum(res)/D
    var = row_sum(res*res)/D - mean*mean
    inv = lax.rsqrt(var+LN_EPS)
    cen = (res-mean)*inv
    gain = vec_ref[4:5,:]
    by_core(core_ref, (cen*gain+vec_ref[5:6,:]).astype(BF), own_ref, away_ref)
    cot = cot_ref[...].astype(F32)
    scaled = cot*gain
    m1 = row_sum(scaled)/D
    m2 = row_sum(scaled*cen)/D
    gtwo = inv*(scaled-m1-cen*m2)
    gtwo_ref[...] = gtwo
    gffn = (vec_ref[1:2,:]*gtwo).astype(BF)
    gffn_ref[...] = gffn
    gffnt_ref[...] = gffn.T
    @pl.when(pl.program_id(0)==0)
    def _(): dn_ref[...] = jnp.zeros(dn_ref.shape, F32)
    dn_ref[0:1,:] += jnp.sum(cot*cen, axis=0, keepdims=True)
    dn_ref[1:2,:] += jnp.sum(cot, axis=0, keepdims=True)

def ffn_out(core, acts, back, cen, cot, vec, T=256):
    half = D//2
    units = 4*half
    return ordered_call(ffn_out_kernel, grid_spec=dict(num_scalar_prefetch=1, grid=(SEQ//T,),
        in_specs=[row_tile(T,units), row_tile(T,units), whole((D,units)), whole((D,units)), row_tile(T,D), row_tile(T,D), whole((8,D))],
        out_specs=[row_tile(T,half), row_tile(T,half), row_tile(T,D), pl.BlockSpec((D,T), lambda r,*_:(0,r)), row_tile(T,D), whole((8,D))]),
        out_shape=[sds((SEQ,half),BF), sds((SEQ,half),BF), hbm((SEQ,D),F32), sds((D,SEQ),BF), sds((SEQ,D),BF), sds((8,D),F32)],
        compiler_params=params_of(32), cost_estimate=LARGE, name="ffn_out")(core[None],in_hbm(acts[0]),in_hbm(acts[1]),back[0],back[1],cen,cot,vec)

def grad_back_kernel(lt_ref, own_ref, away_ref, own_a, own_b, away_a, away_b):
    half_of = pl.program_id(0) // 2
    for which, own, away in ((0, own_a, away_a), (1, own_b, away_b)):

        @pl.when(half_of == which)
        def _():
            away[...] = dot(lt_ref[...], away_ref[...], NN).astype(BF)
            own[...] = dot(lt_ref[...], own_ref[...], NN).astype(BF)


def grad_back(lt, acts):
    width = D // 2
    col = pl.BlockSpec((SEQ, width), lambda n: (0, n))
    first = pl.BlockSpec((D, width), lambda n: (0, jnp.minimum(n, 1)))
    second = pl.BlockSpec((D, width), lambda n: (0, jnp.maximum(n - 2, 0)))
    return ordered_call(
        grad_back_kernel,
        grid=(4,),
        in_specs=[whole((D, SEQ)), col, col],
        out_specs=[first, second, first, second],
        out_shape=[sds((D, 2 * width), BF)] * 4,
        compiler_params=params_of(32),
        cost_estimate=LARGE,
        name="grad_back",
    )(lt, in_hbm(acts[0]), in_hbm(acts[1]))


def inner_bwd_kernel(gffn_ref, sl_a, sl_b, wb_a, wb_b, wi_a, wi_b, wo_a, wo_b, gtwo_ref, cen_ref, inv_ref, vec_ref,
                pre_a, pre_b, gone_ref, gattnt_ref, dctx_a, dctx_b, dn_ref):
    gffn = gffn_ref[...]
    pa = (dot(gffn, wb_a[...], NN)*sl_a[...].astype(F32)).astype(BF)
    pre_a[...] = pa
    pb = (dot(gffn, wb_b[...], NN)*sl_b[...].astype(F32)).astype(BF)
    pre_b[...] = pb
    gn = gtwo_ref[...] + dot(pa, wi_a[...], NT) + dot(pb, wi_b[...], NT)
    cen = cen_ref[...]
    scaled = gn*vec_ref[2:3,:]
    m1 = row_sum(scaled)/D
    m2 = row_sum(scaled*cen)/D
    inv = inv_ref[:,0:1]
    gone = inv*(scaled-m1-cen*m2)
    gone_ref[...] = gone
    gattn = (vec_ref[0:1,:]*gone).astype(BF)
    gattnt_ref[...] = gattn.T
    dctx_a[...] = dot(gattn, wo_a[...], NN).astype(BF)
    dctx_b[...] = dot(gattn, wo_b[...], NN).astype(BF)
    @pl.when(pl.program_id(0)==0)
    def _(): dn_ref[...] = jnp.zeros(dn_ref.shape, F32)
    dn_ref[0:1,:] += jnp.sum(gn*cen, axis=0, keepdims=True)
    dn_ref[1:2,:] += jnp.sum(gn, axis=0, keepdims=True)

def inner_bwd(gffn, slopes, back, win, out, gtwo, cen, inv, vec, T=256):
    half=D//2; units=4*half
    wi = lambda: whole((D,units))
    wo = lambda: whole((D,half))
    return ordered_call(inner_bwd_kernel, grid=(SEQ//T,),
        in_specs=[row_tile(T,D), row_tile(T,units), row_tile(T,units), whole((D,units)), whole((D,units)), wi(), wi(), wo(), wo(), row_tile(T,D), row_tile(T,D), row_tile(T,128), whole((8,D))],
        out_specs=[row_tile(T,units), row_tile(T,units), row_tile(T,D), pl.BlockSpec((D,T), lambda r:(0,r)), row_tile(T,half), row_tile(T,half), whole((8,D))],
        out_shape=[hbm((SEQ,units),BF)]*2+[hbm((SEQ,D),F32), sds((D,SEQ),BF), sds((SEQ,half),BF), sds((SEQ,half),BF), sds((8,D),F32)],
        compiler_params=params_of(44), cost_estimate=LARGE, name="inner_bwd")(gffn,in_hbm(slopes[0]),in_hbm(slopes[1]),back[0],back[1],win[0],win[1],out[0],out[1],in_hbm(gtwo),cen,in_hbm(inv),vec)

def grad_weights_two_kernel(
    lowt_ref, gattnt_ref, pre_own, pre_away, ctx_own, ctx_away, own_a, own_b, away_a, away_b
):
    n = pl.program_id(0)

    @pl.when(n < 3)
    def _():
        away_a[...] = dot(lowt_ref[...], pre_away[...], NN).astype(BF)
        own_a[...] = dot(lowt_ref[...], pre_own[...], NN).astype(BF)

    @pl.when(n == 3)
    def _():
        away_b[...] = dot(lowt_ref[...], pre_away[...], NN).astype(BF)
        own_b[...] = dot(lowt_ref[...], pre_own[...], NN).astype(BF)

    @pl.when(n == 4)
    def _():
        away_b[...] = dot(gattnt_ref[...], ctx_away[...], NN).astype(BF)
        own_b[...] = dot(gattnt_ref[...], ctx_own[...], NN).astype(BF)


def grad_weights_two(lowt, gattnt, pre, ctx):
    half = D // 2
    col = pl.BlockSpec((SEQ, half), lambda n: (0, jnp.minimum(n, 3)))
    first = pl.BlockSpec((D, half), lambda n: (0, jnp.minimum(n, 2)))
    second = pl.BlockSpec((D, half), lambda n: (0, jnp.maximum(n - 3, 0)))
    return ordered_call(
        grad_weights_two_kernel,
        grid=(5,),
        in_specs=[whole((D, SEQ)), whole((D, SEQ)), col, col, whole((SEQ, half)), whole((SEQ, half))],
        out_specs=[first, second, first, second],
        out_shape=[sds((D, 3 * half), BF), sds((D, 2 * half), BF)] * 2,
        compiler_params=params_of(32),
        cost_estimate=LARGE,
        name="grad_weights_two",
    )(lowt, gattnt, in_hbm(pre[0]), in_hbm(pre[1]), ctx[0], ctx[1])


def grad_tokens_kernel(core_ref, gone_ref, d_a, d_b, d_c, d_d, w_a, w_b, own_ref, away_ref):
    cut = d_a.shape[1]
    total = gone_ref[...] + dot(d_a[...], w_a[:, :cut], NT) + dot(d_b[...], w_a[:, cut:], NT)
    total = total + dot(d_c[...], w_b[:, :cut], NT) + dot(d_d[...], w_b[:, cut:], NT)
    by_core(core_ref, total.astype(BF), own_ref, away_ref)


def grad_tokens(core, gone, dqkv, wq, T=256):
    half = D//2
    return ordered_call(grad_tokens_kernel, grid_spec=dict(num_scalar_prefetch=1, grid=(SEQ//T,),
        in_specs=[row_tile(T,D), *[row_tile(T,d.shape[1]) for d in dqkv], whole(wq[0].shape), whole(wq[1].shape)],
        out_specs=[row_tile(T,half)]*2), out_shape=[sds((SEQ,half),BF)]*2,
        compiler_params=params_of(32), cost_estimate=LARGE, name="grad_tokens")(core[None],in_hbm(gone),*[in_hbm(d) for d in dqkv],wq[0],wq[1])


def side_by_side_kernel(core_ref, own_ref, away_ref, out_ref, *turned_ref):
    half = away_ref.shape[1]
    first = jnp.where(core_ref[0] == 0, own_ref[0], away_ref[...])
    second = jnp.where(core_ref[0] == 0, away_ref[...], own_ref[0])
    out_ref[:, :half] = first
    out_ref[:, half:] = second
    if turned_ref:
        turned_ref[0][:half, :] = first.T
        turned_ref[0][half:, :] = second.T


def side_by_side(both, away, core, turned):
    half = away.shape[1]
    tile = 512
    outs = 2 if turned else 1
    return ordered_call(
        side_by_side_kernel,
        grid_spec=dict(
            num_scalar_prefetch=1,
            grid=(SEQ // tile,),
            in_specs=[
                pl.BlockSpec((1, tile, half), lambda r, c: (c[0], r, 0)),
                pl.BlockSpec((tile, half), lambda r, c: (r, 0)),
            ],
            out_specs=[
                pl.BlockSpec((tile, 2 * half), lambda r, c: (r, 0)),
                pl.BlockSpec((2 * half, tile), lambda r, c: (0, r)),
            ][:outs],
        ),
        out_shape=[sds((SEQ, 2 * half), BF), sds((2 * half, SEQ), BF)][:outs],
        compiler_params=params_of(8),
        cost_estimate=SMALL,
        name="side_by_side",
    )(core[None], both, away)


def by_core(core_ref, value, own_ref, away_ref):
    half = own_ref.shape[1]
    first, second = value[:, :half], value[:, half:]
    own_ref[...] = jnp.where(core_ref[0] == 0, first, second)
    away_ref[...] = jnp.where(core_ref[0] == 0, second, first)


def digits_of(count):
    found, shift = [], 0
    while (1 << shift) < count:
        radix = min(4, count >> shift)
        found.append((shift, radix))
        shift += 2 if radix == 4 else 1
    return found


def swap(value, count, mask, axis="dp"):
    return lax.ppermute(value, axis, [(i, i ^ mask) for i in range(count)])


def place_kernel(places_ref, *refs, radix, widths):
    pieces, outs = refs[:radix], refs[radix:]
    for j, piece in enumerate(pieces):

        @pl.when(pl.program_id(0) == j)
        def _():
            start = 0
            for out, width in zip(outs, widths):
                out[:, 0] = piece[:, :, start : start + width]
                start += width


def place(pieces, places, widths=None):
    outer, rows, cols = pieces[0].shape
    radix = len(pieces)
    widths = widths or (cols,)
    placed = ordered_call(
        functools.partial(place_kernel, radix=radix, widths=widths),
        grid_spec=dict(
            num_scalar_prefetch=1,
            grid=(radix,),
            in_specs=[pl.BlockSpec((outer, rows, cols), lambda g, d: (0, 0, 0))] * radix,
            out_specs=[
                pl.BlockSpec((outer, 1, rows, width), lambda g, d: (0, d[g], 0, 0)) for width in widths
            ],
        ),
        out_shape=[sds((outer, radix, rows, width), BF) for width in widths],
        compiler_params=params_of(16),
        cost_estimate=SMALL,
        name="place",
    )(places, *pieces)
    placed = [p.reshape(outer * radix, rows, p.shape[-1]) for p in placed]
    return placed if len(widths) > 1 else placed[0]


def place_two_kernel(digit_ref, a_own, a_got, b_own, b_got, *outs):
    y = pl.program_id(0) // 2
    x = pl.program_id(0) % 2
    width = a_own.shape[-1]
    first = outs[0].shape[-1]
    for source, hit in ((a_own, x == digit_ref[1]), (a_got, x != digit_ref[1])):

        @pl.when(hit)
        def _():
            outs[0][:, 0, 0, :, :width] = source[:, 0]

    for source, hit in ((b_own, y == digit_ref[0]), (b_got, y != digit_ref[0])):

        @pl.when(hit)
        def _():
            outs[0][:, 0, 0, :, width:] = source[:, 0, :, : first - width]
            outs[1][:, 0, 0] = source[:, 0, :, first - width :]


def place_two(a_pieces, b_pieces, digit_y, digit_x, widths):
    outer, rows, a_width = a_pieces[0].shape
    b_width = b_pieces[0].shape[-1]
    outer //= 2
    a_spec = pl.BlockSpec((outer, 1, rows, a_width), lambda g, d: (0, g // 2, 0, 0))
    b_spec = pl.BlockSpec((outer, 1, rows, b_width), lambda g, d: (0, g % 2, 0, 0))
    shaped = [p.reshape(outer, 2, rows, -1) for p in (*a_pieces, *b_pieces)]
    placed = ordered_call(
        place_two_kernel,
        grid_spec=dict(
            num_scalar_prefetch=1,
            grid=(4,),
            in_specs=[a_spec, a_spec, b_spec, b_spec],
            out_specs=[
                pl.BlockSpec((outer, 1, 1, rows, width), lambda g, d: (0, g // 2, g % 2, 0, 0))
                for width in widths
            ],
        ),
        out_shape=[sds((outer, 2, 2, rows, width), BF) for width in widths],
        compiler_params=params_of(32),
        cost_estimate=SMALL,
        name="place_two",
    )(jnp.stack([digit_y, digit_x]), *shaped)
    return [p.reshape(outer * 4 * rows, -1) for p in placed]


def sum_split_kernel(digit_ref, *refs, counts):
    outs = refs[sum(counts) :]
    start = at = 0
    for count in counts:
        terms = refs[at : at + count]
        at += count
        total = terms[0][:, 0].astype(F32)
        for ref in terms[1:]:
            total = total + ref[:, 0].astype(F32)
        total = total.astype(BF)
        stop = start + total.shape[-1]
        for j, out in enumerate(outs):

            @pl.when(pl.program_id(0) == j)
            def _():
                out[:, :, start:stop] = total

        start = stop


def sum_split(runs, digit):
    outer, radix, rows, _ = runs[0][0].shape
    terms = [term for run in runs for term in run]
    cols = sum(run[0].shape[-1] for run in runs)
    return ordered_call(
        functools.partial(sum_split_kernel, counts=[len(run) for run in runs]),
        grid_spec=dict(
            num_scalar_prefetch=1,
            grid=(radix,),
            in_specs=[
                pl.BlockSpec((outer, 1, rows, term.shape[-1]), lambda g, d: (0, d[0] ^ g, 0, 0))
                for term in terms
            ],
            out_specs=[pl.BlockSpec((outer, rows, cols), lambda g, d: (0, 0, 0))] * radix,
        ),
        out_shape=[sds((outer, rows, cols), BF)] * radix,
        compiler_params=params_of(32),
        cost_estimate=SMALL,
        name="sum_split",
    )(digit[None], *terms)


def gather_start(held, count, place_in):
    shift, radix = place_in
    return [held] + [swap(held, count, j << shift) for j in range(1, radix)]


def gather_place(pieces, index, place_in, widths=None):
    shift, radix = place_in
    return place(pieces, ((index >> shift) & (radix - 1)) ^ jnp.arange(radix, dtype=jnp.int32), widths)


def ring(value, count, place_in):
    shift, radix = place_in
    step = 1 << shift
    around = [(i, i + step if (i >> shift) % radix < radix - 1 else i - (radix - 1) * step) for i in range(count)]
    return lax.ppermute(value, "dp", around)


def scatter_split(runs, index, place_in, rows):
    shift, radix = place_in
    shaped = [[t.reshape(-1, radix, rows, t.shape[-1]) for t in run] for run in runs]
    return sum_split(shaped, (index >> shift) & (radix - 1))


def scatter_send(parts, count, place_in):
    return [parts[0]] + [swap(parts[j], count, j << place_in[0]) for j in range(1, place_in[1])]


def sum_all(value, count):
    value = value + swap(value, 2, 1, "mp")
    for shift, radix in digits_of(count):
        parts = [value] + [swap(value, count, j << shift) for j in range(1, radix)]
        value = parts[0] + parts[1]
        if radix == 4:
            value = value + (parts[2] + parts[3])
    return value


def finish_kernel(*refs):
    terms, mask_ref, total_ref, square_ref = refs[:-3], refs[-3], refs[-2], refs[-1]
    total = terms[0][0].astype(F32)
    for term in terms[1:]:
        total = total + term[0].astype(F32)
    total = total * mask_ref[...]
    total_ref[...] = total
    square_ref[...] = jnp.full((8, 128), jnp.sum(total * total), F32)


def finish(terms, mask):
    shape = terms[0].shape
    return ordered_call(
        finish_kernel,
        in_specs=[whole(shape)] * len(terms) + [whole((1, shape[2]))],
        out_specs=[whole(shape[1:]), whole((8, 128))],
        out_shape=[sds(shape[1:], F32), sds((8, 128), F32)],
        compiler_params=params_of(8),
        cost_estimate=SMALL,
        name="finish",
    )(*terms, mask)


def adam_step(weight, gradient, first_mom, second, step_rate, decay_rate):
    first_new = BETA_ONE * first_mom + (1.0 - BETA_ONE) * gradient
    second_new = BETA_TWO * second + (1.0 - BETA_TWO) * gradient * gradient
    update = (
        first_new
        / (1.0 - BETA_ONE**STEP)
        / (jnp.sqrt(second_new / (1.0 - BETA_TWO**STEP)) + ADAM_EPS)
    )
    return (weight - step_rate * (update + decay_rate * weight), first_new, second_new)


def adam_kernel(factor_ref, g_one, g_two, g_back, g_norm, *refs):
    weights, firsts, seconds, outs = refs[:5], refs[5:10], refs[10:15], refs[15:]
    factor = factor_ref[0:1, 0:1]
    half = weights[0].shape[2]

    def step(slot, gradient, at, rate, decay):
        new = adam_step(
            weights[slot][at], gradient * factor, firsts[slot][at], seconds[slot][at], rate, decay
        )
        for kind in range(3):
            outs[5 * kind + slot][at] = new[kind]

    for t in range(3):
        for pair in range(half // PAIR):
            start = (3 * pair + t) * PAIR
            at = (t, slice(None), slice(pair * PAIR, (pair + 1) * PAIR))
            step(0, g_one[:, start : start + PAIR], at, LEARN_RATE, WEIGHT_DECAY)
    everything = (slice(None), slice(None))
    step(1, g_two[:, 4 * half :], everything, LEARN_RATE, WEIGHT_DECAY)
    step(2, g_two[:, : 4 * half], everything, LEARN_RATE, WEIGHT_DECAY)
    step(3, g_back[...], everything, LEARN_RATE, WEIGHT_DECAY)
    step(4, g_norm[...], everything, NORM_RATE, 0.0)


def adam(factor, gradients, weights, firsts, seconds):
    states = (*weights, *firsts, *seconds)
    return ordered_call(
        adam_kernel,
        in_specs=[whole(v.shape) for v in (factor, *gradients, *states)],
        out_specs=[whole(v.shape) for v in states],
        out_shape=[sds(v.shape, F32) for v in states],
        compiler_params=params_of(24),
        cost_estimate=SMALL,
        name="adam",
    )(factor, *gradients, *[in_hbm(v) for v in states])


def shards(
    count,
    tokens,
    cotangent,
    segments,
    head_gates,
    unit_gates,
    hidden_gates,
    layer_gates,
    w_qkv,
    w_out,
    w_in,
    w_back,
    norm_params,
    mom_qkv,
    mom_out,
    mom_in,
    mom_back,
    mom_norm,
    sec_qkv,
    sec_out,
    sec_in,
    sec_back,
    sec_norm,
):
    LINE.clear()
    index = lax.axis_index("dp")
    core = lax.axis_index("mp")
    rows = D // count
    half = D // 2
    pairs = half // PAIR
    head_mask = jnp.repeat(head_gates.astype(F32), HEAD_DIM)
    unit_mask = unit_gates.astype(F32)
    gate_attn = layer_gates[0]
    gate_ffn = layer_gates[1]

    shard_qkv = (
        w_qkv.astype(BF).reshape(3, rows, pairs, PAIR).transpose(1, 2, 0, 3).reshape(rows, 3 * half)
    )
    shard_out = (w_out.T * head_mask[None, :]).astype(BF)
    shard_two = jnp.concatenate([w_in.astype(BF), shard_out], axis=1)
    shard_back = (w_back.T * unit_mask[None, :]).astype(BF)
    digits = digits_of(count)

    def other_core(value):
        return swap(value, 2, 1, "mp")

    def both(own, away):
        return jnp.where(
            core == 0, jnp.concatenate([own, away], axis=-1), jnp.concatenate([away, own], axis=-1)
        )

    plane = digits[0]
    upper = [(bit, 2) for bit in range(plane[1] // 2, count.bit_length() - 1)]
    bit_y, bit_x = (index >> 1) & 1, index & 1

    def direct_start(held):
        for place_in in digits[:1:-1]:
            held = gather_place(gather_start(held, count, place_in), index, place_in)
        return gather_start(held, count, digits[1])

    def halves_start(pieces, widths):
        a, b = gather_place(pieces, index, upper[0], widths)
        return [a, swap(a, count, 2)], [b, swap(b, count, 1)]

    def halves_turn(halves):
        a = gather_place(halves[0], index, (1, 2))
        b = gather_place(halves[1], index, (0, 2))
        return [a, swap(a, count, 1)], [b, swap(b, count, 2)]

    def halves_place(halves):
        return place_two(*halves, bit_y, bit_x, (4 * half, half))

    def grow(pieces, place_in):
        return gather_place(pieces, index, place_in).reshape(1, -1, pieces[0].shape[-1])

    tok_away = other_core(lax.dynamic_index_in_dim(tokens, 1 - core, 0, keepdims=False))
    one = direct_start(shard_qkv[None])
    back = gather_start(shard_back[None], count, (0, 2))
    segment = lax.dynamic_index_in_dim(segments, core, 0, keepdims=False)[0]
    tables = segment_tables(segment)
    vectors = jnp.concatenate([hidden_gates.astype(F32)[None], norm_params], axis=0)
    vectors = both(vectors, other_core(vectors))
    hidden_mask, params = vectors[0], vectors[1:]
    vec = jnp.concatenate(
        [gate_attn * hidden_mask[None], gate_ffn * hidden_mask[None], params, params[:2]], axis=0
    )
    back = gather_start(grow(back, (0, 2)), count, (1, 2))
    wait_for(vec)
    x, xt = side_by_side(tokens, tok_away, core, True)
    wait_for(back[1])
    one = gather_start(gather_place(one, index, digits[1]), count, plane)
    two = gather_start(later(shard_two)[None], count, upper[-1])
    z_digit = digits[1]
    two = gather_place(two, index, upper[-1])
    for place_in in upper[-2:0:-1]:
        two = gather_place(gather_start(two, count, place_in), index, place_in)
    two = halves_start(gather_start(two, count, upper[0]), (1024, 5 * half - 1024))
    mine_qkv = gather_place(one, index, plane).reshape(D, -1)
    away_qkv = other_core(mine_qkv)
    back = grow(back, (1, 2))
    back = [back, ring(back, count, z_digit)]
    qkv_own, ctx_own, lse_own = attend_forward(x, mine_qkv, tables)
    core_later = later(core)
    cot_away = other_core(lax.dynamic_index_in_dim(cotangent, 1 - core_later, 0, keepdims=False))
    wait_for(back[-1])
    two = halves_turn(two)
    while len(back) < z_digit[1] - 1:
        back.append(ring(back[-1], count, z_digit))
    qkv_away, ctx_away, lse_away = attend_forward(x, away_qkv, tables)
    wait_for(back[-1])
    (grad_out,) = side_by_side(cotangent, cot_away, core, False)
    mine_in, mine_out = halves_place(two)
    away_out = other_core(mine_out)
    away_in = other_core(mine_in)
    if len(back) < z_digit[1]:
        back.append(ring(back[-1], count, z_digit))
    ctx = (ctx_own, ctx_away)
    lse = (lse_own, lse_away)
    qkv = (qkv_own, qkv_away)
    qkv_sides = (mine_qkv, away_qkv)
    in_sides = (mine_in, away_in)
    out_sides = (mine_out, away_out)
    centred_one, inv_one, normed_low, normed_turned = mid(ctx, out_sides, x, vec)
    act_own, slope_own = ffn_in(normed_low, mine_in)
    z_here = (index >> z_digit[0]) & (z_digit[1] - 1)
    z_from = (z_here - jnp.arange(z_digit[1], dtype=jnp.int32)) & (z_digit[1] - 1)
    back = place(back, z_from).reshape(1, -1, back[0].shape[-1])
    for place_in in digits[2:]:
        back = grow(gather_start(back, count, place_in), place_in)
    mine_back = back.reshape(D, -1)
    away_back = other_core(mine_back)
    act_away, slope_away = ffn_in(normed_low, away_in)
    acts, slopes = (act_own, act_away), (slope_own, slope_away)
    back_sides = (mine_back, away_back)
    result_own, result_away, grad_two, grad_ffn_turned, grad_ffn, dnorm_two = ffn_out(
        core, acts, back_sides, centred_one, grad_out, vec
    )
    cores_here = jnp.stack([core, 1 - core])

    def send_back(own, away):
        return place([own[None], other_core(away)[None]], cores_here)

    bit = [(0, 2), (1, 2)]

    def over_cores(own, away):
        return [own, other_core(away)]

    def split_a(terms, step):
        return scatter_send(scatter_split([terms], index, bit[step], rows), count, bit[step])

    def split_b(terms, step):
        place_in = bit[1 - step]
        return scatter_send(scatter_split([terms], index, place_in, rows * (2 - step)), count, place_in)

    def split_z(runs, level):
        place_in = upper[level]
        return [scatter_send(scatter_split(runs, index, place_in, rows), count, place_in)]

    back_own_a, back_own_b, back_away_a, back_away_b = grad_back(grad_ffn_turned, acts)
    back_a, back_b = over_cores(back_own_a, back_away_a), over_cores(back_own_b, back_away_b)
    pre_own, pre_away, grad_one, grad_attn_turned, dctx_own, dctx_away, dnorm_one = inner_bwd(
        grad_ffn, slopes, back_sides, in_sides, out_sides, grad_two, centred_one, inv_one, vec
    )
    back_a, back_b = split_a(back_a, 0), split_b(back_b, 0)
    out_tokens = send_back(result_own, result_away)
    two_own_a, two_own_b, two_away_a, two_away_b = grad_weights_two(
        normed_turned, grad_attn_turned, (pre_own, pre_away), ctx
    )
    back_a, back_b = split_a(back_a, 1), split_b(back_b, 1)
    two_a, two_b = over_cores(two_own_a, two_away_a), over_cores(two_own_b, two_away_b)

    def attend_back(side, start, many):
        dctx = (dctx_own, dctx_away)[side]
        return attend_backward(qkv[side], dctx, ctx[side], lse[side], tables, xt, start, many)

    away_dqkv_a, away_gq_a = attend_back(1, 0, 1)
    back = split_z([back_a, back_b], 0)
    two_a, two_b = split_a(two_a, 0), split_b(two_b, 0)
    away_dqkv_b, away_gq_b = attend_back(1, 1, pairs - 1)
    for level in range(1, len(upper)):
        back = split_z(back, level)
    two_a, two_b = split_a(two_a, 1), split_b(two_b, 1)
    own_dqkv_b, own_gq_b = attend_back(0, 1, pairs - 1)
    sum_back, square_back = finish(back[0], unit_mask[None])
    two = [two_a, two_b]
    for place_in in digits[1:]:
        two = [scatter_send(scatter_split(two, index, place_in, rows), count, place_in)]
    one_b = split_b(over_cores(own_gq_b, away_gq_b), 0)
    own_dqkv_a, own_gq_a = attend_back(0, 0, 1)
    one_a = scatter_split([over_cores(own_gq_a, away_gq_a)], index, plane, rows)
    one_a = scatter_send(one_a, count, plane)
    one_b = split_b(one_b, 1)
    mask_two = jnp.concatenate([jnp.ones((4 * half,), F32), head_mask])
    sum_two, square_two = finish(two[0], mask_two[None])
    token_own, token_away = grad_tokens(
        core, grad_one, (own_dqkv_a, own_dqkv_b, away_dqkv_a, away_dqkv_b), qkv_sides
    )
    one = [one_a, one_b]
    for place_in in digits[1:]:
        one = [scatter_send(scatter_split(one, index, place_in, rows), count, place_in)]
    sum_one, square_one = finish(one[0], jnp.ones((1, 3 * half), F32))
    input_grad = send_back(token_own, token_away)

    square = (square_back + square_two + square_one) / 1024.0
    norm_rows = jnp.concatenate([dnorm_one[:2], dnorm_two[:2]]).reshape(-1, 128)
    packed = jnp.concatenate([norm_rows, square], axis=0)
    packed = sum_all(packed, count)
    norm_full = packed[:-8].reshape(4, D)
    total_square = jnp.sum(packed[-8:]) + jnp.sum(norm_full * norm_full)
    grad_norm = jnp.sqrt(total_square)
    factor = jnp.minimum(1.0, CLIP_NORM / grad_norm)
    norm_here = lax.dynamic_slice_in_dim(norm_full, core * half, half, 1)
    def turn(values):
        return [v.T if slot in (1, 3) else v for slot, v in enumerate(values)]

    states = adam(
        jnp.full((8, 128), factor, F32),
        (sum_one, sum_two, sum_back, norm_here),
        turn((w_qkv, w_out, w_in, w_back, norm_params)),
        turn((mom_qkv, mom_out, mom_in, mom_back, mom_norm)),
        turn((sec_qkv, sec_out, sec_in, sec_back, sec_norm)),
    )
    return (
        out_tokens,
        input_grad,
        grad_norm,
        *turn(states[:5]),
        *turn(states[5:10]),
        *turn(states[10:]),
    )


def solution(mesh):
    weight_specs = (P(None, "dp", "mp"), P("mp", "dp"), P("dp", "mp"), P("mp", "dp"), P(None, "mp"))
    in_specs = (
        P(None, "dp", "mp"),
        P(None, "dp", "mp"),
        P(None, "dp", None),
        P("mp"),
        P("mp"),
        P("mp"),
        P(),
    ) + weight_specs * 3
    out_specs = (P(None, "dp", "mp"), P(None, "dp", "mp"), P()) + weight_specs * 3
    count = mesh.shape["dp"]

    def body(*args):
        return shards(count, *args)

    return jax.shard_map(body, mesh=mesh, in_specs=in_specs, out_specs=out_specs, check_vma=False)
```

```python
import functools

import jax
import jax.numpy as jnp
from jax import lax
from jax.experimental import pallas as pl
from jax.experimental.pallas import tpu as pltpu
from jax.sharding import PartitionSpec as P

D = 768
HEAD_DIM = 64
SEQ = 1024
STEP = 10
TILE = 256
TILES = SEQ // TILE
PAIR = 128

LN_EPS = 1e-12
CLIP_NORM = 1.0
LEARN_RATE = 0.06
NORM_RATE = 0.3
WEIGHT_DECAY = 0.01
BETA_ONE = 0.9
BETA_TWO = 0.999
ADAM_EPS = 1e-08
ATTN_SCALE = HEAD_DIM ** (-0.5)
MASK_STEP = float(2**30)
NT = (((1,), (1,)), ((), ()))
NN = (((1,), (0,)), ((), ()))
TN = (((0,), (0,)), ((), ()))
BF = jnp.bfloat16
F32 = jnp.float32
LARGE = pl.CostEstimate(flops=33 * 10**9, bytes_accessed=1024, transcendentals=0)
SMALL = pl.CostEstimate(flops=1024, bytes_accessed=1024, transcendentals=0)


def dot(left, right, dims):
    return lax.dot_general(left, right, dims, preferred_element_type=F32)


def later(value):
    return lax.optimization_barrier((value, LINE[-1]))[0]


def hbm(shape, dtype):
    return pltpu.HBM(shape, dtype)


def in_hbm(value):
    return pltpu.with_memory_space_constraint(value, pltpu.HBM)


LINE = []


def wait_for(value):
    LINE.append(in_hbm(value))


def ordered_call(kernel, *, out_shape, grid=(), in_specs=(), out_specs=(), grid_spec=None, **rest):
    spec = dict(num_scalar_prefetch=0, grid=grid, in_specs=in_specs, out_specs=out_specs, scratch_shapes=())
    spec.update(grid_spec or {})
    single = not isinstance(out_shape, (list, tuple))
    shapes = [out_shape] if single else list(out_shape)
    outs = [spec["out_specs"]] if single else list(spec["out_specs"])
    before = list(LINE)
    first = spec["num_scalar_prefetch"] + len(spec["in_specs"])

    def body(*refs):
        after = refs[first + len(before) :]
        after[len(outs)][...] = jnp.zeros((8, 128), F32)
        kernel(*refs[:first], *after[: len(outs)], *after[len(outs) + 1 :])

    call = pl.pallas_call(
        body,
        grid_spec=pltpu.PrefetchScalarGridSpec(
            num_scalar_prefetch=spec["num_scalar_prefetch"],
            grid=spec["grid"],
            in_specs=list(spec["in_specs"]) + [pl.BlockSpec(memory_space=pl.ANY)] * len(before),
            out_specs=outs + [whole((8, 128))],
            scratch_shapes=spec["scratch_shapes"],
        ),
        out_shape=shapes + [sds((8, 128), F32)],
        **rest,
    )

    def run(*args):
        results = call(*args, *before)
        LINE[:] = [results[-1]]
        return results[0] if single else list(results[:-1])

    return run


def params_of(mebibytes):
    return pltpu.CompilerParams(vmem_limit_bytes=mebibytes << 20)


def whole(shape):
    return pl.BlockSpec(shape, lambda *_: (0,) * len(shape))


def resident():
    return pl.BlockSpec(memory_space=pltpu.VMEM)


def row_tile(tile, cols):
    return pl.BlockSpec((tile, cols), lambda r, *_: (r, 0))


def sds(shape, dtype):
    return jax.ShapeDtypeStruct(shape, dtype)


def row_sum(value):
    return jnp.sum(value, axis=1, keepdims=True)


def segment_tables(segment):
    first = segment[::TILE]
    last = segment[TILE - 1 :: TILE]
    low = jnp.sum((last[None, :] < first[:, None]).astype(jnp.int32), axis=1)
    high = jnp.sum((first[None, :] <= last[:, None]).astype(jnp.int32), axis=1)
    lane = lax.broadcasted_iota(jnp.int32, (SEQ, PAIR), 1) % HEAD_DIM
    same = lane == segment[:, None]
    key_lanes = jnp.where(same, 1.0, 0.0).astype(BF)
    query_lanes = jnp.where((lane < 4) & (~same), -MASK_STEP, 0.0).astype(BF)
    return low, high, key_lanes, query_lanes


def attend_fwd_kernel(
    low_ref, high_ref, x_ref, w_ref, klane_ref, qlane_ref, qkv_ref, ctx_ref, lse_ref, kh_ref, qh_ref, ls_ref
):
    pairs = w_ref.shape[1] // (3 * PAIR)
    lane = lax.broadcasted_iota(jnp.int32, (SEQ, PAIR), 1)
    for p in range(pairs):
        at = 3 * p * PAIR
        qkv_ref[:, at : at + 3 * PAIR] = dot(x_ref[...], w_ref[:, at : at + 3 * PAIR], NN).astype(BF)
        query = qkv_ref[:, at : at + PAIR] * ATTN_SCALE
        keys = qkv_ref[:, at + PAIR : at + 2 * PAIR]
        for h in range(2):
            mine = (lane // HEAD_DIM) == h
            kh_ref[2 * p + h] = jnp.where(mine, keys, klane_ref[...])
            qh_ref[2 * p + h] = jnp.where(mine, query, qlane_ref[...])
    is_first = lax.broadcasted_iota(jnp.int32, (TILE, PAIR), 1) < HEAD_DIM

    def row_block(qb, carry):
        low = low_ref[qb]
        count = high_ref[qb] - low
        rows = pl.ds(pl.multiple_of(qb * TILE, TILE), TILE)
        for width in range(1, TILES + 1):

            @pl.when(count == width)
            def _():
                span = pl.ds(pl.multiple_of(low * TILE, TILE), width * TILE)

                def scores_of(p):
                    return [dot(qh_ref[2 * p + h, rows, :], kh_ref[2 * p + h, span, :], NT) for h in range(2)]

                coming = scores_of(0)
                for p in range(pairs):
                    scores = coming
                    if p + 1 < pairs:
                        coming = scores_of(p + 1)
                    at = (3 * p + 2) * PAIR
                    tops = [jnp.max(s, axis=1, keepdims=True) for s in scores]
                    expo = [jnp.exp(s - m) for s, m in zip(scores, tops)]
                    sums = [row_sum(e) for e in expo]
                    outs = [dot(e.astype(BF), qkv_ref[span, at : at + PAIR], NN) for e in expo]
                    ctx_ref[rows, p * PAIR : (p + 1) * PAIR] = jnp.where(
                        is_first, outs[0] / sums[0], outs[1] / sums[1]
                    ).astype(BF)
                    ls_ref[p, rows, :] = jnp.where(
                        is_first, tops[0] + jnp.log(sums[0]), tops[1] + jnp.log(sums[1])
                    )

        return carry

    lax.fori_loop(0, TILES, row_block, 0)
    for p in range(pairs):
        turned = ls_ref[p].T
        lse_ref[p, 0:1, :] = turned[0:1]
        lse_ref[p, 1:2, :] = turned[HEAD_DIM : HEAD_DIM + 1]


def attend_forward(x, weight, tables):
    pairs = weight.shape[1] // (3 * PAIR)
    low, high, key_lanes, query_lanes = tables
    return ordered_call(
        attend_fwd_kernel,
        grid_spec=dict(
            num_scalar_prefetch=2,
            grid=(1,),
            in_specs=[resident(), resident(), whole((SEQ, PAIR)), whole((SEQ, PAIR))],
            out_specs=[whole((SEQ, pairs * 3 * PAIR)), whole((SEQ, pairs * PAIR)), whole((pairs, 2, SEQ))],
            scratch_shapes=[
                pltpu.VMEM((2 * pairs, SEQ, PAIR), BF),
                pltpu.VMEM((2 * pairs, SEQ, PAIR), BF),
                pltpu.VMEM((pairs, SEQ, PAIR), F32),
            ],
        ),
        out_shape=[
            hbm((SEQ, pairs * 3 * PAIR), BF),
            sds((SEQ, pairs * PAIR), BF),
            sds((pairs, 2, SEQ), F32),
        ],
        compiler_params=params_of(32),
        cost_estimate=LARGE,
        name="attend_fwd",
    )(low, high, x, weight, key_lanes, query_lanes)


def attend_bwd_kernel(
    low_ref, high_ref, qkv_ref, dctx_ref, ctx_ref, lse_ref, klane_ref, qlane_ref, xt_ref, dqkv_ref, gq_ref,
    kh_ref, qh_ref, kt_ref, q0_ref, d0_ref, delta_ref, dqt_ref,
    *, start, pairs,
):
    lane = lax.broadcasted_iota(jnp.int32, (SEQ, PAIR), 1)
    zero = jnp.zeros((SEQ, PAIR), BF)
    for p in range(pairs):
        at = 3 * (p + start) * PAIR
        query = qkv_ref[:, at : at + PAIR] * ATTN_SCALE
        keys = qkv_ref[:, at + PAIR : at + 2 * PAIR]
        dctx = dctx_ref[:, (p + start) * PAIR : (p + start + 1) * PAIR]
        kt_ref[p] = keys.T
        context = ctx_ref[:, (p + start) * PAIR : (p + start + 1) * PAIR]
        prod = (dctx.astype(F32) * context.astype(F32)).T
        for h in range(2):
            mine = (lane // HEAD_DIM) == h
            slot = 2 * p + h
            kh_ref[slot] = jnp.where(mine, keys, klane_ref[...])
            qh_ref[slot] = jnp.where(mine, query, qlane_ref[...])
            q0_ref[slot] = jnp.where(mine, query, zero)
            d0_ref[slot] = jnp.where(mine, dctx, zero)
            delta_ref[slot : slot + 1, :] = jnp.sum(
                prod[h * HEAD_DIM : (h + 1) * HEAD_DIM], axis=0, keepdims=True
            )
        dqt_ref[p] = jnp.zeros((PAIR, SEQ), F32)

    def key_block(kb, carry):
        low = low_ref[kb]
        count = high_ref[kb] - low
        cols = pl.ds(pl.multiple_of(kb * TILE, TILE), TILE)
        for width in range(1, TILES + 1):

            @pl.when(count == width)
            def _():
                span = pl.ds(pl.multiple_of(low * TILE, TILE), width * TILE)

                def products_of(p):
                    at = (3 * (p + start) + 2) * PAIR
                    values = qkv_ref[cols, at : at + PAIR]
                    scores = [dot(kh_ref[2 * p + h, cols, :], qh_ref[2 * p + h, span, :], NT) for h in range(2)]
                    return scores, [dot(values, d0_ref[2 * p + h, span, :], NT) for h in range(2)]

                coming = products_of(0)
                for p in range(pairs):
                    scores, dprob = coming
                    if p + 1 < pairs:
                        coming = products_of(p + 1)
                    prob = [jnp.exp(scores[h] - lse_ref[p + start, h : h + 1, span]) for h in range(2)]
                    low_p = [v.astype(BF) for v in prob]
                    dscore = [
                        (prob[h] * (dprob[h] - delta_ref[2 * p + h : 2 * p + h + 1, span])).astype(BF)
                        for h in range(2)
                    ]
                    a, b = 2 * p, 2 * p + 1
                    dvals = dot(low_p[0], d0_ref[a, span, :], NN) + dot(low_p[1], d0_ref[b, span, :], NN)
                    dkeys = dot(dscore[0], q0_ref[a, span, :], NN) + dot(dscore[1], q0_ref[b, span, :], NN)
                    for h in range(2):
                        part = slice(h * HEAD_DIM, (h + 1) * HEAD_DIM)
                        dqt_ref[p, part, span] += dot(kt_ref[p, part, cols], dscore[h], NN)
                    at = 3 * p * PAIR
                    dqkv_ref[cols, at + PAIR : at + 2 * PAIR] = dkeys.astype(BF)
                    dqkv_ref[cols, at + 2 * PAIR : at + 3 * PAIR] = dvals.astype(BF)

        return carry

    lax.fori_loop(0, TILES, key_block, 0)
    for p in range(pairs):
        at = 3 * p * PAIR
        dqkv_ref[:, at : at + PAIR] = (dqt_ref[p].T * ATTN_SCALE).astype(BF)
        gq_ref[:, at : at + 3 * PAIR] = dot(xt_ref[...], dqkv_ref[:, at : at + 3 * PAIR], NN).astype(BF)


def attend_backward(qkv, dctx, ctx, lse, tables, xt, start, pairs):
    low, high, key_lanes, query_lanes = tables
    return ordered_call(
        functools.partial(attend_bwd_kernel, start=start, pairs=pairs),
        grid_spec=dict(
            num_scalar_prefetch=2,
            grid=(1,),
            in_specs=[
                resident(),
                resident(),
                resident(),
                whole(lse.shape),
                whole((SEQ, PAIR)),
                whole((SEQ, PAIR)),
                resident(),
            ],
            out_specs=[whole((SEQ, pairs * 3 * PAIR)), resident()],
            scratch_shapes=[
                pltpu.VMEM((2 * pairs, SEQ, PAIR), BF),
                pltpu.VMEM((2 * pairs, SEQ, PAIR), BF),
                pltpu.VMEM((pairs, PAIR, SEQ), BF),
                pltpu.VMEM((2 * pairs, SEQ, PAIR), BF),
                pltpu.VMEM((2 * pairs, SEQ, PAIR), BF),
                pltpu.VMEM((2 * pairs, SEQ), F32),
                pltpu.VMEM((pairs, PAIR, SEQ), F32),
            ],
        ),
        out_shape=[hbm((SEQ, pairs * 3 * PAIR), BF), sds((D, pairs * 3 * PAIR), BF)],
        compiler_params=params_of(32),
        cost_estimate=LARGE,
        name="attend_bwd",
    )(low, high, qkv, dctx, ctx, lse, key_lanes, query_lanes, xt)


def mid_kernel(ctx_a, ctx_b, wo_a, wo_b, x_ref, vec_ref, cen_ref, inv_ref, low_ref, lowt_ref):
    attn = dot(ctx_a[...], wo_a[...], NT) + dot(ctx_b[...], wo_b[...], NT)
    res = x_ref[...].astype(F32) + vec_ref[0:1,:]*attn
    mean = row_sum(res)/D
    var = row_sum(res*res)/D - mean*mean
    inv = lax.rsqrt(var+LN_EPS)
    cen = (res-mean)*inv
    cen_ref[...] = cen
    inv_ref[...] = jnp.broadcast_to(inv, inv_ref.shape)
    low = (cen*vec_ref[2:3,:]+vec_ref[3:4,:]).astype(BF)
    low_ref[...] = low
    lowt_ref[...] = low.T

def mid(ctx, out, x, vec, T=256):
    half = D//2
    wo = lambda: whole((D, half))
    return ordered_call(mid_kernel, grid=(SEQ//T,),
        in_specs=[row_tile(T,half), row_tile(T,half), wo(), wo(), row_tile(T,D), whole((8,D))],
        out_specs=[row_tile(T,D), row_tile(T,128), row_tile(T,D), pl.BlockSpec((D,T), lambda r:(0,r))],
        out_shape=[sds((SEQ,D),F32), hbm((SEQ,128),F32), sds((SEQ,D),BF), sds((D,SEQ),BF)],
        compiler_params=params_of(32), cost_estimate=LARGE, name="mid")(ctx[0],ctx[1],out[0],out[1],x,vec)

def gelu_pair(value):
    phi = 0.5 + 0.5 * lax.erf(value * 0.7071067811865476)
    bell = jnp.exp(-0.5 * value * value)
    return value * phi, phi + value * bell * 0.3989422804014327

def ffn_in_kernel(x_ref, w_ref, act_ref, slope_ref):
    pre = dot(x_ref[...], w_ref[...], NN)
    act, slope = gelu_pair(pre)
    act_ref[...] = act.astype(BF)
    slope_ref[...] = slope.astype(BF)

def ffn_in(low, two, width=256):
    units = 4*(D//2)
    return ordered_call(ffn_in_kernel, grid=(units//width,),
        in_specs=[whole((SEQ,D)), pl.BlockSpec((D,width), lambda n:(0,n))],
        out_specs=[pl.BlockSpec((SEQ,width), lambda n:(0,n))]*2,
        out_shape=[hbm((SEQ,units),BF)]*2,
        compiler_params=params_of(32), cost_estimate=LARGE, name="ffn_in")(low, two)

def ffn_out_kernel(core_ref, act_a, act_b, wb_a, wb_b, cen_ref, cot_ref, vec_ref, own_ref, away_ref, gtwo_ref, gffnt_ref, gffn_ref, dn_ref):
    ffn = dot(act_a[...], wb_a[...], NT) + dot(act_b[...], wb_b[...], NT)
    normed = cen_ref[...]*vec_ref[2:3,:]+vec_ref[3:4,:]
    res = normed + vec_ref[1:2,:]*ffn
    mean = row_sum(res)/D
    var = row_sum(res*res)/D - mean*mean
    inv = lax.rsqrt(var+LN_EPS)
    cen = (res-mean)*inv
    gain = vec_ref[4:5,:]
    by_core(core_ref, (cen*gain+vec_ref[5:6,:]).astype(BF), own_ref, away_ref)
    cot = cot_ref[...].astype(F32)
    scaled = cot*gain
    m1 = row_sum(scaled)/D
    m2 = row_sum(scaled*cen)/D
    gtwo = inv*(scaled-m1-cen*m2)
    gtwo_ref[...] = gtwo
    gffn = (vec_ref[1:2,:]*gtwo).astype(BF)
    gffn_ref[...] = gffn
    gffnt_ref[...] = gffn.T
    @pl.when(pl.program_id(0)==0)
    def _(): dn_ref[...] = jnp.zeros(dn_ref.shape, F32)
    dn_ref[0:1,:] += jnp.sum(cot*cen, axis=0, keepdims=True)
    dn_ref[1:2,:] += jnp.sum(cot, axis=0, keepdims=True)

def ffn_out(core, acts, back, cen, cot, vec, T=256):
    half = D//2
    units = 4*half
    return ordered_call(ffn_out_kernel, grid_spec=dict(num_scalar_prefetch=1, grid=(SEQ//T,),
        in_specs=[row_tile(T,units), row_tile(T,units), whole((D,units)), whole((D,units)), row_tile(T,D), row_tile(T,D), whole((8,D))],
        out_specs=[row_tile(T,half), row_tile(T,half), row_tile(T,D), pl.BlockSpec((D,T), lambda r,*_:(0,r)), row_tile(T,D), whole((8,D))]),
        out_shape=[sds((SEQ,half),BF), sds((SEQ,half),BF), hbm((SEQ,D),F32), sds((D,SEQ),BF), sds((SEQ,D),BF), sds((8,D),F32)],
        compiler_params=params_of(32), cost_estimate=LARGE, name="ffn_out")(core[None],in_hbm(acts[0]),in_hbm(acts[1]),back[0],back[1],cen,cot,vec)

def grad_back_kernel(lt_ref, own_ref, away_ref, own_a, own_b, away_a, away_b):
    half_of = pl.program_id(0) // 2
    for which, own, away in ((0, own_a, away_a), (1, own_b, away_b)):

        @pl.when(half_of == which)
        def _():
            away[...] = dot(lt_ref[...], away_ref[...], NN).astype(BF)
            own[...] = dot(lt_ref[...], own_ref[...], NN).astype(BF)


def grad_back(lt, acts):
    width = D // 2
    col = pl.BlockSpec((SEQ, width), lambda n: (0, n))
    first = pl.BlockSpec((D, width), lambda n: (0, jnp.minimum(n, 1)))
    second = pl.BlockSpec((D, width), lambda n: (0, jnp.maximum(n - 2, 0)))
    return ordered_call(
        grad_back_kernel,
        grid=(4,),
        in_specs=[whole((D, SEQ)), col, col],
        out_specs=[first, second, first, second],
        out_shape=[sds((D, 2 * width), BF)] * 4,
        compiler_params=params_of(32),
        cost_estimate=LARGE,
        name="grad_back",
    )(lt, in_hbm(acts[0]), in_hbm(acts[1]))


def inner_bwd_kernel(gffn_ref, sl_a, sl_b, wb_a, wb_b, wi_a, wi_b, wo_a, wo_b, gtwo_ref, cen_ref, inv_ref, vec_ref,
                pre_a, pre_b, gone_ref, gattnt_ref, dctx_a, dctx_b, dn_ref):
    gffn = gffn_ref[...]
    width = 512
    steps = [
        (side, slice(c, c + width))
        for side in ((pre_a, sl_a, wb_a, wi_a), (pre_b, sl_b, wb_b, wi_b))
        for c in range(0, sl_a.shape[1], width)
    ]
    coming = dot(gffn, wb_a[:, steps[0][1]], NN)
    gn = gtwo_ref[...]
    for k, ((pre, slope, _, wi), at) in enumerate(steps):
        hidden = coming
        if k + 1 < len(steps):
            coming = dot(gffn, steps[k + 1][0][2][:, steps[k + 1][1]], NN)
        low = (hidden * slope[:, at].astype(F32)).astype(BF)
        pre[:, at] = low
        gn = gn + dot(low, wi[:, at], NT)
    cen = cen_ref[...]
    scaled = gn*vec_ref[2:3,:]
    m1 = row_sum(scaled)/D
    m2 = row_sum(scaled*cen)/D
    inv = inv_ref[:,0:1]
    gone = inv*(scaled-m1-cen*m2)
    gone_ref[...] = gone
    gattn = (vec_ref[0:1,:]*gone).astype(BF)
    gattnt_ref[...] = gattn.T
    dctx_a[...] = dot(gattn, wo_a[...], NN).astype(BF)
    dctx_b[...] = dot(gattn, wo_b[...], NN).astype(BF)
    @pl.when(pl.program_id(0)==0)
    def _(): dn_ref[...] = jnp.zeros(dn_ref.shape, F32)
    dn_ref[0:1,:] += jnp.sum(gn*cen, axis=0, keepdims=True)
    dn_ref[1:2,:] += jnp.sum(gn, axis=0, keepdims=True)

def inner_bwd(gffn, slopes, back, win, out, gtwo, cen, inv, vec, T=256):
    half=D//2; units=4*half
    wi = lambda: whole((D,units))
    wo = lambda: whole((D,half))
    return ordered_call(inner_bwd_kernel, grid=(SEQ//T,),
        in_specs=[row_tile(T,D), row_tile(T,units), row_tile(T,units), whole((D,units)), whole((D,units)), wi(), wi(), wo(), wo(), row_tile(T,D), row_tile(T,D), row_tile(T,128), whole((8,D))],
        out_specs=[row_tile(T,units), row_tile(T,units), row_tile(T,D), pl.BlockSpec((D,T), lambda r:(0,r)), row_tile(T,half), row_tile(T,half), whole((8,D))],
        out_shape=[hbm((SEQ,units),BF)]*2+[hbm((SEQ,D),F32), sds((D,SEQ),BF), sds((SEQ,half),BF), sds((SEQ,half),BF), sds((8,D),F32)],
        compiler_params=params_of(44), cost_estimate=LARGE, name="inner_bwd")(gffn,in_hbm(slopes[0]),in_hbm(slopes[1]),back[0],back[1],win[0],win[1],out[0],out[1],in_hbm(gtwo),cen,in_hbm(inv),vec)

def grad_weights_two_kernel(
    lowt_ref, gattnt_ref, pre_own, pre_away, ctx_own, ctx_away, own_a, own_b, away_a, away_b
):
    n = pl.program_id(0)

    @pl.when(n < 3)
    def _():
        away_a[...] = dot(lowt_ref[...], pre_away[...], NN).astype(BF)
        own_a[...] = dot(lowt_ref[...], pre_own[...], NN).astype(BF)

    @pl.when(n == 3)
    def _():
        away_b[...] = dot(lowt_ref[...], pre_away[...], NN).astype(BF)
        own_b[...] = dot(lowt_ref[...], pre_own[...], NN).astype(BF)

    @pl.when(n == 4)
    def _():
        away_b[...] = dot(gattnt_ref[...], ctx_away[...], NN).astype(BF)
        own_b[...] = dot(gattnt_ref[...], ctx_own[...], NN).astype(BF)


def grad_weights_two(lowt, gattnt, pre, ctx):
    half = D // 2
    col = pl.BlockSpec((SEQ, half), lambda n: (0, jnp.minimum(n, 3)))
    first = pl.BlockSpec((D, half), lambda n: (0, jnp.minimum(n, 2)))
    second = pl.BlockSpec((D, half), lambda n: (0, jnp.maximum(n - 3, 0)))
    return ordered_call(
        grad_weights_two_kernel,
        grid=(5,),
        in_specs=[whole((D, SEQ)), whole((D, SEQ)), col, col, whole((SEQ, half)), whole((SEQ, half))],
        out_specs=[first, second, first, second],
        out_shape=[sds((D, 3 * half), BF), sds((D, 2 * half), BF)] * 2,
        compiler_params=params_of(32),
        cost_estimate=LARGE,
        name="grad_weights_two",
    )(lowt, gattnt, in_hbm(pre[0]), in_hbm(pre[1]), ctx[0], ctx[1])


def grad_tokens_kernel(core_ref, gone_ref, d_a, d_b, d_c, d_d, w_a, w_b, own_ref, away_ref):
    cut = d_a.shape[1]
    total = gone_ref[...] + dot(d_a[...], w_a[:, :cut], NT) + dot(d_b[...], w_a[:, cut:], NT)
    total = total + dot(d_c[...], w_b[:, :cut], NT) + dot(d_d[...], w_b[:, cut:], NT)
    by_core(core_ref, total.astype(BF), own_ref, away_ref)


def grad_tokens(core, gone, dqkv, wq, T=256):
    half = D//2
    return ordered_call(grad_tokens_kernel, grid_spec=dict(num_scalar_prefetch=1, grid=(SEQ//T,),
        in_specs=[row_tile(T,D), *[row_tile(T,d.shape[1]) for d in dqkv], whole(wq[0].shape), whole(wq[1].shape)],
        out_specs=[row_tile(T,half)]*2), out_shape=[sds((SEQ,half),BF)]*2,
        compiler_params=params_of(32), cost_estimate=LARGE, name="grad_tokens")(core[None],in_hbm(gone),*[in_hbm(d) for d in dqkv],wq[0],wq[1])


def side_by_side_kernel(core_ref, own_ref, away_ref, out_ref, *turned_ref):
    half = away_ref.shape[1]
    first = jnp.where(core_ref[0] == 0, own_ref[0], away_ref[...])
    second = jnp.where(core_ref[0] == 0, away_ref[...], own_ref[0])
    out_ref[:, :half] = first
    out_ref[:, half:] = second
    if turned_ref:
        turned_ref[0][:half, :] = first.T
        turned_ref[0][half:, :] = second.T


def side_by_side(both, away, core, turned):
    half = away.shape[1]
    tile = 512
    outs = 2 if turned else 1
    return ordered_call(
        side_by_side_kernel,
        grid_spec=dict(
            num_scalar_prefetch=1,
            grid=(SEQ // tile,),
            in_specs=[
                pl.BlockSpec((1, tile, half), lambda r, c: (c[0], r, 0)),
                pl.BlockSpec((tile, half), lambda r, c: (r, 0)),
            ],
            out_specs=[
                pl.BlockSpec((tile, 2 * half), lambda r, c: (r, 0)),
                pl.BlockSpec((2 * half, tile), lambda r, c: (0, r)),
            ][:outs],
        ),
        out_shape=[sds((SEQ, 2 * half), BF), hbm((2 * half, SEQ), BF)][:outs],
        compiler_params=params_of(8),
        cost_estimate=SMALL,
        name="side_by_side",
    )(core[None], both, away)


def by_core(core_ref, value, own_ref, away_ref):
    half = own_ref.shape[1]
    first, second = value[:, :half], value[:, half:]
    own_ref[...] = jnp.where(core_ref[0] == 0, first, second)
    away_ref[...] = jnp.where(core_ref[0] == 0, second, first)


def digits_of(count):
    found, shift = [], 0
    while (1 << shift) < count:
        radix = min(4, count >> shift)
        found.append((shift, radix))
        shift += 2 if radix == 4 else 1
    return found


def swap(value, count, mask, axis="dp"):
    return lax.ppermute(value, axis, [(i, i ^ mask) for i in range(count)])


def place_kernel(places_ref, *refs, radix, widths):
    pieces, outs = refs[:radix], refs[radix:]
    for j, piece in enumerate(pieces):

        @pl.when(pl.program_id(0) == j)
        def _():
            start = 0
            for out, width in zip(outs, widths):
                out[:, 0] = piece[:, :, start : start + width]
                start += width


def place(pieces, places, widths=None):
    outer, rows, cols = pieces[0].shape
    radix = len(pieces)
    widths = widths or (cols,)
    placed = ordered_call(
        functools.partial(place_kernel, radix=radix, widths=widths),
        grid_spec=dict(
            num_scalar_prefetch=1,
            grid=(radix,),
            in_specs=[pl.BlockSpec((outer, rows, cols), lambda g, d: (0, 0, 0))] * radix,
            out_specs=[
                pl.BlockSpec((outer, 1, rows, width), lambda g, d: (0, d[g], 0, 0)) for width in widths
            ],
        ),
        out_shape=[sds((outer, radix, rows, width), BF) for width in widths],
        compiler_params=params_of(16),
        cost_estimate=SMALL,
        name="place",
    )(places, *pieces)
    placed = [p.reshape(outer * radix, rows, p.shape[-1]) for p in placed]
    return placed if len(widths) > 1 else placed[0]


def place_two_kernel(digit_ref, a_own, a_got, b_own, b_got, *outs):
    y = pl.program_id(0) // 2
    x = pl.program_id(0) % 2
    width = a_own.shape[-1]
    first = outs[0].shape[-1]
    for source, hit in ((a_own, x == digit_ref[1]), (a_got, x != digit_ref[1])):

        @pl.when(hit)
        def _():
            outs[0][:, 0, 0, :, :width] = source[:, 0]

    for source, hit in ((b_own, y == digit_ref[0]), (b_got, y != digit_ref[0])):

        @pl.when(hit)
        def _():
            outs[0][:, 0, 0, :, width:] = source[:, 0, :, : first - width]
            outs[1][:, 0, 0] = source[:, 0, :, first - width :]


def place_two(a_pieces, b_pieces, digit_y, digit_x, widths):
    outer, rows, a_width = a_pieces[0].shape
    b_width = b_pieces[0].shape[-1]
    outer //= 2
    a_spec = pl.BlockSpec((outer, 1, rows, a_width), lambda g, d: (0, g // 2, 0, 0))
    b_spec = pl.BlockSpec((outer, 1, rows, b_width), lambda g, d: (0, g % 2, 0, 0))
    shaped = [p.reshape(outer, 2, rows, -1) for p in (*a_pieces, *b_pieces)]
    placed = ordered_call(
        place_two_kernel,
        grid_spec=dict(
            num_scalar_prefetch=1,
            grid=(4,),
            in_specs=[a_spec, a_spec, b_spec, b_spec],
            out_specs=[
                pl.BlockSpec((outer, 1, 1, rows, width), lambda g, d: (0, g // 2, g % 2, 0, 0))
                for width in widths
            ],
        ),
        out_shape=[sds((outer, 2, 2, rows, width), BF) for width in widths],
        compiler_params=params_of(32),
        cost_estimate=SMALL,
        name="place_two",
    )(jnp.stack([digit_y, digit_x]), *shaped)
    return [p.reshape(outer * 4 * rows, -1) for p in placed]


def sum_split_kernel(digit_ref, *refs, counts):
    outs = refs[sum(counts) :]
    start = at = 0
    for count in counts:
        terms = refs[at : at + count]
        at += count
        total = terms[0][:, 0].astype(F32)
        for ref in terms[1:]:
            total = total + ref[:, 0].astype(F32)
        total = total.astype(BF)
        stop = start + total.shape[-1]
        for j, out in enumerate(outs):

            @pl.when(pl.program_id(0) == j)
            def _():
                out[:, :, start:stop] = total

        start = stop


def sum_split(runs, digit):
    outer, radix, rows, _ = runs[0][0].shape
    terms = [term for run in runs for term in run]
    cols = sum(run[0].shape[-1] for run in runs)
    return ordered_call(
        functools.partial(sum_split_kernel, counts=[len(run) for run in runs]),
        grid_spec=dict(
            num_scalar_prefetch=1,
            grid=(radix,),
            in_specs=[
                pl.BlockSpec((outer, 1, rows, term.shape[-1]), lambda g, d: (0, d[0] ^ g, 0, 0))
                for term in terms
            ],
            out_specs=[pl.BlockSpec((outer, rows, cols), lambda g, d: (0, 0, 0))] * radix,
        ),
        out_shape=[sds((outer, rows, cols), BF)] * radix,
        compiler_params=params_of(32),
        cost_estimate=SMALL,
        name="sum_split",
    )(digit[None], *terms)


def gather_start(held, count, place_in):
    shift, radix = place_in
    return [held] + [swap(held, count, j << shift) for j in range(1, radix)]


def gather_place(pieces, index, place_in, widths=None):
    shift, radix = place_in
    return place(pieces, ((index >> shift) & (radix - 1)) ^ jnp.arange(radix, dtype=jnp.int32), widths)


def ring(value, count, place_in):
    shift, radix = place_in
    step = 1 << shift
    around = [(i, i + step if (i >> shift) % radix < radix - 1 else i - (radix - 1) * step) for i in range(count)]
    return lax.ppermute(value, "dp", around)


def scatter_split(runs, index, place_in, rows):
    shift, radix = place_in
    shaped = [[t.reshape(-1, radix, rows, t.shape[-1]) for t in run] for run in runs]
    return sum_split(shaped, (index >> shift) & (radix - 1))


def scatter_send(parts, count, place_in):
    return [parts[0]] + [swap(parts[j], count, j << place_in[0]) for j in range(1, place_in[1])]


def sum_all(value, count):
    value = value + swap(value, 2, 1, "mp")
    for shift, radix in digits_of(count):
        parts = [value] + [swap(value, count, j << shift) for j in range(1, radix)]
        value = parts[0] + parts[1]
        if radix == 4:
            value = value + (parts[2] + parts[3])
    return value


def finish_kernel(*refs):
    terms, mask_ref, total_ref, square_ref = refs[:-3], refs[-3], refs[-2], refs[-1]
    total = terms[0][0].astype(F32)
    for term in terms[1:]:
        total = total + term[0].astype(F32)
    total = total * mask_ref[...]
    total_ref[...] = total
    square_ref[...] = jnp.full((8, 128), jnp.sum(total * total), F32)


def finish(terms, mask):
    shape = terms[0].shape
    return ordered_call(
        finish_kernel,
        in_specs=[whole(shape)] * len(terms) + [whole((1, shape[2]))],
        out_specs=[whole(shape[1:]), whole((8, 128))],
        out_shape=[sds(shape[1:], F32), sds((8, 128), F32)],
        compiler_params=params_of(8),
        cost_estimate=SMALL,
        name="finish",
    )(*terms, mask)


def adam_step(weight, gradient, first_mom, second, step_rate, decay_rate):
    first_new = BETA_ONE * first_mom + (1.0 - BETA_ONE) * gradient
    second_new = BETA_TWO * second + (1.0 - BETA_TWO) * gradient * gradient
    update = (
        first_new
        / (1.0 - BETA_ONE**STEP)
        / (jnp.sqrt(second_new / (1.0 - BETA_TWO**STEP)) + ADAM_EPS)
    )
    return (weight - step_rate * (update + decay_rate * weight), first_new, second_new)


def adam_kernel(factor_ref, g_one, g_two, g_back, g_norm, *refs):
    weights, firsts, seconds, outs = refs[:5], refs[5:10], refs[10:15], refs[15:]
    factor = factor_ref[0:1, 0:1]
    half = weights[0].shape[2]

    def step(slot, gradient, at, rate, decay):
        new = adam_step(
            weights[slot][at], gradient * factor, firsts[slot][at], seconds[slot][at], rate, decay
        )
        for kind in range(3):
            outs[5 * kind + slot][at] = new[kind]

    for t in range(3):
        for pair in range(half // PAIR):
            start = (3 * pair + t) * PAIR
            at = (t, slice(None), slice(pair * PAIR, (pair + 1) * PAIR))
            step(0, g_one[:, start : start + PAIR], at, LEARN_RATE, WEIGHT_DECAY)
    everything = (slice(None), slice(None))
    step(1, g_two[:, 4 * half :], everything, LEARN_RATE, WEIGHT_DECAY)
    step(2, g_two[:, : 4 * half], everything, LEARN_RATE, WEIGHT_DECAY)
    step(3, g_back[...], everything, LEARN_RATE, WEIGHT_DECAY)
    step(4, g_norm[...], everything, NORM_RATE, 0.0)


def adam(factor, gradients, weights, firsts, seconds):
    states = (*weights, *firsts, *seconds)
    return ordered_call(
        adam_kernel,
        in_specs=[whole(v.shape) for v in (factor, *gradients, *states)],
        out_specs=[whole(v.shape) for v in states],
        out_shape=[sds(v.shape, F32) for v in states],
        compiler_params=params_of(24),
        cost_estimate=SMALL,
        name="adam",
    )(factor, *gradients, *[in_hbm(v) for v in states])


def shards(
    count,
    tokens,
    cotangent,
    segments,
    head_gates,
    unit_gates,
    hidden_gates,
    layer_gates,
    w_qkv,
    w_out,
    w_in,
    w_back,
    norm_params,
    mom_qkv,
    mom_out,
    mom_in,
    mom_back,
    mom_norm,
    sec_qkv,
    sec_out,
    sec_in,
    sec_back,
    sec_norm,
):
    LINE.clear()
    index = lax.axis_index("dp")
    core = lax.axis_index("mp")
    rows = D // count
    half = D // 2
    pairs = half // PAIR
    head_mask = jnp.repeat(head_gates.astype(F32), HEAD_DIM)
    unit_mask = unit_gates.astype(F32)
    gate_attn = layer_gates[0]
    gate_ffn = layer_gates[1]

    shard_qkv = (
        w_qkv.astype(BF).reshape(3, rows, pairs, PAIR).transpose(1, 2, 0, 3).reshape(rows, 3 * half)
    )
    shard_out = (w_out.T * head_mask[None, :]).astype(BF)
    shard_two = jnp.concatenate([w_in.astype(BF), shard_out], axis=1)
    shard_back = (w_back.T * unit_mask[None, :]).astype(BF)
    digits = digits_of(count)

    def other_core(value):
        return swap(value, 2, 1, "mp")

    def both(own, away):
        return jnp.where(
            core == 0, jnp.concatenate([own, away], axis=-1), jnp.concatenate([away, own], axis=-1)
        )

    plane = digits[0]
    upper = [(bit, 2) for bit in range(plane[1] // 2, count.bit_length() - 1)]
    bit_y, bit_x = (index >> 1) & 1, index & 1

    def direct_start(held):
        for place_in in digits[:1:-1]:
            held = gather_place(gather_start(held, count, place_in), index, place_in)
        return gather_start(held, count, digits[1])

    def halves_start(pieces, widths):
        a, b = gather_place(pieces, index, upper[0], widths)
        return [a, swap(a, count, 2)], [b, swap(b, count, 1)]

    def halves_turn(halves):
        a = gather_place(halves[0], index, (1, 2))
        b = gather_place(halves[1], index, (0, 2))
        return [a, swap(a, count, 1)], [b, swap(b, count, 2)]

    def halves_place(halves):
        return place_two(*halves, bit_y, bit_x, (4 * half, half))

    def grow(pieces, place_in):
        return gather_place(pieces, index, place_in).reshape(1, -1, pieces[0].shape[-1])

    tok_away = other_core(lax.dynamic_index_in_dim(tokens, 1 - core, 0, keepdims=False))
    one = direct_start(shard_qkv[None])
    back = gather_start(shard_back[None], count, (0, 2))
    segment = lax.dynamic_index_in_dim(segments, core, 0, keepdims=False)[0]
    tables = segment_tables(segment)
    vectors = jnp.concatenate([hidden_gates.astype(F32)[None], norm_params], axis=0)
    vectors = both(vectors, other_core(vectors))
    hidden_mask, params = vectors[0], vectors[1:]
    vec = jnp.concatenate(
        [gate_attn * hidden_mask[None], gate_ffn * hidden_mask[None], params, params[:2]], axis=0
    )
    back = gather_start(grow(back, (0, 2)), count, (1, 2))
    wait_for(vec)
    x, xt = side_by_side(tokens, tok_away, core, True)
    wait_for(back[1])
    one = gather_start(gather_place(one, index, digits[1]), count, plane)
    two = gather_start(later(shard_two)[None], count, upper[-1])
    z_digit = digits[1]
    two = gather_place(two, index, upper[-1])
    for place_in in upper[-2:0:-1]:
        two = gather_place(gather_start(two, count, place_in), index, place_in)
    two = halves_start(gather_start(two, count, upper[0]), (1024, 5 * half - 1024))
    mine_qkv = gather_place(one, index, plane).reshape(D, -1)
    away_qkv = other_core(mine_qkv)
    back = grow(back, (1, 2))
    back = [back, ring(back, count, z_digit)]
    qkv_own, ctx_own, lse_own = attend_forward(x, mine_qkv, tables)
    core_later = later(core)
    cot_away = other_core(lax.dynamic_index_in_dim(cotangent, 1 - core_later, 0, keepdims=False))
    wait_for(back[-1])
    two = halves_turn(two)
    while len(back) < z_digit[1] - 1:
        back.append(ring(back[-1], count, z_digit))
    qkv_away, ctx_away, lse_away = attend_forward(x, away_qkv, tables)
    wait_for(back[-1])
    (grad_out,) = side_by_side(cotangent, cot_away, core, False)
    mine_in, mine_out = halves_place(two)
    away_out = other_core(mine_out)
    away_in = other_core(mine_in)
    if len(back) < z_digit[1]:
        back.append(ring(back[-1], count, z_digit))
    ctx = (ctx_own, ctx_away)
    lse = (lse_own, lse_away)
    qkv = (qkv_own, qkv_away)
    qkv_sides = (mine_qkv, away_qkv)
    in_sides = (mine_in, away_in)
    out_sides = (mine_out, away_out)
    centred_one, inv_one, normed_low, normed_turned = mid(ctx, out_sides, x, vec)
    act_own, slope_own = ffn_in(normed_low, mine_in)
    z_here = (index >> z_digit[0]) & (z_digit[1] - 1)
    z_from = (z_here - jnp.arange(z_digit[1], dtype=jnp.int32)) & (z_digit[1] - 1)
    back = place(back, z_from).reshape(1, -1, back[0].shape[-1])
    for place_in in digits[2:]:
        back = grow(gather_start(back, count, place_in), place_in)
    mine_back = back.reshape(D, -1)
    away_back = other_core(mine_back)
    act_away, slope_away = ffn_in(normed_low, away_in)
    acts, slopes = (act_own, act_away), (slope_own, slope_away)
    back_sides = (mine_back, away_back)
    result_own, result_away, grad_two, grad_ffn_turned, grad_ffn, dnorm_two = ffn_out(
        core, acts, back_sides, centred_one, grad_out, vec
    )
    cores_here = jnp.stack([core, 1 - core])

    def send_back(own, away):
        return place([own[None], other_core(away)[None]], cores_here)

    bit = [(0, 2), (1, 2)]

    def over_cores(own, away):
        return [own, other_core(away)]

    def split_a(terms, step):
        return scatter_send(scatter_split([terms], index, bit[step], rows), count, bit[step])

    def split_b(terms, step):
        place_in = bit[1 - step]
        return scatter_send(scatter_split([terms], index, place_in, rows * (2 - step)), count, place_in)

    def split_z(runs, level):
        place_in = upper[level]
        return [scatter_send(scatter_split(runs, index, place_in, rows), count, place_in)]

    back_own_a, back_own_b, back_away_a, back_away_b = grad_back(grad_ffn_turned, acts)
    back_a, back_b = over_cores(back_own_a, back_away_a), over_cores(back_own_b, back_away_b)
    pre_own, pre_away, grad_one, grad_attn_turned, dctx_own, dctx_away, dnorm_one = inner_bwd(
        grad_ffn, slopes, back_sides, in_sides, out_sides, grad_two, centred_one, inv_one, vec
    )
    back_a, back_b = split_a(back_a, 0), split_b(back_b, 0)
    out_tokens = send_back(result_own, result_away)
    two_own_a, two_own_b, two_away_a, two_away_b = grad_weights_two(
        normed_turned, grad_attn_turned, (pre_own, pre_away), ctx
    )
    back_a, back_b = split_a(back_a, 1), split_b(back_b, 1)
    two_a, two_b = over_cores(two_own_a, two_away_a), over_cores(two_own_b, two_away_b)

    def attend_back(side, start, many):
        dctx = (dctx_own, dctx_away)[side]
        return attend_backward(qkv[side], dctx, ctx[side], lse[side], tables, xt, start, many)

    away_dqkv_a, away_gq_a = attend_back(1, 0, 1)
    back = split_z([back_a, back_b], 0)
    two_a, two_b = split_a(two_a, 0), split_b(two_b, 0)
    away_dqkv_b, away_gq_b = attend_back(1, 1, pairs - 1)
    for level in range(1, len(upper)):
        back = split_z(back, level)
    two_a, two_b = split_a(two_a, 1), split_b(two_b, 1)
    own_dqkv_b, own_gq_b = attend_back(0, 1, pairs - 1)
    sum_back, square_back = finish(back[0], unit_mask[None])
    two = [two_a, two_b]
    for place_in in digits[1:]:
        two = [scatter_send(scatter_split(two, index, place_in, rows), count, place_in)]
    one_b = split_b(over_cores(own_gq_b, away_gq_b), 0)
    own_dqkv_a, own_gq_a = attend_back(0, 0, 1)
    one_a = scatter_split([over_cores(own_gq_a, away_gq_a)], index, plane, rows)
    one_a = scatter_send(one_a, count, plane)
    one_b = split_b(one_b, 1)
    mask_two = jnp.concatenate([jnp.ones((4 * half,), F32), head_mask])
    sum_two, square_two = finish(two[0], mask_two[None])
    token_own, token_away = grad_tokens(
        core, grad_one, (own_dqkv_a, own_dqkv_b, away_dqkv_a, away_dqkv_b), qkv_sides
    )
    one = [one_a, one_b]
    for place_in in digits[1:]:
        one = [scatter_send(scatter_split(one, index, place_in, rows), count, place_in)]
    sum_one, square_one = finish(one[0], jnp.ones((1, 3 * half), F32))
    line = list(LINE)
    input_grad = send_back(token_own, token_away)
    LINE[:] = line

    square = (square_back + square_two + square_one) / 1024.0
    norm_rows = jnp.concatenate([dnorm_one[:2], dnorm_two[:2]]).reshape(-1, 128)
    packed = jnp.concatenate([norm_rows, square], axis=0)
    packed = sum_all(packed, count)
    norm_full = packed[:-8].reshape(4, D)
    total_square = jnp.sum(packed[-8:]) + jnp.sum(norm_full * norm_full)
    grad_norm = jnp.sqrt(total_square)
    factor = jnp.minimum(1.0, CLIP_NORM / grad_norm)
    norm_here = lax.dynamic_slice_in_dim(norm_full, core * half, half, 1)
    def turn(values):
        return [v.T if slot in (1, 3) else v for slot, v in enumerate(values)]

    states = adam(
        jnp.full((8, 128), factor, F32),
        (sum_one, sum_two, sum_back, norm_here),
        turn((w_qkv, w_out, w_in, w_back, norm_params)),
        turn((mom_qkv, mom_out, mom_in, mom_back, mom_norm)),
        turn((sec_qkv, sec_out, sec_in, sec_back, sec_norm)),
    )
    return (
        out_tokens,
        input_grad,
        grad_norm,
        *turn(states[:5]),
        *turn(states[5:10]),
        *turn(states[10:]),
    )


def solution(mesh):
    weight_specs = (P(None, "dp", "mp"), P("mp", "dp"), P("dp", "mp"), P("mp", "dp"), P(None, "mp"))
    in_specs = (
        P(None, "dp", "mp"),
        P(None, "dp", "mp"),
        P(None, "dp", None),
        P("mp"),
        P("mp"),
        P("mp"),
        P(),
    ) + weight_specs * 3
    out_specs = (P(None, "dp", "mp"), P(None, "dp", "mp"), P()) + weight_specs * 3
    count = mesh.shape["dp"]

    def body(*args):
        return shards(count, *args)

    return jax.shard_map(body, mesh=mesh, in_specs=in_specs, out_specs=out_specs, check_vma=False)
```

```python
import functools

import jax
import jax.numpy as jnp
from jax import lax
from jax.experimental import pallas as pl
from jax.experimental.pallas import tpu as pltpu
from jax.sharding import PartitionSpec as P

D = 768
HEAD_DIM = 64
SEQ = 1024
STEP = 10
TILE = 256
TILES = SEQ // TILE
PAIR = 128

LN_EPS = 1e-12
CLIP_NORM = 1.0
LEARN_RATE = 0.06
NORM_RATE = 0.3
WEIGHT_DECAY = 0.01
BETA_ONE = 0.9
BETA_TWO = 0.999
ADAM_EPS = 1e-08
ATTN_SCALE = HEAD_DIM ** (-0.5)
MASK_STEP = float(2**30)
NT = (((1,), (1,)), ((), ()))
NN = (((1,), (0,)), ((), ()))
TN = (((0,), (0,)), ((), ()))
BF = jnp.bfloat16
F32 = jnp.float32
LARGE = pl.CostEstimate(flops=33 * 10**9, bytes_accessed=1024, transcendentals=0)
SMALL = pl.CostEstimate(flops=1024, bytes_accessed=1024, transcendentals=0)


def dot(left, right, dims):
    return lax.dot_general(left, right, dims, preferred_element_type=F32)


def later(value):
    return lax.optimization_barrier((value, LINE[-1]))[0]


def hbm(shape, dtype):
    return pltpu.HBM(shape, dtype)


def in_hbm(value):
    return pltpu.with_memory_space_constraint(value, pltpu.HBM)


LINE = []


def wait_for(value):
    LINE.append(in_hbm(value))


def ordered_call(kernel, *, out_shape, grid=(), in_specs=(), out_specs=(), grid_spec=None, **rest):
    spec = dict(num_scalar_prefetch=0, grid=grid, in_specs=in_specs, out_specs=out_specs, scratch_shapes=())
    spec.update(grid_spec or {})
    single = not isinstance(out_shape, (list, tuple))
    shapes = [out_shape] if single else list(out_shape)
    outs = [spec["out_specs"]] if single else list(spec["out_specs"])
    before = list(LINE)
    first = spec["num_scalar_prefetch"] + len(spec["in_specs"])

    def body(*refs):
        after = refs[first + len(before) :]
        after[len(outs)][...] = jnp.zeros((8, 128), F32)
        kernel(*refs[:first], *after[: len(outs)], *after[len(outs) + 1 :])

    call = pl.pallas_call(
        body,
        grid_spec=pltpu.PrefetchScalarGridSpec(
            num_scalar_prefetch=spec["num_scalar_prefetch"],
            grid=spec["grid"],
            in_specs=list(spec["in_specs"]) + [pl.BlockSpec(memory_space=pl.ANY)] * len(before),
            out_specs=outs + [whole((8, 128))],
            scratch_shapes=spec["scratch_shapes"],
        ),
        out_shape=shapes + [sds((8, 128), F32)],
        **rest,
    )

    def run(*args):
        results = call(*args, *before)
        LINE[:] = [results[-1]]
        return results[0] if single else list(results[:-1])

    return run


def params_of(mebibytes):
    return pltpu.CompilerParams(vmem_limit_bytes=mebibytes << 20)


def whole(shape):
    return pl.BlockSpec(shape, lambda *_: (0,) * len(shape))


def resident():
    return pl.BlockSpec(memory_space=pltpu.VMEM)


def row_tile(tile, cols):
    return pl.BlockSpec((tile, cols), lambda r, *_: (r, 0))


def sds(shape, dtype):
    return jax.ShapeDtypeStruct(shape, dtype)


def row_sum(value):
    return jnp.sum(value, axis=1, keepdims=True)


def segment_tables(segment):
    first = segment[::TILE]
    last = segment[TILE - 1 :: TILE]
    low = jnp.sum((last[None, :] < first[:, None]).astype(jnp.int32), axis=1)
    high = jnp.sum((first[None, :] <= last[:, None]).astype(jnp.int32), axis=1)
    lane = lax.broadcasted_iota(jnp.int32, (SEQ, PAIR), 1) % HEAD_DIM
    same = lane == segment[:, None]
    key_lanes = jnp.where(same, 1.0, 0.0).astype(BF)
    query_lanes = jnp.where((lane < 4) & (~same), -MASK_STEP, 0.0).astype(BF)
    return low, high, key_lanes, query_lanes


def attend_fwd_kernel(
    low_ref, high_ref, x_ref, w_ref, klane_ref, qlane_ref, qkv_ref, ctx_ref, lse_ref, kh_ref, qh_ref, ls_ref
):
    pairs = w_ref.shape[1] // (3 * PAIR)
    lane = lax.broadcasted_iota(jnp.int32, (SEQ, PAIR), 1)
    for p in range(pairs):
        at = 3 * p * PAIR
        qkv_ref[:, at : at + 3 * PAIR] = dot(x_ref[...], w_ref[:, at : at + 3 * PAIR], NN).astype(BF)
        query = qkv_ref[:, at : at + PAIR] * ATTN_SCALE
        keys = qkv_ref[:, at + PAIR : at + 2 * PAIR]
        for h in range(2):
            mine = (lane // HEAD_DIM) == h
            kh_ref[2 * p + h] = jnp.where(mine, keys, klane_ref[...])
            qh_ref[2 * p + h] = jnp.where(mine, query, qlane_ref[...])
    is_first = lax.broadcasted_iota(jnp.int32, (TILE, PAIR), 1) < HEAD_DIM

    def row_block(qb, carry):
        low = low_ref[qb]
        count = high_ref[qb] - low
        rows = pl.ds(pl.multiple_of(qb * TILE, TILE), TILE)
        for width in range(1, TILES + 1):

            @pl.when(count == width)
            def _():
                span = pl.ds(pl.multiple_of(low * TILE, TILE), width * TILE)

                def scores_of(p):
                    return [dot(qh_ref[2 * p + h, rows, :], kh_ref[2 * p + h, span, :], NT) for h in range(2)]

                coming = scores_of(0)
                for p in range(pairs):
                    scores = coming
                    if p + 1 < pairs:
                        coming = scores_of(p + 1)
                    at = (3 * p + 2) * PAIR
                    tops = [jnp.max(s, axis=1, keepdims=True) for s in scores]
                    expo = [jnp.exp(s - m) for s, m in zip(scores, tops)]
                    sums = [row_sum(e) for e in expo]
                    outs = [dot(e.astype(BF), qkv_ref[span, at : at + PAIR], NN) for e in expo]
                    ctx_ref[rows, p * PAIR : (p + 1) * PAIR] = jnp.where(
                        is_first, outs[0] / sums[0], outs[1] / sums[1]
                    ).astype(BF)
                    ls_ref[p, rows, :] = jnp.where(
                        is_first, tops[0] + jnp.log(sums[0]), tops[1] + jnp.log(sums[1])
                    )

        return carry

    lax.fori_loop(0, TILES, row_block, 0)
    for p in range(pairs):
        turned = ls_ref[p].T
        lse_ref[p, 0:1, :] = turned[0:1]
        lse_ref[p, 1:2, :] = turned[HEAD_DIM : HEAD_DIM + 1]


def attend_forward(x, weight, tables):
    pairs = weight.shape[1] // (3 * PAIR)
    low, high, key_lanes, query_lanes = tables
    return ordered_call(
        attend_fwd_kernel,
        grid_spec=dict(
            num_scalar_prefetch=2,
            grid=(1,),
            in_specs=[resident(), resident(), whole((SEQ, PAIR)), whole((SEQ, PAIR))],
            out_specs=[whole((SEQ, pairs * 3 * PAIR)), whole((SEQ, pairs * PAIR)), whole((pairs, 2, SEQ))],
            scratch_shapes=[
                pltpu.VMEM((2 * pairs, SEQ, PAIR), BF),
                pltpu.VMEM((2 * pairs, SEQ, PAIR), BF),
                pltpu.VMEM((pairs, SEQ, PAIR), F32),
            ],
        ),
        out_shape=[
            hbm((SEQ, pairs * 3 * PAIR), BF),
            sds((SEQ, pairs * PAIR), BF),
            sds((pairs, 2, SEQ), F32),
        ],
        compiler_params=params_of(32),
        cost_estimate=LARGE,
        name="attend_fwd",
    )(low, high, x, weight, key_lanes, query_lanes)


def attend_bwd_kernel(
    low_ref, high_ref, qkv_ref, dctx_ref, ctx_ref, lse_ref, klane_ref, qlane_ref, xt_ref, dqkv_ref, gq_ref,
    kh_ref, qh_ref, kt_ref, q0_ref, d0_ref, delta_ref, dqt_ref,
    *, start, pairs,
):
    lane = lax.broadcasted_iota(jnp.int32, (SEQ, PAIR), 1)
    zero = jnp.zeros((SEQ, PAIR), BF)
    for p in range(pairs):
        at = 3 * (p + start) * PAIR
        query = qkv_ref[:, at : at + PAIR] * ATTN_SCALE
        keys = qkv_ref[:, at + PAIR : at + 2 * PAIR]
        dctx = dctx_ref[:, (p + start) * PAIR : (p + start + 1) * PAIR]
        kt_ref[p] = keys.T
        context = ctx_ref[:, (p + start) * PAIR : (p + start + 1) * PAIR]
        prod = (dctx.astype(F32) * context.astype(F32)).T
        for h in range(2):
            mine = (lane // HEAD_DIM) == h
            slot = 2 * p + h
            kh_ref[slot] = jnp.where(mine, keys, klane_ref[...])
            qh_ref[slot] = jnp.where(mine, query, qlane_ref[...])
            q0_ref[slot] = jnp.where(mine, query, zero)
            d0_ref[slot] = jnp.where(mine, dctx, zero)
            delta_ref[slot : slot + 1, :] = jnp.sum(
                prod[h * HEAD_DIM : (h + 1) * HEAD_DIM], axis=0, keepdims=True
            )
        dqt_ref[p] = jnp.zeros((PAIR, SEQ), F32)

    def key_block(kb, carry):
        low = low_ref[kb]
        count = high_ref[kb] - low
        cols = pl.ds(pl.multiple_of(kb * TILE, TILE), TILE)
        for width in range(1, TILES + 1):

            @pl.when(count == width)
            def _():
                span = pl.ds(pl.multiple_of(low * TILE, TILE), width * TILE)

                def products_of(p):
                    at = (3 * (p + start) + 2) * PAIR
                    values = qkv_ref[cols, at : at + PAIR]
                    scores = [dot(kh_ref[2 * p + h, cols, :], qh_ref[2 * p + h, span, :], NT) for h in range(2)]
                    return scores, [dot(values, d0_ref[2 * p + h, span, :], NT) for h in range(2)]

                coming = products_of(0)
                for p in range(pairs):
                    scores, dprob = coming
                    if p + 1 < pairs:
                        coming = products_of(p + 1)
                    prob = [jnp.exp(scores[h] - lse_ref[p + start, h : h + 1, span]) for h in range(2)]
                    low_p = [v.astype(BF) for v in prob]
                    dscore = [
                        (prob[h] * (dprob[h] - delta_ref[2 * p + h : 2 * p + h + 1, span])).astype(BF)
                        for h in range(2)
                    ]
                    a, b = 2 * p, 2 * p + 1
                    dvals = dot(low_p[0], d0_ref[a, span, :], NN) + dot(low_p[1], d0_ref[b, span, :], NN)
                    dkeys = dot(dscore[0], q0_ref[a, span, :], NN) + dot(dscore[1], q0_ref[b, span, :], NN)
                    for h in range(2):
                        part = slice(h * HEAD_DIM, (h + 1) * HEAD_DIM)
                        dqt_ref[p, part, span] += dot(kt_ref[p, part, cols], dscore[h], NN)
                    at = 3 * p * PAIR
                    dqkv_ref[cols, at + PAIR : at + 2 * PAIR] = dkeys.astype(BF)
                    dqkv_ref[cols, at + 2 * PAIR : at + 3 * PAIR] = dvals.astype(BF)

        return carry

    lax.fori_loop(0, TILES, key_block, 0)
    for p in range(pairs):
        at = 3 * p * PAIR
        dqkv_ref[:, at : at + PAIR] = (dqt_ref[p].T * ATTN_SCALE).astype(BF)
        gq_ref[:, at : at + 3 * PAIR] = dot(xt_ref[...], dqkv_ref[:, at : at + 3 * PAIR], NN).astype(BF)


def attend_backward(qkv, dctx, ctx, lse, tables, xt, start, pairs):
    low, high, key_lanes, query_lanes = tables
    return ordered_call(
        functools.partial(attend_bwd_kernel, start=start, pairs=pairs),
        grid_spec=dict(
            num_scalar_prefetch=2,
            grid=(1,),
            in_specs=[
                resident(),
                resident(),
                resident(),
                whole(lse.shape),
                whole((SEQ, PAIR)),
                whole((SEQ, PAIR)),
                resident(),
            ],
            out_specs=[whole((SEQ, pairs * 3 * PAIR)), resident()],
            scratch_shapes=[
                pltpu.VMEM((2 * pairs, SEQ, PAIR), BF),
                pltpu.VMEM((2 * pairs, SEQ, PAIR), BF),
                pltpu.VMEM((pairs, PAIR, SEQ), BF),
                pltpu.VMEM((2 * pairs, SEQ, PAIR), BF),
                pltpu.VMEM((2 * pairs, SEQ, PAIR), BF),
                pltpu.VMEM((2 * pairs, SEQ), F32),
                pltpu.VMEM((pairs, PAIR, SEQ), F32),
            ],
        ),
        out_shape=[hbm((SEQ, pairs * 3 * PAIR), BF), sds((D, pairs * 3 * PAIR), BF)],
        compiler_params=params_of(32),
        cost_estimate=LARGE,
        name="attend_bwd",
    )(low, high, qkv, dctx, ctx, lse, key_lanes, query_lanes, xt)


def mid_kernel(ctx_a, ctx_b, wo_a, wo_b, x_ref, vec_ref, cen_ref, inv_ref, low_ref, lowt_ref):
    attn = dot(ctx_a[...], wo_a[...], NT) + dot(ctx_b[...], wo_b[...], NT)
    res = x_ref[...].astype(F32) + vec_ref[0:1,:]*attn
    mean = row_sum(res)/D
    var = row_sum(res*res)/D - mean*mean
    inv = lax.rsqrt(var+LN_EPS)
    cen = (res-mean)*inv
    cen_ref[...] = cen
    inv_ref[...] = jnp.broadcast_to(inv, inv_ref.shape)
    low = (cen*vec_ref[2:3,:]+vec_ref[3:4,:]).astype(BF)
    low_ref[...] = low
    lowt_ref[...] = low.T

def mid(ctx, out, x, vec, T=256):
    half = D//2
    wo = lambda: whole((D, half))
    return ordered_call(mid_kernel, grid=(SEQ//T,),
        in_specs=[row_tile(T,half), row_tile(T,half), wo(), wo(), row_tile(T,D), whole((8,D))],
        out_specs=[row_tile(T,D), row_tile(T,128), row_tile(T,D), pl.BlockSpec((D,T), lambda r:(0,r))],
        out_shape=[sds((SEQ,D),F32), hbm((SEQ,128),F32), sds((SEQ,D),BF), sds((D,SEQ),BF)],
        compiler_params=params_of(32), cost_estimate=LARGE, name="mid")(ctx[0],ctx[1],out[0],out[1],x,vec)

def gelu_pair(value):
    phi = 0.5 + 0.5 * lax.erf(value * 0.7071067811865476)
    bell = jnp.exp(-0.5 * value * value)
    return value * phi, phi + value * bell * 0.3989422804014327

def ffn_in_kernel(x_ref, w_ref, act_ref, slope_ref):
    pre = dot(x_ref[...], w_ref[...], NN)
    act, slope = gelu_pair(pre)
    act_ref[...] = act.astype(BF)
    slope_ref[...] = slope.astype(BF)

def ffn_in(low, two, width=256):
    units = 4*(D//2)
    return ordered_call(ffn_in_kernel, grid=(units//width,),
        in_specs=[whole((SEQ,D)), pl.BlockSpec((D,width), lambda n:(0,n))],
        out_specs=[pl.BlockSpec((SEQ,width), lambda n:(0,n))]*2,
        out_shape=[hbm((SEQ,units),BF)]*2,
        compiler_params=params_of(32), cost_estimate=LARGE, name="ffn_in")(low, two)

def ffn_out_kernel(core_ref, act_a, act_b, wb_a, wb_b, cen_ref, cot_ref, vec_ref, own_ref, away_ref, gtwo_ref, gffnt_ref, gffn_ref, dn_ref):
    ffn = dot(act_a[...], wb_a[...], NT) + dot(act_b[...], wb_b[...], NT)
    normed = cen_ref[...]*vec_ref[2:3,:]+vec_ref[3:4,:]
    res = normed + vec_ref[1:2,:]*ffn
    mean = row_sum(res)/D
    var = row_sum(res*res)/D - mean*mean
    inv = lax.rsqrt(var+LN_EPS)
    cen = (res-mean)*inv
    gain = vec_ref[4:5,:]
    by_core(core_ref, (cen*gain+vec_ref[5:6,:]).astype(BF), own_ref, away_ref)
    cot = cot_ref[...].astype(F32)
    scaled = cot*gain
    m1 = row_sum(scaled)/D
    m2 = row_sum(scaled*cen)/D
    gtwo = inv*(scaled-m1-cen*m2)
    gtwo_ref[...] = gtwo
    gffn = (vec_ref[1:2,:]*gtwo).astype(BF)
    gffn_ref[...] = gffn
    gffnt_ref[...] = gffn.T
    @pl.when(pl.program_id(0)==0)
    def _(): dn_ref[...] = jnp.zeros(dn_ref.shape, F32)
    dn_ref[0:1,:] += jnp.sum(cot*cen, axis=0, keepdims=True)
    dn_ref[1:2,:] += jnp.sum(cot, axis=0, keepdims=True)

def ffn_out(core, acts, back, cen, cot, vec, T=256):
    half = D//2
    units = 4*half
    return ordered_call(ffn_out_kernel, grid_spec=dict(num_scalar_prefetch=1, grid=(SEQ//T,),
        in_specs=[row_tile(T,units), row_tile(T,units), whole((D,units)), whole((D,units)), row_tile(T,D), row_tile(T,D), whole((8,D))],
        out_specs=[row_tile(T,half), row_tile(T,half), row_tile(T,D), pl.BlockSpec((D,T), lambda r,*_:(0,r)), row_tile(T,D), whole((8,D))]),
        out_shape=[sds((SEQ,half),BF), sds((SEQ,half),BF), hbm((SEQ,D),F32), sds((D,SEQ),BF), sds((SEQ,D),BF), sds((8,D),F32)],
        compiler_params=params_of(32), cost_estimate=LARGE, name="ffn_out")(core[None],in_hbm(acts[0]),in_hbm(acts[1]),back[0],back[1],cen,cot,vec)

def grad_back_kernel(lt_ref, own_ref, away_ref, own_a, own_b, away_a, away_b):
    for which, own, away in ((0, own_a, away_a), (1, own_b, away_b)):

        @pl.when(pl.program_id(0) == which)
        def _():
            away[...] = dot(lt_ref[...], away_ref[...], NN).astype(BF)
            own[...] = dot(lt_ref[...], own_ref[...], NN).astype(BF)


def grad_back(lt, acts):
    width = D
    col = pl.BlockSpec((SEQ, width), lambda n: (0, n))
    return ordered_call(
        grad_back_kernel,
        grid=(2,),
        in_specs=[whole((D, SEQ)), col, col],
        out_specs=[resident()] * 4,
        out_shape=[sds((D, width), BF)] * 4,
        compiler_params=params_of(32),
        cost_estimate=LARGE,
        name="grad_back",
    )(lt, in_hbm(acts[0]), in_hbm(acts[1]))


def inner_bwd_kernel(gffn_ref, sl_a, sl_b, wb_a, wb_b, wi_a, wi_b, wo_a, wo_b, gtwo_ref, cen_ref, inv_ref, vec_ref,
                pre_a, pre_b, gone_ref, gattnt_ref, dctx_a, dctx_b, dn_ref):
    gffn = gffn_ref[...]
    width = 512
    steps = [
        (side, slice(c, c + width))
        for side in ((pre_a, sl_a, wb_a, wi_a), (pre_b, sl_b, wb_b, wi_b))
        for c in range(0, sl_a.shape[1], width)
    ]
    coming = dot(gffn, wb_a[:, steps[0][1]], NN)
    gn = gtwo_ref[...]
    for k, ((pre, slope, _, wi), at) in enumerate(steps):
        hidden = coming
        if k + 1 < len(steps):
            coming = dot(gffn, steps[k + 1][0][2][:, steps[k + 1][1]], NN)
        low = (hidden * slope[:, at].astype(F32)).astype(BF)
        pre[:, at] = low
        gn = gn + dot(low, wi[:, at], NT)
    cen = cen_ref[...]
    scaled = gn*vec_ref[2:3,:]
    m1 = row_sum(scaled)/D
    m2 = row_sum(scaled*cen)/D
    inv = inv_ref[:,0:1]
    gone = inv*(scaled-m1-cen*m2)
    gone_ref[...] = gone
    gattn = (vec_ref[0:1,:]*gone).astype(BF)
    gattnt_ref[...] = gattn.T
    dctx_a[...] = dot(gattn, wo_a[...], NN).astype(BF)
    dctx_b[...] = dot(gattn, wo_b[...], NN).astype(BF)
    @pl.when(pl.program_id(0)==0)
    def _(): dn_ref[...] = jnp.zeros(dn_ref.shape, F32)
    dn_ref[0:1,:] += jnp.sum(gn*cen, axis=0, keepdims=True)
    dn_ref[1:2,:] += jnp.sum(gn, axis=0, keepdims=True)

def inner_bwd(gffn, slopes, back, win, out, gtwo, cen, inv, vec, T=256):
    half=D//2; units=4*half
    wi = lambda: whole((D,units))
    wo = lambda: whole((D,half))
    return ordered_call(inner_bwd_kernel, grid=(SEQ//T,),
        in_specs=[row_tile(T,D), row_tile(T,units), row_tile(T,units), whole((D,units)), whole((D,units)), wi(), wi(), wo(), wo(), row_tile(T,D), row_tile(T,D), row_tile(T,128), whole((8,D))],
        out_specs=[row_tile(T,units), row_tile(T,units), row_tile(T,D), pl.BlockSpec((D,T), lambda r:(0,r)), row_tile(T,half), row_tile(T,half), whole((8,D))],
        out_shape=[hbm((SEQ,units),BF)]*2+[hbm((SEQ,D),F32), sds((D,SEQ),BF), sds((SEQ,half),BF), sds((SEQ,half),BF), sds((8,D),F32)],
        compiler_params=params_of(44), cost_estimate=LARGE, name="inner_bwd")(gffn,in_hbm(slopes[0]),in_hbm(slopes[1]),back[0],back[1],win[0],win[1],out[0],out[1],in_hbm(gtwo),cen,in_hbm(inv),vec)

def grad_weights_two_kernel(
    lowt_ref, gattnt_ref, pre_own, pre_away, ctx_own, ctx_away, own_a, own_b, away_a, away_b
):
    n = pl.program_id(0)
    half = ctx_own.shape[1]
    sides = ((pre_away, ctx_away, away_a, away_b), (pre_own, ctx_own, own_a, own_b))

    @pl.when(n == 0)
    def _():
        for pre, _, a, _ in sides:
            a[:, : 2 * half] = dot(lowt_ref[...], pre[...], NN).astype(BF)

    @pl.when(n == 1)
    def _():
        for pre, context, a, b in sides:
            product = dot(lowt_ref[...], pre[...], NN).astype(BF)
            a[:, 2 * half :] = product[:, :half]
            b[:, :half] = product[:, half:]
            b[:, half:] = dot(gattnt_ref[...], context[...], NN).astype(BF)


def grad_weights_two(lowt, gattnt, pre, ctx):
    half = D // 2
    col = pl.BlockSpec((SEQ, D), lambda n: (0, n))
    return ordered_call(
        grad_weights_two_kernel,
        grid=(2,),
        in_specs=[whole((D, SEQ)), resident(), col, col, resident(), resident()],
        out_specs=[resident()] * 4,
        out_shape=[sds((D, 3 * half), BF), sds((D, 2 * half), BF)] * 2,
        compiler_params=params_of(32),
        cost_estimate=LARGE,
        name="grad_weights_two",
    )(lowt, gattnt, in_hbm(pre[0]), in_hbm(pre[1]), ctx[0], ctx[1])


def grad_tokens_kernel(core_ref, gone_ref, d_a, d_b, d_c, d_d, w_a, w_b, own_ref, away_ref):
    cut = d_a.shape[1]
    total = gone_ref[...] + dot(d_a[...], w_a[:, :cut], NT) + dot(d_b[...], w_a[:, cut:], NT)
    total = total + dot(d_c[...], w_b[:, :cut], NT) + dot(d_d[...], w_b[:, cut:], NT)
    by_core(core_ref, total.astype(BF), own_ref, away_ref)


def grad_tokens(core, gone, dqkv, wq, T=256):
    half = D//2
    return ordered_call(grad_tokens_kernel, grid_spec=dict(num_scalar_prefetch=1, grid=(SEQ//T,),
        in_specs=[row_tile(T,D), *[row_tile(T,d.shape[1]) for d in dqkv], whole(wq[0].shape), whole(wq[1].shape)],
        out_specs=[row_tile(T,half)]*2), out_shape=[sds((SEQ,half),BF)]*2,
        compiler_params=params_of(32), cost_estimate=LARGE, name="grad_tokens")(core[None],in_hbm(gone),*[in_hbm(d) for d in dqkv],wq[0],wq[1])


def side_by_side_kernel(core_ref, own_ref, away_ref, out_ref, *turned_ref):
    half = away_ref.shape[1]
    first = jnp.where(core_ref[0] == 0, own_ref[0], away_ref[...])
    second = jnp.where(core_ref[0] == 0, away_ref[...], own_ref[0])
    out_ref[:, :half] = first
    out_ref[:, half:] = second
    if turned_ref:
        turned_ref[0][:half, :] = first.T
        turned_ref[0][half:, :] = second.T


def side_by_side(both, away, core, turned):
    half = away.shape[1]
    tile = 512
    outs = 2 if turned else 1
    return ordered_call(
        side_by_side_kernel,
        grid_spec=dict(
            num_scalar_prefetch=1,
            grid=(SEQ // tile,),
            in_specs=[
                pl.BlockSpec((1, tile, half), lambda r, c: (c[0], r, 0)),
                pl.BlockSpec((tile, half), lambda r, c: (r, 0)),
            ],
            out_specs=[
                pl.BlockSpec((tile, 2 * half), lambda r, c: (r, 0)),
                pl.BlockSpec((2 * half, tile), lambda r, c: (0, r)),
            ][:outs],
        ),
        out_shape=[sds((SEQ, 2 * half), BF), hbm((2 * half, SEQ), BF)][:outs],
        compiler_params=params_of(8),
        cost_estimate=SMALL,
        name="side_by_side",
    )(core[None], both, away)


def by_core(core_ref, value, own_ref, away_ref):
    half = own_ref.shape[1]
    first, second = value[:, :half], value[:, half:]
    own_ref[...] = jnp.where(core_ref[0] == 0, first, second)
    away_ref[...] = jnp.where(core_ref[0] == 0, second, first)


def digits_of(count):
    found, shift = [], 0
    while (1 << shift) < count:
        radix = min(4, count >> shift)
        found.append((shift, radix))
        shift += 2 if radix == 4 else 1
    return found


def swap(value, count, mask, axis="dp"):
    return lax.ppermute(value, axis, [(i, i ^ mask) for i in range(count)])


def place_kernel(places_ref, *refs, radix, widths):
    pieces, outs = refs[:radix], refs[radix:]
    for j, piece in enumerate(pieces):

        @pl.when(pl.program_id(0) == j)
        def _():
            start = 0
            for out, width in zip(outs, widths):
                out[:, 0] = piece[:, :, start : start + width]
                start += width


def place(pieces, places, widths=None):
    outer, rows, cols = pieces[0].shape
    radix = len(pieces)
    widths = widths or (cols,)
    placed = ordered_call(
        functools.partial(place_kernel, radix=radix, widths=widths),
        grid_spec=dict(
            num_scalar_prefetch=1,
            grid=(radix,),
            in_specs=[pl.BlockSpec((outer, rows, cols), lambda g, d: (0, 0, 0))] * radix,
            out_specs=[
                pl.BlockSpec((outer, 1, rows, width), lambda g, d: (0, d[g], 0, 0)) for width in widths
            ],
        ),
        out_shape=[sds((outer, radix, rows, width), BF) for width in widths],
        compiler_params=params_of(16),
        cost_estimate=SMALL,
        name="place",
    )(places, *pieces)
    placed = [p.reshape(outer * radix, rows, p.shape[-1]) for p in placed]
    return placed if len(widths) > 1 else placed[0]


def place_two_kernel(digit_ref, a_own, a_got, b_own, b_got, *outs):
    y = pl.program_id(0) // 2
    x = pl.program_id(0) % 2
    width = a_own.shape[-1]
    first = outs[0].shape[-1]
    for source, hit in ((a_own, x == digit_ref[1]), (a_got, x != digit_ref[1])):

        @pl.when(hit)
        def _():
            outs[0][:, 0, 0, :, :width] = source[:, 0]

    for source, hit in ((b_own, y == digit_ref[0]), (b_got, y != digit_ref[0])):

        @pl.when(hit)
        def _():
            outs[0][:, 0, 0, :, width:] = source[:, 0, :, : first - width]
            outs[1][:, 0, 0] = source[:, 0, :, first - width :]


def place_two(a_pieces, b_pieces, digit_y, digit_x, widths):
    outer, rows, a_width = a_pieces[0].shape
    b_width = b_pieces[0].shape[-1]
    outer //= 2
    a_spec = pl.BlockSpec((outer, 1, rows, a_width), lambda g, d: (0, g // 2, 0, 0))
    b_spec = pl.BlockSpec((outer, 1, rows, b_width), lambda g, d: (0, g % 2, 0, 0))
    shaped = [p.reshape(outer, 2, rows, -1) for p in (*a_pieces, *b_pieces)]
    placed = ordered_call(
        place_two_kernel,
        grid_spec=dict(
            num_scalar_prefetch=1,
            grid=(4,),
            in_specs=[a_spec, a_spec, b_spec, b_spec],
            out_specs=[
                pl.BlockSpec((outer, 1, 1, rows, width), lambda g, d: (0, g // 2, g % 2, 0, 0))
                for width in widths
            ],
        ),
        out_shape=[sds((outer, 2, 2, rows, width), BF) for width in widths],
        compiler_params=params_of(32),
        cost_estimate=SMALL,
        name="place_two",
    )(jnp.stack([digit_y, digit_x]), *shaped)
    return [p.reshape(outer * 4 * rows, -1) for p in placed]


def sum_split_kernel(digit_ref, *refs, counts):
    outs = refs[sum(counts) :]
    start = at = 0
    for count in counts:
        terms = refs[at : at + count]
        at += count
        total = terms[0][:, 0].astype(F32)
        for ref in terms[1:]:
            total = total + ref[:, 0].astype(F32)
        total = total.astype(BF)
        stop = start + total.shape[-1]
        for j, out in enumerate(outs):

            @pl.when(pl.program_id(0) == j)
            def _():
                out[:, :, start:stop] = total

        start = stop


def sum_split(runs, digit):
    outer, radix, rows, _ = runs[0][0].shape
    terms = [term for run in runs for term in run]
    cols = sum(run[0].shape[-1] for run in runs)
    return ordered_call(
        functools.partial(sum_split_kernel, counts=[len(run) for run in runs]),
        grid_spec=dict(
            num_scalar_prefetch=1,
            grid=(radix,),
            in_specs=[
                pl.BlockSpec((outer, 1, rows, term.shape[-1]), lambda g, d: (0, d[0] ^ g, 0, 0))
                for term in terms
            ],
            out_specs=[pl.BlockSpec((outer, rows, cols), lambda g, d: (0, 0, 0))] * radix,
        ),
        out_shape=[sds((outer, rows, cols), BF)] * radix,
        compiler_params=params_of(32),
        cost_estimate=SMALL,
        name="sum_split",
    )(digit[None], *terms)


def gather_start(held, count, place_in):
    shift, radix = place_in
    return [held] + [swap(held, count, j << shift) for j in range(1, radix)]


def gather_place(pieces, index, place_in, widths=None):
    shift, radix = place_in
    return place(pieces, ((index >> shift) & (radix - 1)) ^ jnp.arange(radix, dtype=jnp.int32), widths)


def ring(value, count, place_in):
    shift, radix = place_in
    step = 1 << shift
    around = [(i, i + step if (i >> shift) % radix < radix - 1 else i - (radix - 1) * step) for i in range(count)]
    return lax.ppermute(value, "dp", around)


def scatter_split(runs, index, place_in, rows):
    shift, radix = place_in
    shaped = [[t.reshape(-1, radix, rows, t.shape[-1]) for t in run] for run in runs]
    return sum_split(shaped, (index >> shift) & (radix - 1))


def scatter_send(parts, count, place_in):
    return [parts[0]] + [swap(parts[j], count, j << place_in[0]) for j in range(1, place_in[1])]


def sum_all(value, count):
    value = value + swap(value, 2, 1, "mp")
    for shift, radix in digits_of(count):
        parts = [value] + [swap(value, count, j << shift) for j in range(1, radix)]
        value = parts[0] + parts[1]
        if radix == 4:
            value = value + (parts[2] + parts[3])
    return value


def finish_kernel(*refs):
    terms, mask_ref, total_ref, square_ref = refs[:-3], refs[-3], refs[-2], refs[-1]
    total = terms[0][0].astype(F32)
    for term in terms[1:]:
        total = total + term[0].astype(F32)
    total = total * mask_ref[...]
    total_ref[...] = total
    square_ref[...] = jnp.full((8, 128), jnp.sum(total * total), F32)


def finish(terms, mask):
    shape = terms[0].shape
    return ordered_call(
        finish_kernel,
        in_specs=[whole(shape)] * len(terms) + [whole((1, shape[2]))],
        out_specs=[whole(shape[1:]), whole((8, 128))],
        out_shape=[sds(shape[1:], F32), sds((8, 128), F32)],
        compiler_params=params_of(8),
        cost_estimate=SMALL,
        name="finish",
    )(*terms, mask)


def adam_step(weight, gradient, first_mom, second, step_rate, decay_rate):
    first_new = BETA_ONE * first_mom + (1.0 - BETA_ONE) * gradient
    second_new = BETA_TWO * second + (1.0 - BETA_TWO) * gradient * gradient
    update = (
        first_new
        / (1.0 - BETA_ONE**STEP)
        / (jnp.sqrt(second_new / (1.0 - BETA_TWO**STEP)) + ADAM_EPS)
    )
    return (weight - step_rate * (update + decay_rate * weight), first_new, second_new)


def adam_kernel(factor_ref, g_one, g_two, g_back, g_norm, *refs):
    weights, firsts, seconds, outs = refs[:5], refs[5:10], refs[10:15], refs[15:]
    factor = factor_ref[0:1, 0:1]
    half = weights[0].shape[2]

    def step(slot, gradient, at, rate, decay):
        new = adam_step(
            weights[slot][at], gradient * factor, firsts[slot][at], seconds[slot][at], rate, decay
        )
        for kind in range(3):
            outs[5 * kind + slot][at] = new[kind]

    for t in range(3):
        for pair in range(half // PAIR):
            start = (3 * pair + t) * PAIR
            at = (t, slice(None), slice(pair * PAIR, (pair + 1) * PAIR))
            step(0, g_one[:, start : start + PAIR], at, LEARN_RATE, WEIGHT_DECAY)
    everything = (slice(None), slice(None))
    step(1, g_two[:, 4 * half :], everything, LEARN_RATE, WEIGHT_DECAY)
    step(2, g_two[:, : 4 * half], everything, LEARN_RATE, WEIGHT_DECAY)
    step(3, g_back[...], everything, LEARN_RATE, WEIGHT_DECAY)
    step(4, g_norm[...], everything, NORM_RATE, 0.0)


def adam(factor, gradients, weights, firsts, seconds):
    states = (*weights, *firsts, *seconds)
    return ordered_call(
        adam_kernel,
        in_specs=[whole(v.shape) for v in (factor, *gradients, *states)],
        out_specs=[whole(v.shape) for v in states],
        out_shape=[sds(v.shape, F32) for v in states],
        compiler_params=params_of(24),
        cost_estimate=SMALL,
        name="adam",
    )(factor, *gradients, *[in_hbm(v) for v in states])


def shards(
    count,
    tokens,
    cotangent,
    segments,
    head_gates,
    unit_gates,
    hidden_gates,
    layer_gates,
    w_qkv,
    w_out,
    w_in,
    w_back,
    norm_params,
    mom_qkv,
    mom_out,
    mom_in,
    mom_back,
    mom_norm,
    sec_qkv,
    sec_out,
    sec_in,
    sec_back,
    sec_norm,
):
    LINE.clear()
    index = lax.axis_index("dp")
    core = lax.axis_index("mp")
    rows = D // count
    half = D // 2
    pairs = half // PAIR
    head_mask = jnp.repeat(head_gates.astype(F32), HEAD_DIM)
    unit_mask = unit_gates.astype(F32)
    gate_attn = layer_gates[0]
    gate_ffn = layer_gates[1]

    shard_qkv = (
        w_qkv.astype(BF).reshape(3, rows, pairs, PAIR).transpose(1, 2, 0, 3).reshape(rows, 3 * half)
    )
    shard_out = (w_out.T * head_mask[None, :]).astype(BF)
    shard_two = jnp.concatenate([w_in.astype(BF), shard_out], axis=1)
    shard_back = (w_back.T * unit_mask[None, :]).astype(BF)
    digits = digits_of(count)

    def other_core(value):
        return swap(value, 2, 1, "mp")

    def both(own, away):
        return jnp.where(
            core == 0, jnp.concatenate([own, away], axis=-1), jnp.concatenate([away, own], axis=-1)
        )

    plane = digits[0]
    upper = [(bit, 2) for bit in range(plane[1] // 2, count.bit_length() - 1)]
    bit_y, bit_x = (index >> 1) & 1, index & 1

    def direct_start(held):
        for place_in in digits[:1:-1]:
            held = gather_place(gather_start(held, count, place_in), index, place_in)
        return gather_start(held, count, digits[1])

    def halves_start(pieces, widths):
        a, b = gather_place(pieces, index, upper[0], widths)
        return [a, swap(a, count, 2)], [b, swap(b, count, 1)]

    def halves_turn(halves):
        a = gather_place(halves[0], index, (1, 2))
        b = gather_place(halves[1], index, (0, 2))
        return [a, swap(a, count, 1)], [b, swap(b, count, 2)]

    def halves_place(halves):
        return place_two(*halves, bit_y, bit_x, (4 * half, half))

    def grow(pieces, place_in):
        return gather_place(pieces, index, place_in).reshape(1, -1, pieces[0].shape[-1])

    tok_away = other_core(lax.dynamic_index_in_dim(tokens, 1 - core, 0, keepdims=False))
    one = direct_start(shard_qkv[None])
    back = gather_start(shard_back[None], count, (0, 2))
    segment = lax.dynamic_index_in_dim(segments, core, 0, keepdims=False)[0]
    tables = segment_tables(segment)
    vectors = jnp.concatenate([hidden_gates.astype(F32)[None], norm_params], axis=0)
    vectors = both(vectors, other_core(vectors))
    hidden_mask, params = vectors[0], vectors[1:]
    vec = jnp.concatenate(
        [gate_attn * hidden_mask[None], gate_ffn * hidden_mask[None], params, params[:2]], axis=0
    )
    back = gather_start(grow(back, (0, 2)), count, (1, 2))
    wait_for(vec)
    x, xt = side_by_side(tokens, tok_away, core, True)
    wait_for(back[1])
    one = gather_start(gather_place(one, index, digits[1]), count, plane)
    two = gather_start(later(shard_two)[None], count, upper[-1])
    z_digit = digits[1]
    two = gather_place(two, index, upper[-1])
    for place_in in upper[-2:0:-1]:
        two = gather_place(gather_start(two, count, place_in), index, place_in)
    two = halves_start(gather_start(two, count, upper[0]), (1024, 5 * half - 1024))
    mine_qkv = gather_place(one, index, plane).reshape(D, -1)
    away_qkv = other_core(mine_qkv)
    back = grow(back, (1, 2))
    back = [back, ring(back, count, z_digit)]
    qkv_own, ctx_own, lse_own = attend_forward(x, mine_qkv, tables)
    core_later = later(core)
    cot_away = other_core(lax.dynamic_index_in_dim(cotangent, 1 - core_later, 0, keepdims=False))
    wait_for(back[-1])
    two = halves_turn(two)
    while len(back) < z_digit[1] - 1:
        back.append(ring(back[-1], count, z_digit))
    qkv_away, ctx_away, lse_away = attend_forward(x, away_qkv, tables)
    wait_for(back[-1])
    (grad_out,) = side_by_side(cotangent, cot_away, core, False)
    mine_in, mine_out = halves_place(two)
    away_out = other_core(mine_out)
    away_in = other_core(mine_in)
    if len(back) < z_digit[1]:
        back.append(ring(back[-1], count, z_digit))
    ctx = (ctx_own, ctx_away)
    lse = (lse_own, lse_away)
    qkv = (qkv_own, qkv_away)
    qkv_sides = (mine_qkv, away_qkv)
    in_sides = (mine_in, away_in)
    out_sides = (mine_out, away_out)
    centred_one, inv_one, normed_low, normed_turned = mid(ctx, out_sides, x, vec)
    act_own, slope_own = ffn_in(normed_low, mine_in)
    z_here = (index >> z_digit[0]) & (z_digit[1] - 1)
    z_from = (z_here - jnp.arange(z_digit[1], dtype=jnp.int32)) & (z_digit[1] - 1)
    back = place(back, z_from).reshape(1, -1, back[0].shape[-1])
    for place_in in digits[2:]:
        back = grow(gather_start(back, count, place_in), place_in)
    mine_back = back.reshape(D, -1)
    away_back = other_core(mine_back)
    act_away, slope_away = ffn_in(normed_low, away_in)
    acts, slopes = (act_own, act_away), (slope_own, slope_away)
    back_sides = (mine_back, away_back)
    result_own, result_away, grad_two, grad_ffn_turned, grad_ffn, dnorm_two = ffn_out(
        core, acts, back_sides, centred_one, grad_out, vec
    )
    cores_here = jnp.stack([core, 1 - core])

    def send_back(own, away):
        return place([own[None], other_core(away)[None]], cores_here)

    bit = [(0, 2), (1, 2)]

    def over_cores(own, away):
        return [own, other_core(away)]

    def split_a(terms, step):
        return scatter_send(scatter_split([terms], index, bit[step], rows), count, bit[step])

    def split_b(terms, step):
        place_in = bit[1 - step]
        return scatter_send(scatter_split([terms], index, place_in, rows * (2 - step)), count, place_in)

    def split_z(runs, level):
        place_in = upper[level]
        return [scatter_send(scatter_split(runs, index, place_in, rows), count, place_in)]

    back_own_a, back_own_b, back_away_a, back_away_b = grad_back(grad_ffn_turned, acts)
    back_a, back_b = over_cores(back_own_a, back_away_a), over_cores(back_own_b, back_away_b)
    pre_own, pre_away, grad_one, grad_attn_turned, dctx_own, dctx_away, dnorm_one = inner_bwd(
        grad_ffn, slopes, back_sides, in_sides, out_sides, grad_two, centred_one, inv_one, vec
    )
    back_a, back_b = split_a(back_a, 0), split_b(back_b, 0)
    out_tokens = send_back(result_own, result_away)
    two_own_a, two_own_b, two_away_a, two_away_b = grad_weights_two(
        normed_turned, grad_attn_turned, (pre_own, pre_away), ctx
    )
    back_a, back_b = split_a(back_a, 1), split_b(back_b, 1)
    two_a, two_b = over_cores(two_own_a, two_away_a), over_cores(two_own_b, two_away_b)

    def attend_back(side, start, many):
        dctx = (dctx_own, dctx_away)[side]
        return attend_backward(qkv[side], dctx, ctx[side], lse[side], tables, xt, start, many)

    away_dqkv_a, away_gq_a = attend_back(1, 0, 1)
    back = split_z([back_a, back_b], 0)
    two_a, two_b = split_a(two_a, 0), split_b(two_b, 0)
    away_dqkv_b, away_gq_b = attend_back(1, 1, pairs - 1)
    for level in range(1, len(upper)):
        back = split_z(back, level)
    two_a, two_b = split_a(two_a, 1), split_b(two_b, 1)
    own_dqkv_b, own_gq_b = attend_back(0, 1, pairs - 1)
    sum_back, square_back = finish(back[0], unit_mask[None])
    two = [two_a, two_b]
    for place_in in digits[1:]:
        two = [scatter_send(scatter_split(two, index, place_in, rows), count, place_in)]
    one_b = split_b(over_cores(own_gq_b, away_gq_b), 0)
    own_dqkv_a, own_gq_a = attend_back(0, 0, 1)
    one_a = scatter_split([over_cores(own_gq_a, away_gq_a)], index, plane, rows)
    one_a = scatter_send(one_a, count, plane)
    one_b = split_b(one_b, 1)
    mask_two = jnp.concatenate([jnp.ones((4 * half,), F32), head_mask])
    sum_two, square_two = finish(two[0], mask_two[None])
    token_own, token_away = grad_tokens(
        core, grad_one, (own_dqkv_a, own_dqkv_b, away_dqkv_a, away_dqkv_b), qkv_sides
    )
    one = [one_a, one_b]
    for place_in in digits[1:]:
        one = [scatter_send(scatter_split(one, index, place_in, rows), count, place_in)]
    sum_one, square_one = finish(one[0], jnp.ones((1, 3 * half), F32))
    line = list(LINE)
    input_grad = send_back(token_own, token_away)
    LINE[:] = line

    square = (square_back + square_two + square_one) / 1024.0
    norm_rows = jnp.concatenate([dnorm_one[:2], dnorm_two[:2]]).reshape(-1, 128)
    packed = jnp.concatenate([norm_rows, square], axis=0)
    packed = sum_all(packed, count)
    norm_full = packed[:-8].reshape(4, D)
    total_square = jnp.sum(packed[-8:]) + jnp.sum(norm_full * norm_full)
    grad_norm = jnp.sqrt(total_square)
    factor = jnp.minimum(1.0, CLIP_NORM / grad_norm)
    norm_here = lax.dynamic_slice_in_dim(norm_full, core * half, half, 1)
    def turn(values):
        return [v.T if slot in (1, 3) else v for slot, v in enumerate(values)]

    states = adam(
        jnp.full((8, 128), factor, F32),
        (sum_one, sum_two, sum_back, norm_here),
        turn((w_qkv, w_out, w_in, w_back, norm_params)),
        turn((mom_qkv, mom_out, mom_in, mom_back, mom_norm)),
        turn((sec_qkv, sec_out, sec_in, sec_back, sec_norm)),
    )
    return (
        out_tokens,
        input_grad,
        grad_norm,
        *turn(states[:5]),
        *turn(states[5:10]),
        *turn(states[10:]),
    )


def solution(mesh):
    weight_specs = (P(None, "dp", "mp"), P("mp", "dp"), P("dp", "mp"), P("mp", "dp"), P(None, "mp"))
    in_specs = (
        P(None, "dp", "mp"),
        P(None, "dp", "mp"),
        P(None, "dp", None),
        P("mp"),
        P("mp"),
        P("mp"),
        P(),
    ) + weight_specs * 3
    out_specs = (P(None, "dp", "mp"), P(None, "dp", "mp"), P()) + weight_specs * 3
    count = mesh.shape["dp"]

    def body(*args):
        return shards(count, *args)

    return jax.shard_map(body, mesh=mesh, in_specs=in_specs, out_specs=out_specs, check_vma=False)
```
